32 devices in a mesh: gx: 8 (over z, y), gy: 4 (over x, core).
Axes of the slice: x: 2, y: 2, z: 4, core: 2. Of those that a mesh axis runs over, the one named last changes fastest.
Arguments:
- displacement: float32 [3, 256, 96, 128], P(None, 'gx', 'gy'), may hold values from -6 to 6
- density: float32 [256, 96, 128], P('gx', 'gy'), may hold values from 0.05 to 1
- element_kind: int32 [256, 96, 128], P('gx', 'gy'), may hold values from 0 to 7
- load_x: int32 [1024], replicated, may hold values from 0 to 255
- load_y: int32 [1024], replicated, may hold values from 0 to 95
- load_z: int32 [1024], replicated, may hold values from 0 to 127
- load_force: float32 [3, 1024], replicated, may hold values from -8 to 8
Outputs:
- sensitivity: float32 [256, 96, 128], P('gx', 'gy')
- residual: float32 [3, 256, 96, 128], P(None, 'gx', 'gy')
- compliance: float32 [], replicated
- volume: float32 [], replicated
The draws below stay inside these ranges and needn't reach their ends.
Inputs may be any that keep to these rules, and one draw needn't show every extreme that they name: `element_kind`: 1 marks a passive void element, 2 a passive solid element, any other value a design element. `load_x`: each load acts on one node; several loads may share a node.
All inputs are finite; a program needn't handle non-finite values.
Results may differ from the reference program's by a relative error of at most 0.0001.
Values sent between devices are 32-bit elements; how exact they have to be, the bound alone decides.
No kernel may reach another device: no remote copies, remote signals or barrier semaphores. Data moves between devices by JAX's collectives and lax.ppermute only.
A program may use at most 128 MiB of HBM per device.

```python
import jax
import jax.numpy as jnp
import numpy as np
from jax import lax

NZ = 128
RADIUS = 3
LOADS = 1024
NX = 256
NY = 96


def draw_density(key, part):
    place = jnp.arange(NX).astype(jnp.float32) / float(max(NX - 1, 1))
    level = 0.1 + 0.8 * place
    spread = jax.random.uniform(key, (NX, NY, NZ), jnp.float32, 0.5, 1.1)
    return (level[:, None, None] * spread).astype(jnp.float32)


def set_ends(entries, stream_key, smallest, high):
    index_at = [jax.random.randint(jax.random.fold_in(stream_key, axis), (), 0, length) for axis, length in enumerate(entries.shape)]
    main_axis = entries.shape.index(max(entries.shape))
    next_to = index_at[:main_axis] + [(index_at[main_axis] + 1) % entries.shape[main_axis]] + index_at[main_axis + 1:]
    return entries.at[tuple(index_at)].set(smallest).at[tuple(next_to)].set(high)


def shard_levels(key, extent, shards, least, high):
    level, own = 1.0, jax.random.fold_in(key, 6)
    for position, shards_of in shards:
        steps = jnp.exp(jax.random.uniform(jax.random.fold_in(own, position), (shards_of,), jnp.float32, least / len(shards), high / len(shards)))
        level = level * jnp.repeat(steps, extent[position] // shards_of).reshape([-1 if axis == position else 1 for axis in range(len(extent))])
    return level


def noise(rng, dims, scale, most, cuts=(), kind=jnp.bfloat16):
    drawn = scale * jax.random.normal(rng, dims, jnp.float32)
    if cuts:
        drawn = drawn * shard_levels(rng, dims, cuts, -0.22, 0.18)
    return jnp.clip(drawn, -most, most).astype(kind)


def setup_inputs(seed: int = 0) -> dict:
    key_list = jax.random.split(jax.random.key(seed), 8)
    return {
        "displacement": noise(key_list[0], (3, NX, NY, NZ), 1.0, 6.0, ((1, 8), (2, 4)), jnp.float32),
        "density": draw_density(jax.random.fold_in(key_list[7], 71), 0),
        "element_kind": set_ends(jax.random.randint(key_list[2], (NX, NY, NZ), 0, 8), jax.random.fold_in(key_list[2], 1), 0, 7).astype(jnp.int32),
        "load_x": set_ends(jax.random.randint(key_list[3], (LOADS,), 0, NX), jax.random.fold_in(key_list[3], 1), 0, NX - 1).astype(jnp.int32),
        "load_y": set_ends(jax.random.randint(key_list[4], (LOADS,), 0, NY), jax.random.fold_in(key_list[4], 1), 0, NY - 1).astype(jnp.int32),
        "load_z": set_ends(jax.random.randint(key_list[5], (LOADS,), 0, NZ), jax.random.fold_in(key_list[5], 1), 0, NZ - 1).astype(jnp.int32),
        "load_force": noise(key_list[6], (3, LOADS), 2.0, 8.0, (), jnp.float32),
    }


PENALTY = 3.0
STIFF_FLOOR = 0.001
POISSON = 0.3

def corner_list():
    return [(side_x, side_y, side_z) for side_x in (0, 1) for side_y in (0, 1) for side_z in (0, 1)]

def element_matrix():
    lame_first = POISSON / ((1.0 + POISSON) * (1.0 - 2.0 * POISSON))
    shear_modulus = 0.5 / (1.0 + POISSON)
    material = np.zeros((6, 6))
    material[:3, :3] = lame_first
    for diagonal in range(3):
        material[diagonal, diagonal] += 2.0 * shear_modulus
        material[diagonal + 3, diagonal + 3] = shear_modulus
    points = [0.5 - 0.5 / np.sqrt(3.0), 0.5 + 0.5 / np.sqrt(3.0)]
    result = np.zeros((24, 24))
    for point_x in points:
        for point_y in points:
            for point_z in points:
                strain = np.zeros((6, 24))
                for corner, (side_x, side_y, side_z) in enumerate(corner_list()):
                    value_x = point_x if side_x else 1.0 - point_x
                    value_y = point_y if side_y else 1.0 - point_y
                    value_z = point_z if side_z else 1.0 - point_z
                    slope_x = (1.0 if side_x else -1.0) * value_y * value_z
                    slope_y = value_x * (1.0 if side_y else -1.0) * value_z
                    slope_z = value_x * value_y * (1.0 if side_z else -1.0)
                    column = 3 * corner
                    strain[0, column] = slope_x
                    strain[1, column + 1] = slope_y
                    strain[2, column + 2] = slope_z
                    strain[3, column] = slope_y
                    strain[3, column + 1] = slope_x
                    strain[4, column + 1] = slope_z
                    strain[4, column + 2] = slope_y
                    strain[5, column + 2] = slope_x
                    strain[5, column] = slope_z
                result += strain.T @ material @ strain / 8.0
    return result

def filter_pairs():
    reach_cells = RADIUS + 0.5
    return [(shift_x, shift_y) for shift_x in range(-RADIUS, RADIUS + 1) for shift_y in range(-RADIUS, RADIUS + 1) if shift_x * shift_x + shift_y * shift_y < reach_cells * reach_cells]

def filter_bands(depth_cells):
    places = jnp.arange(depth_cells)
    spacing = (places[:, None] - places[None, :]).astype(jnp.float32)
    reach_cells = RADIUS + 0.5
    return jnp.stack([jnp.maximum(0.0, reach_cells - jnp.sqrt(float(shift_x * shift_x + shift_y * shift_y) + spacing * spacing)) for shift_x, shift_y in filter_pairs()])

def weight_totals(start_x, count_x, start_y, count_y, total_x, total_y, band_stack):
    column_sums = lax.optimization_barrier(jnp.sum(band_stack, axis=2))
    result = jnp.zeros((count_x, count_y, band_stack.shape[1]), jnp.float32)
    places_x = start_x + jnp.arange(count_x)
    places_y = start_y + jnp.arange(count_y)
    for pair_rank, (shift_x, shift_y) in enumerate(filter_pairs()):
        inside_x = ((places_x + shift_x >= 0) & (places_x + shift_x < total_x)).astype(jnp.float32)
        inside_y = ((places_y + shift_y >= 0) & (places_y + shift_y < total_y)).astype(jnp.float32)
        result = result + inside_x[:, None, None] * inside_y[None, :, None] * column_sums[pair_rank][None, None, :]
    return result

def filter_apply(scaled_ext, band_stack, rows_x, rows_y):
    depth_cells = scaled_ext.shape[2]
    running = jnp.zeros((rows_x * rows_y, depth_cells), jnp.float32)
    for pair_rank, (shift_x, shift_y) in enumerate(filter_pairs()):
        slab_part = scaled_ext[RADIUS + shift_x:RADIUS + shift_x + rows_x, RADIUS + shift_y:RADIUS + shift_y + rows_y]
        slab_part = slab_part.reshape(rows_x * rows_y, depth_cells)
        running = running + jnp.dot(slab_part, band_stack[pair_rank], precision=lax.Precision.HIGHEST, preferred_element_type=jnp.float32)
    return running.reshape(rows_x, rows_y, depth_cells)

def reference(displacement, density, element_kind, load_x, load_y, load_z, load_force):
    physical = jnp.where(element_kind == 1, 0.0, jnp.where(element_kind == 2, 1.0, density)).astype(jnp.float32)
    design = ((element_kind != 1) & (element_kind != 2)).astype(jnp.float32)
    stiffness = STIFF_FLOOR + (1.0 - STIFF_FLOOR) * physical ** 3
    factor = -PENALTY * (1.0 - STIFF_FLOOR) * physical ** 2 * design
    volume = jnp.mean(physical)
    element_stiff = jnp.asarray(element_matrix(), jnp.float32)
    unodes = jnp.pad(displacement, ((0, 0), (0, 1), (0, 1), (0, 1)))

    def element_row(row_rank):
        nodes_here = lax.dynamic_slice_in_dim(unodes, row_rank, 2, 1)
        corner_values = jnp.stack([nodes_here[component, side_x, side_y:side_y + NY, side_z:side_z + NZ] for side_x, side_y, side_z in corner_list() for component in range(3)])
        product = jnp.einsum('ij,jyz->iyz', element_stiff, corner_values, precision=lax.Precision.HIGHEST)
        energy = lax.optimization_barrier(jnp.sum(corner_values * product, axis=0))
        forces = product * lax.dynamic_index_in_dim(stiffness, row_rank, 0, keepdims=False)[None]
        lower_part = jnp.zeros((3, NY, NZ), jnp.float32)
        upper_part = jnp.zeros((3, NY, NZ), jnp.float32)
        for corner, (side_x, side_y, side_z) in enumerate(corner_list()):
            slab_part = jnp.pad(forces[3 * corner:3 * corner + 3], ((0, 0), (side_y, 0), (side_z, 0)))[:, :NY, :NZ]
            if side_x == 0:
                lower_part = lower_part + slab_part
            else:
                upper_part = upper_part + slab_part
        return (energy, lower_part, upper_part)
    energy, lower_part, upper_part = lax.map(element_row, jnp.arange(NX))
    lower_part = jnp.moveaxis(lower_part, 0, 1)
    upper_part = jnp.moveaxis(upper_part, 0, 1)
    node_force = lower_part + jnp.pad(upper_part, ((0, 0), (1, 0), (0, 0), (0, 0)))[:, :NX]
    flat_index = ((load_x * NY + load_y) * NZ + load_z).astype(jnp.int32)
    applied = jnp.zeros((3, NX * NY * NZ), jnp.float32).at[:, flat_index].add(load_force).reshape(3, NX, NY, NZ)
    residual = applied - node_force
    compliance = jnp.sum(stiffness * energy)
    band_stack = filter_bands(NZ)
    totals = weight_totals(0, NX, 0, NY, NX, NY, band_stack)
    scaled = factor * energy / totals
    scaled_ext = jnp.pad(scaled, ((RADIUS, RADIUS), (RADIUS, RADIUS), (0, 0)))
    filtered = filter_apply(scaled_ext, band_stack, NX, NY)
    sensitivity = filtered * (float(NX * NY * NZ) / compliance)
    return (sensitivity, residual, compliance, volume)
```

```python
import functools

import jax
import jax.numpy as jnp
import numpy as np
from jax import lax
from jax.experimental import pallas as pl
from jax.experimental.pallas import tpu as pltpu
from jax.sharding import PartitionSpec as P

RADIUS = 3
PENALTY = 3.0
STIFF_FLOOR = 0.001
POISSON = 0.3
HALO = 8
BOTH = ("gx", "gy")
FULL = jax.ShapeDtypeStruct


def element_matrix():
    lame_first = POISSON / ((1.0 + POISSON) * (1.0 - 2.0 * POISSON))
    shear_modulus = 0.5 / (1.0 + POISSON)
    material = np.zeros((6, 6))
    material[:3, :3] = lame_first
    for diagonal in range(3):
        material[diagonal, diagonal] += 2.0 * shear_modulus
        material[diagonal + 3, diagonal + 3] = shear_modulus
    points = [0.5 - 0.5 / np.sqrt(3.0), 0.5 + 0.5 / np.sqrt(3.0)]
    corners = [(a, b, e) for a in (0, 1) for b in (0, 1) for e in (0, 1)]
    result = np.zeros((24, 24))
    for point_x in points:
        for point_y in points:
            for point_z in points:
                strain = np.zeros((6, 24))
                for corner, (side_x, side_y, side_z) in enumerate(corners):
                    value_x = point_x if side_x else 1.0 - point_x
                    value_y = point_y if side_y else 1.0 - point_y
                    value_z = point_z if side_z else 1.0 - point_z
                    slope_x = (1.0 if side_x else -1.0) * value_y * value_z
                    slope_y = value_x * (1.0 if side_y else -1.0) * value_z
                    slope_z = value_x * value_y * (1.0 if side_z else -1.0)
                    column = 3 * corner
                    strain[0, column] = slope_x
                    strain[1, column + 1] = slope_y
                    strain[2, column + 2] = slope_z
                    strain[3, column] = slope_y
                    strain[3, column + 1] = slope_x
                    strain[4, column + 1] = slope_z
                    strain[4, column + 2] = slope_y
                    strain[5, column + 2] = slope_x
                    strain[5, column] = slope_z
                result += strain.T @ material @ strain / 8.0
    return result


def modal_matrix():
    pair = np.array([[1.0, 1.0], [-1.0, 1.0]])
    turn = np.kron(np.kron(np.kron(pair, pair), pair), np.eye(3))
    return turn @ element_matrix() @ turn.T / 64.0


SHEARS = ((3, 14), (4, 8), (6, 13))
NORMALS = (5, 7, 12)
PAIRS = ((10, 15), (11, 18), (17, 19))
TRIO = (9, 16, 20)
LASTS = (21, 22, 23)


def modal_constants():
    modal = modal_matrix()
    known = np.zeros((24, 24))
    shear = modal[3, 3]
    for first, second in SHEARS:
        known[np.ix_((first, second), (first, second))] = shear
    normal_off = modal[5, 7]
    normal_own = modal[5, 5] - normal_off
    known[np.ix_(NORMALS, NORMALS)] = normal_off
    pair_off = modal[10, 15]
    pair_own = modal[10, 10] - pair_off
    for both in PAIRS:
        known[np.ix_(both, both)] = pair_off
    trio = modal[9, 16]
    known[np.ix_(TRIO, TRIO)] = trio
    last = modal[21, 21]
    for group, own in ((NORMALS, normal_own), (sum(PAIRS, ()), pair_own), (TRIO, trio), (LASTS, last)):
        for degree in group:
            known[degree, degree] += own
    assert np.abs(known - modal).max() < 1e-12
    return tuple(float(v) for v in (shear, normal_off, normal_own, pair_off, pair_own, trio, last))


def weight_of(square):
    return max(0.0, RADIUS + 0.5 - float(np.sqrt(square)))


CLASSES = (0, 1, 2, 4, 5, 8, 9, 10)


def stiffness_of(physical):
    return STIFF_FLOOR + (1.0 - STIFF_FLOOR) * (physical * physical * physical)


def physical_of(density, kind):
    return jnp.where(kind == 1, 0.0, jnp.where(kind == 2, 1.0, density))


def factor_of(physical, kind):
    design = (kind != 1) & (kind != 2)
    return jnp.where(design, (-PENALTY * (1.0 - STIFF_FLOOR)) * (physical * physical), 0.0)


def pack_y(rows, cols, disp, dens, kind, out_a, out_b, vol):
    depth = disp.shape[-1]

    def column(ref, index):
        return ref[pl.ds(index, rows, stride=cols), :]

    def state(index):
        code = column(kind, index)
        physical = physical_of(column(dens, index), code)
        return physical, code

    def fill(low, high):
        slot = 0
        for c in range(3):
            for index in range(RADIUS + 1):
                low[pl.ds(slot * rows, rows), :] = disp[pl.ds(c * rows * cols + index, rows, stride=cols), :]
                slot += 1
        for index in range(RADIUS):
            low[pl.ds(slot * rows, rows), :] = factor_of(*state(index))
            slot += 1
        slot = 0
        for c in range(3):
            for index in range(cols - RADIUS, cols):
                high[pl.ds(slot * rows, rows), :] = disp[pl.ds(c * rows * cols + index, rows, stride=cols), :]
                slot += 1
        for index in range(cols - RADIUS, cols):
            physical, code = state(index)
            high[pl.ds(slot * rows, rows), :] = factor_of(physical, code)
            slot += 1
        high[pl.ds(slot * rows, rows), :] = stiffness_of(physical)

    odd = lax.axis_index("gy") % 2

    @pl.when(odd == 0)
    def _():
        fill(out_b, out_a)

    @pl.when(odd == 1)
    def _():
        fill(out_a, out_b)

    def add(step, total):
        at = pl.ds(pl.multiple_of(step * 32, 32), 32)
        return total + physical_of(dens[at, :], kind[at, :])

    total = lax.fori_loop(0, rows * cols // 32, add, jnp.zeros((32, depth), jnp.float32), unroll=4)
    vol[...] = jnp.sum(total.reshape(4, 8, depth), axis=0)


def unpack_y(rows, cols, count_y, disp, dens, kind, got_a, got_b, edge_u, edge_f, edge_s, out_a, out_b):
    here = lax.axis_index("gy")
    depth = disp.shape[-1]
    has_low = here > 0
    has_high = here < count_y - 1

    def fill(low, high):
        def put(ref, start, sublane, value):
            ref[pl.ds(start + sublane, rows, stride=HALO), :] = value

        zero = jnp.zeros((rows, depth), jnp.float32)
        slot = 0
        for c in range(3):
            for index in range(RADIUS + 1):
                put(edge_u, c * rows * HALO, index, jnp.where(has_high, high[pl.ds(slot * rows, rows), :], 0.0))
                slot += 1
        for index in range(RADIUS):
            put(edge_f, 0, index, jnp.where(has_high, high[pl.ds(slot * rows, rows), :], 0.0))
            slot += 1
        slot = 0
        for c in range(3):
            put(edge_u, c * rows * HALO, RADIUS + 1, zero)
            for index in range(HALO - RADIUS, HALO):
                put(edge_u, c * rows * HALO, index, low[pl.ds(slot * rows, rows), :])
                slot += 1
        for index in range(RADIUS, HALO - RADIUS):
            put(edge_f, 0, index, zero)
        for index in range(HALO - RADIUS, HALO):
            put(edge_f, 0, index, jnp.where(has_low, low[pl.ds(slot * rows, rows), :], 0.0))
            slot += 1
        edge_s[...] = jnp.zeros_like(edge_s)
        put(edge_s, 0, HALO - 1, jnp.where(has_low, low[pl.ds(slot * rows, rows), :], 0.0))

    odd = here % 2

    @pl.when(odd == 0)
    def _():
        fill(got_b, got_a)

    @pl.when(odd == 1)
    def _():
        fill(got_a, got_b)

    def send(out, row, with_stiff):
        for c in range(3):
            out[c, :cols, :] = disp[pl.ds((c * rows + row) * cols, cols), :]
            out[c, cols:, :] = edge_u[pl.ds((c * rows + row) * HALO, HALO), :]
        if with_stiff:
            at = pl.ds(row * cols, cols)
            out[3, :cols, :] = stiffness_of(physical_of(dens[at, :], kind[at, :]))
            out[3, cols:, :] = edge_s[pl.ds(row * HALO, HALO), :]
        else:
            out[3] = jnp.zeros_like(out[3])

    odd_x = lax.axis_index("gx") % 2

    @pl.when(odd_x == 0)
    def _():
        send(out_a, rows - 1, True)
        send(out_b, 0, False)

    @pl.when(odd_x == 1)
    def _():
        send(out_a, 0, False)
        send(out_b, rows - 1, True)


def loads_and_weights(rows, cols, count_x, count_y, after, load_x, load_y, load_z, force, sums, applied, inverse):
    del after
    depth = applied.shape[-1]
    place_x = lax.axis_index("gx") * rows
    place_y = lax.axis_index("gy") * cols
    local_x = load_x[...] - place_x
    local_y = load_y[...] - place_y
    owned = (local_x >= 0) & (local_x < rows) & (local_y >= 0) & (local_y < cols)
    target = jnp.where(owned, local_x * cols + local_y, -1)
    loads = target.shape[1]
    lanes = lax.broadcasted_iota(jnp.int32, (depth, loads), 0)
    hit_z = lanes == load_z[...]
    right = []
    for c in range(3):
        value = force[c : c + 1, :]
        coarse = value.astype(jnp.bfloat16).astype(jnp.float32)
        for part in (coarse, value - coarse):
            right.append(jnp.where(hit_z, part, 0.0).astype(jnp.bfloat16))
    right = jnp.concatenate(right, axis=0)
    block = 128

    def one(step, carry):
        first = pl.multiple_of(step * block, block)
        place = lax.broadcasted_iota(jnp.int32, (block, loads), 0) + first
        left = jnp.where(place == target, 1.0, 0.0).astype(jnp.bfloat16)
        product = lax.dot_general(
            left, right, (((1,), (1,)), ((), ())), preferred_element_type=jnp.float32
        )
        for c in range(3):
            part = product[:, 2 * c * depth : (2 * c + 1) * depth]
            rest = product[:, (2 * c + 1) * depth : (2 * c + 2) * depth]
            applied[c, pl.ds(first, block), :] = part + rest
        return carry

    lax.fori_loop(0, rows * cols // block, one, 0)

    wide = cols + HALO
    total_x, total_y = rows * count_x, cols * count_y
    sublane = lax.broadcasted_iota(jnp.int32, (wide, depth), 0)
    node_y = jnp.where(sublane >= wide - RADIUS, sublane - wide, sublane) + place_y
    inside_y = {
        shift: ((node_y + shift >= 0) & (node_y + shift < total_y)).astype(jnp.float32)
        for shift in range(-RADIUS, RADIUS + 1)
    }
    for kind in range(2 * RADIUS + 1):
        row = kind if kind <= RADIUS else rows - 2 * RADIUS - 1 + kind
        result = jnp.zeros((wide, depth), jnp.float32)
        for shift_y in range(-RADIUS, RADIUS + 1):
            line = jnp.zeros((1, depth), jnp.float32)
            for shift_x in range(-RADIUS, RADIUS + 1):
                square = shift_x * shift_x + shift_y * shift_y
                if square in CLASSES:
                    at = place_x + (row + shift_x)
                    inside = ((at >= 0) & (at < total_x)).astype(jnp.float32)
                    rank = CLASSES.index(square)
                    line = line + inside * sums[rank : rank + 1, :]
            result = result + inside_y[shift_y] * line
        inverse[kind] = 1.0 / jnp.where(result > 0.0, result, 1.0)


def elements(
    rows, cols, count_x, devices,
    disp, dens, kind, edge_u, edge_f, edge_s, got_a, got_b, applied, inverse, vol,
    resid, scaled, out_a, out_b, parts,
    node_u, waves, force,
):
    depth = disp.shape[-1]
    wide = cols + HALO
    blocks = wide // 8
    shear, normal_off, normal_own, pair_off, pair_own, trio, last = modal_constants()
    here = lax.axis_index("gx")
    has_low = here > 0
    has_high = here < count_x - 1
    odd = here % 2
    lane = lax.broadcasted_iota(jnp.int32, (wide, depth), 1)

    def transform(slot, values):
        for c in range(3):
            here_y = values[c]
            next_y = pltpu.roll(here_y, wide - 1, 0)
            for q, along_y in enumerate((here_y + next_y, next_y - here_y)):
                next_z = jnp.where(lane == depth - 1, 0.0, pltpu.roll(along_y, depth - 1, 1))
                waves[slot, (2 * q + 0) * 3 + c] = along_y + next_z
                waves[slot, (2 * q + 1) * 3 + c] = next_z - along_y

    def own_row(row):
        return [
            jnp.concatenate(
                [
                    disp[pl.ds(pl.multiple_of((c * rows + row) * cols, 8), cols), :],
                    edge_u[pl.ds(pl.multiple_of((c * rows + row) * HALO, 8), HALO), :],
                ],
                axis=0,
            )
            for c in range(3)
        ]

    def modal(before, after, block, stiff):
        at = pl.ds(block * 8, 8)
        u = [None] * 24
        for low in range(12):
            first, second = waves[before, low, at, :], waves[after, low, at, :]
            if low >= 3:
                u[low] = first + second
            u[12 + low] = second - first
        f = [None] * 24
        energy = None

        def add(value):
            nonlocal energy
            energy = value if energy is None else energy + value

        for first, second in SHEARS:
            both = u[first] + u[second]
            pull = shear * both
            add(pull * both)
            f[first] = f[second] = pull * stiff
        common = normal_off * (u[5] + u[7] + u[12])
        for degree in NORMALS:
            pull = common + normal_own * u[degree]
            add(pull * u[degree])
            f[degree] = pull * stiff
        for first, second in PAIRS:
            common = pair_off * (u[first] + u[second])
            for degree in (first, second):
                pull = common + pair_own * u[degree]
                add(pull * u[degree])
                f[degree] = pull * stiff
        common = u[9] + u[16] + u[20]
        for degree in TRIO:
            pull = trio * (common + u[degree])
            add(pull * u[degree])
            f[degree] = pull * stiff
        for degree in LASTS:
            pull = last * u[degree]
            add(pull * u[degree])
            f[degree] = pull * stiff
        return energy, f

    def spread(block, f, start, finish):
        at = pl.ds(block * 8, 8)
        for low in range(12):
            near, far = f[low], f[12 + low]
            if start:
                lower = (near - far) if near is not None else -far
                force[1, low, at, :] = force[0, low, at, :] + lower
            if finish:
                force[0, low, at, :] = (near + far) if near is not None else far

    def gather(row):
        for c in range(3):
            along = []
            for r in range(2):
                first = force[1, r * 3 + c]
                second = force[1, (2 + r) * 3 + c]
                along.append((first - second) + pltpu.roll(first + second, 1, 0))
            upper = jnp.where(lane == 0, 0.0, pltpu.roll(along[0] + along[1], 1, 1))
            total = (along[0] - along[1]) + upper
            at = pl.ds(pl.multiple_of(row * cols, 8), cols)
            resid[c, at, :] = applied[c, at, :] - total[:cols]

    def take(low, high):
        transform(0, [low[c] for c in range(3)])
        transform(1, own_row(0))
        for block in range(blocks):
            at = pl.ds(block * 8, 8)
            stiff = jnp.where(has_low, low[3, at, :], 0.0)
            energy, f = modal(0, 1, block, stiff)
            spread(block, f, False, True)
        for c in range(3):
            node_u[c] = jnp.where(has_high, high[c], 0.0)

    @pl.when(odd == 0)
    def _():
        take(got_b, got_a)

    @pl.when(odd == 1)
    def _():
        take(got_a, got_b)

    def element_row(row, total, next_row, before, after):
        transform(after, next_row)
        kind_of_row = jnp.where(
            row < RADIUS, row, jnp.where(row >= rows - RADIUS, row - (rows - 2 * RADIUS - 1), RADIUS)
        )
        for block in range(blocks):
            if block * 8 < cols:
                at = pl.ds(pl.multiple_of(row * cols + block * 8, 8), 8)
                code = kind[at, :]
                physical = physical_of(dens[at, :], code)
                stiff = stiffness_of(physical)
                factor = factor_of(physical, code)
            else:
                at = pl.ds(pl.multiple_of(row * HALO, 8), HALO)
                stiff = edge_s[at, :]
                factor = edge_f[at, :]
            energy, f = modal(before, after, block, stiff)
            spread(block, f, True, True)
            scaled[row, pl.ds(block * 8, 8), :] = factor * energy * inverse[kind_of_row, pl.ds(block * 8, 8), :]
            if block * 8 < cols:
                total = total + stiff * energy
        gather(row)
        return total

    def two_rows(step, total):
        row = 2 * step
        total = element_row(row, total, own_row(row + 1), 1, 0)
        return element_row(row + 1, total, own_row(row + 2), 0, 1)

    total = jnp.zeros((8, depth), jnp.float32)
    total = lax.fori_loop(0, rows // 2 - 1, two_rows, total)
    total = element_row(rows - 2, total, own_row(rows - 1), 1, 0)
    total = element_row(rows - 1, total, [node_u[c] for c in range(3)], 0, 1)

    half = depth // 2
    pieces = []
    for value in (total, vol[...]):
        line = jnp.sum(value, axis=0, keepdims=True)
        pieces.append(line + pltpu.roll(line, half, 1))
    line = jnp.where(lax.broadcasted_iota(jnp.int32, (1, depth), 1) < half, pieces[0], pieces[1])
    parts[...] = jnp.broadcast_to(line, (devices, depth))

    @pl.when(odd == 0)
    def _():
        out_a[...] = scaled[rows - RADIUS :]
        out_b[...] = scaled[:RADIUS]

    @pl.when(odd == 1)
    def _():
        out_a[...] = scaled[:RADIUS]
        out_b[...] = scaled[rows - RADIUS :]


def filter_rows(rows, cols, count_x, cells, scaled, got_a, got_b, parts, sens, comp, vol, near):
    depth = sens.shape[-1]
    wide = cols + HALO
    here = lax.axis_index("gx")
    has_low = here > 0
    has_high = here < count_x - 1
    odd = here % 2
    half = depth // 2
    line = jnp.sum(parts[...], axis=0, keepdims=True)
    first = lax.broadcasted_iota(jnp.int32, (1, depth), 1) < half
    compliance = jnp.sum(jnp.where(first, line, 0.0))
    volume = jnp.sum(jnp.where(first, 0.0, line))
    comp[0, 0] = compliance
    vol[0, 0] = volume / cells
    scale = cells / jnp.broadcast_to(compliance, (8, depth))

    def along_y(row, value):
        near[0, row] = value[:cols]
        for shift in range(1, RADIUS + 1):
            both = pltpu.roll(value, shift, 0) + pltpu.roll(value, wide - shift, 0)
            near[shift, row] = both[:cols]

    def take(low, high):
        for index in range(RADIUS):
            along_y(index, jnp.where(has_low, low[index], 0.0))
            along_y(rows + RADIUS + index, jnp.where(has_high, high[index], 0.0))

    @pl.when(odd == 0)
    def _():
        take(got_b, got_a)

    @pl.when(odd == 1)
    def _():
        take(got_a, got_b)

    def own(row, carry):
        along_y(row + RADIUS, scaled[row])
        return carry

    lax.fori_loop(0, rows, own, 0, unroll=2)
    lane = lax.broadcasted_iota(jnp.int32, (8, depth), 1)

    def out_row(row, carry):
        for block in range(cols // 8):
            at = pl.ds(block * 8, 8)
            classes = {}
            for shift_x in range(RADIUS + 1):
                for shift_y in range(RADIUS + 1):
                    square = shift_x * shift_x + shift_y * shift_y
                    if square not in CLASSES:
                        continue
                    value = near[shift_y, row + (RADIUS + shift_x), at, :]
                    if shift_x:
                        value = value + near[shift_y, row + (RADIUS - shift_x), at, :]
                    classes[square] = value if square not in classes else classes[square] + value
            result = None
            for shift_z in range(RADIUS + 1):
                line = None
                for square, value in classes.items():
                    weight = weight_of(square + shift_z * shift_z)
                    if weight > 0.0:
                        line = weight * value if line is None else line + weight * value
                if shift_z:
                    up = jnp.where(lane < shift_z, 0.0, pltpu.roll(line, shift_z, 1))
                    down = jnp.where(lane >= depth - shift_z, 0.0, pltpu.roll(line, depth - shift_z, 1))
                    line = up + down
                result = line if result is None else result + line
            sens[row, at, :] = result * scale
        return carry

    lax.fori_loop(0, rows, out_row, 0, unroll=2)


def call(body, shapes, inputs, scratch=(), any_first=False, smem_out=(), flops=0, limit=24):
    in_specs = [pl.BlockSpec(memory_space=pltpu.VMEM) for _ in inputs]
    if any_first:
        in_specs[0] = pl.BlockSpec(memory_space=pl.ANY)
    out_specs = [
        pl.BlockSpec(memory_space=pltpu.SMEM if rank in smem_out else pltpu.VMEM)
        for rank in range(len(shapes))
    ]
    moved = sum(int(np.prod(v.shape)) * 4 for v in list(inputs) + list(shapes))
    return pl.pallas_call(
        body,
        out_shape=[FULL(v.shape, v.dtype) for v in shapes],
        in_specs=in_specs,
        out_specs=out_specs,
        scratch_shapes=list(scratch),
        cost_estimate=pl.CostEstimate(flops=flops, bytes_accessed=moved, transcendentals=0),
        compiler_params=pltpu.CompilerParams(vmem_limit_bytes=limit * 1024 * 1024),
    )(*inputs)


def f32(*shape):
    return FULL(shape, jnp.float32)


def on_device(count_x, count_y, displacement, density, element_kind, load_x, load_y, load_z, load_force):
    rows, cols, depth = density.shape
    wide = cols + HALO
    devices = count_x * count_y
    cells = float(rows * cols * depth * devices)

    pairs_ya = [(k, k ^ 1) for k in range(count_y)]
    pairs_yb = [(k, (((k + 1) ^ 1) - 1) % count_y) for k in range(count_y)]
    pairs_xa = [(k, k ^ 1) for k in range(count_x)]
    pairs_xb = []
    for i in range(count_x):
        for j in range(count_y):
            if 0 < i < count_x - 1:
                other = (((i + 1) ^ 1) - 1, j)
            else:
                other = (i, j ^ 1)
            pairs_xb.append((i * count_y + j, other[0] * count_y + other[1]))

    disp = displacement.reshape(3 * rows * cols, depth)
    dens = density.reshape(rows * cols, depth)
    kind = element_kind.reshape(rows * cols, depth)

    slots = 4 * RADIUS + RADIUS
    send_a, send_b, vol = call(
        functools.partial(pack_y, rows, cols),
        [f32(slots * rows, depth), f32(slots * rows, depth), f32(8, depth)],
        [disp, dens, kind],
    )
    got_a = lax.ppermute(send_a, "gy", pairs_ya)
    got_b = lax.ppermute(send_b, "gy", pairs_yb)

    sums = np.zeros((8, depth), np.float32)
    for rank, square in enumerate(CLASSES):
        for z in range(depth):
            sums[rank, z] = sum(
                weight_of(square + s * s) for s in range(-RADIUS, RADIUS + 1) if 0 <= z + s < depth
            )
    count = load_x.shape[0]
    applied, inverse = call(
        functools.partial(loads_and_weights, rows, cols, count_x, count_y),
        [f32(3, rows * cols, depth), f32(2 * RADIUS + 1, wide, depth)],
        [vol, load_x.reshape(1, count), load_y.reshape(1, count), load_z.reshape(1, count), load_force, jnp.asarray(sums)],
        any_first=True,
        flops=2 * rows * cols * count * 6 * depth,
    )

    edge_u, edge_f, edge_s, send_a, send_b = call(
        functools.partial(unpack_y, rows, cols, count_y),
        [f32(3 * rows * HALO, depth), f32(rows * HALO, depth), f32(rows * HALO, depth)] + [f32(4, wide, depth)] * 2,
        [disp, dens, kind, got_a, got_b],
    )
    got_a = lax.ppermute(send_a, "gx", pairs_xa)
    got_b = lax.ppermute(send_b, BOTH, pairs_xb)

    resid, scaled, send_a, send_b, parts = call(
        functools.partial(elements, rows, cols, count_x, devices),
        [f32(3, rows * cols, depth), f32(rows, wide, depth)] + [f32(RADIUS, wide, depth)] * 2 + [f32(devices, depth)],
        [disp, dens, kind, edge_u, edge_f, edge_s, got_a, got_b, applied, inverse, vol],
        scratch=[
            pltpu.VMEM((3, wide, depth), jnp.float32),
            pltpu.VMEM((2, 12, wide, depth), jnp.float32),
            pltpu.VMEM((2, 12, wide, depth), jnp.float32),
        ],
        flops=250 * rows * wide * depth,
    )
    got_a = lax.ppermute(send_a, "gx", pairs_xa)
    got_b = lax.ppermute(send_b, BOTH, pairs_xb)
    parts = lax.all_to_all(parts, BOTH, 0, 0, tiled=True)

    sens, comp, volume = call(
        functools.partial(filter_rows, rows, cols, count_x, cells),
        [f32(rows, cols, depth), f32(1, 1), f32(1, 1)],
        [scaled, got_a, got_b, parts],
        scratch=[pltpu.VMEM((RADIUS + 1, rows + 2 * RADIUS, cols, depth), jnp.float32)],
        smem_out=(1, 2),
        flops=60 * rows * cols * depth,
    )
    return (
        sens,
        resid.reshape(3, rows, cols, depth),
        comp.reshape(()),
        volume.reshape(()),
    )


def solution(mesh):
    placed = (
        P(None, "gx", "gy", None),
        P("gx", "gy", None),
        P("gx", "gy", None),
        P(),
        P(),
        P(),
        P(),
    )
    return jax.shard_map(
        functools.partial(on_device, mesh.shape["gx"], mesh.shape["gy"]),
        mesh=mesh,
        in_specs=placed,
        out_specs=(P("gx", "gy", None), P(None, "gx", "gy", None), P(), P()),
        check_vma=False,
    )
```

```python
import functools

import jax
import jax.numpy as jnp
import numpy as np
from jax import lax
from jax.experimental import pallas as pl
from jax.experimental.pallas import tpu as pltpu
from jax.sharding import PartitionSpec as P

RADIUS = 3
PENALTY = 3.0
STIFF_FLOOR = 0.001
POISSON = 0.3
HALO = 8
BOTH = ("gx", "gy")
FULL = jax.ShapeDtypeStruct


def element_matrix():
    lame_first = POISSON / ((1.0 + POISSON) * (1.0 - 2.0 * POISSON))
    shear_modulus = 0.5 / (1.0 + POISSON)
    material = np.zeros((6, 6))
    material[:3, :3] = lame_first
    for diagonal in range(3):
        material[diagonal, diagonal] += 2.0 * shear_modulus
        material[diagonal + 3, diagonal + 3] = shear_modulus
    points = [0.5 - 0.5 / np.sqrt(3.0), 0.5 + 0.5 / np.sqrt(3.0)]
    corners = [(a, b, e) for a in (0, 1) for b in (0, 1) for e in (0, 1)]
    result = np.zeros((24, 24))
    for point_x in points:
        for point_y in points:
            for point_z in points:
                strain = np.zeros((6, 24))
                for corner, (side_x, side_y, side_z) in enumerate(corners):
                    value_x = point_x if side_x else 1.0 - point_x
                    value_y = point_y if side_y else 1.0 - point_y
                    value_z = point_z if side_z else 1.0 - point_z
                    slope_x = (1.0 if side_x else -1.0) * value_y * value_z
                    slope_y = value_x * (1.0 if side_y else -1.0) * value_z
                    slope_z = value_x * value_y * (1.0 if side_z else -1.0)
                    column = 3 * corner
                    strain[0, column] = slope_x
                    strain[1, column + 1] = slope_y
                    strain[2, column + 2] = slope_z
                    strain[3, column] = slope_y
                    strain[3, column + 1] = slope_x
                    strain[4, column + 1] = slope_z
                    strain[4, column + 2] = slope_y
                    strain[5, column + 2] = slope_x
                    strain[5, column] = slope_z
                result += strain.T @ material @ strain / 8.0
    return result


def modal_matrix():
    pair = np.array([[1.0, 1.0], [-1.0, 1.0]])
    turn = np.kron(np.kron(np.kron(pair, pair), pair), np.eye(3))
    return turn @ element_matrix() @ turn.T / 64.0


SHEARS = ((3, 14), (4, 8), (6, 13))
NORMALS = (5, 7, 12)
PAIRS = ((10, 15), (11, 18), (17, 19))
TRIO = (9, 16, 20)
LASTS = (21, 22, 23)


def modal_constants():
    modal = modal_matrix()
    known = np.zeros((24, 24))
    shear = modal[3, 3]
    for first, second in SHEARS:
        known[np.ix_((first, second), (first, second))] = shear
    normal_off = modal[5, 7]
    normal_own = modal[5, 5] - normal_off
    known[np.ix_(NORMALS, NORMALS)] = normal_off
    pair_off = modal[10, 15]
    pair_own = modal[10, 10] - pair_off
    for both in PAIRS:
        known[np.ix_(both, both)] = pair_off
    trio = modal[9, 16]
    known[np.ix_(TRIO, TRIO)] = trio
    last = modal[21, 21]
    for group, own in ((NORMALS, normal_own), (sum(PAIRS, ()), pair_own), (TRIO, trio), (LASTS, last)):
        for degree in group:
            known[degree, degree] += own
    assert np.abs(known - modal).max() < 1e-12
    return tuple(float(v) for v in (shear, normal_off, normal_own, pair_off, pair_own, trio, last))


def weight_of(square):
    return max(0.0, RADIUS + 0.5 - float(np.sqrt(square)))


CLASSES = (0, 1, 2, 4, 5, 8, 9, 10)


def stiffness_of(physical):
    return STIFF_FLOOR + (1.0 - STIFF_FLOOR) * (physical * physical * physical)


def physical_of(density, kind):
    return jnp.where(kind == 1, 0.0, jnp.where(kind == 2, 1.0, density))


def factor_of(physical, kind):
    design = (kind != 1) & (kind != 2)
    return jnp.where(design, (-PENALTY * (1.0 - STIFF_FLOOR)) * (physical * physical), 0.0)


def pack_y(rows, cols, disp, dens, kind, out_a, out_b, edge_d, edge_p, edge_k, sems):
    half = HALO // 2
    copies = []
    for side, start in ((0, 0), (half, cols - half)):
        for source, target in ((disp, edge_d), (dens, edge_p), (kind, edge_k)):
            lead = (slice(None),) * (len(source.shape) - 2)
            copies.append(
                pltpu.make_async_copy(
                    source.at[(*lead, pl.ds(start, half), slice(None))],
                    target.at[(*lead, pl.ds(side, half), slice(None))],
                    sems.at[len(copies)],
                )
            )
    for copy in copies:
        copy.start()
    for copy in copies:
        copy.wait()
    depth = disp.shape[-1]
    flat_d = edge_d.reshape(3 * rows * HALO, depth)
    flat_p = edge_p.reshape(rows * HALO, depth)
    flat_k = edge_k.reshape(rows * HALO, depth)

    def state(index):
        code = flat_k[pl.ds(index, rows, stride=HALO), :]
        return physical_of(flat_p[pl.ds(index, rows, stride=HALO), :], code), code

    def fill(low, high):
        slot = 0
        for c in range(3):
            for index in range(RADIUS + 1):
                low[pl.ds(slot * rows, rows), :] = flat_d[pl.ds(c * rows * HALO + index, rows, stride=HALO), :]
                slot += 1
        for index in range(RADIUS):
            low[pl.ds(slot * rows, rows), :] = factor_of(*state(index))
            slot += 1
        slot = 0
        for c in range(3):
            for index in range(HALO - RADIUS, HALO):
                high[pl.ds(slot * rows, rows), :] = flat_d[pl.ds(c * rows * HALO + index, rows, stride=HALO), :]
                slot += 1
        for index in range(HALO - RADIUS, HALO):
            physical, code = state(index)
            high[pl.ds(slot * rows, rows), :] = factor_of(physical, code)
            slot += 1
        high[pl.ds(slot * rows, rows), :] = stiffness_of(physical)

    odd = lax.axis_index("gy") % 2

    @pl.when(odd == 0)
    def _():
        fill(out_b, out_a)

    @pl.when(odd == 1)
    def _():
        fill(out_a, out_b)


def unpack_y(rows, cols, count_y, after, disp, dens, kind, got_a, got_b, edge_u, edge_f, edge_s, out_a, out_b):
    del after
    here = lax.axis_index("gy")
    depth = disp.shape[-1]
    has_low = here > 0
    has_high = here < count_y - 1

    def fill(low, high):
        def put(ref, start, sublane, value):
            ref[pl.ds(start + sublane, rows, stride=HALO), :] = value

        zero = jnp.zeros((rows, depth), jnp.float32)
        slot = 0
        for c in range(3):
            for index in range(RADIUS + 1):
                put(edge_u, c * rows * HALO, index, jnp.where(has_high, high[pl.ds(slot * rows, rows), :], 0.0))
                slot += 1
        for index in range(RADIUS):
            put(edge_f, 0, index, jnp.where(has_high, high[pl.ds(slot * rows, rows), :], 0.0))
            slot += 1
        slot = 0
        for c in range(3):
            put(edge_u, c * rows * HALO, RADIUS + 1, zero)
            for index in range(HALO - RADIUS, HALO):
                put(edge_u, c * rows * HALO, index, low[pl.ds(slot * rows, rows), :])
                slot += 1
        for index in range(RADIUS, HALO - RADIUS):
            put(edge_f, 0, index, zero)
        for index in range(HALO - RADIUS, HALO):
            put(edge_f, 0, index, jnp.where(has_low, low[pl.ds(slot * rows, rows), :], 0.0))
            slot += 1
        edge_s[...] = jnp.zeros_like(edge_s)
        put(edge_s, 0, HALO - 1, jnp.where(has_low, low[pl.ds(slot * rows, rows), :], 0.0))

    odd = here % 2

    @pl.when(odd == 0)
    def _():
        fill(got_b, got_a)

    @pl.when(odd == 1)
    def _():
        fill(got_a, got_b)

    def send(out, row, with_stiff):
        for c in range(3):
            out[c, :cols, :] = disp[pl.ds((c * rows + row) * cols, cols), :]
            out[c, cols:, :] = edge_u[pl.ds((c * rows + row) * HALO, HALO), :]
        if with_stiff:
            at = pl.ds(row * cols, cols)
            out[3, :cols, :] = stiffness_of(physical_of(dens[at, :], kind[at, :]))
            out[3, cols:, :] = edge_s[pl.ds(row * HALO, HALO), :]
        else:
            out[3] = jnp.zeros_like(out[3])

    odd_x = lax.axis_index("gx") % 2

    @pl.when(odd_x == 0)
    def _():
        send(out_a, rows - 1, True)
        send(out_b, 0, False)

    @pl.when(odd_x == 1)
    def _():
        send(out_a, 0, False)
        send(out_b, rows - 1, True)


def loads_and_weights(rows, cols, count_x, count_y, after, load_x, load_y, load_z, force, sums, applied, inverse):
    del after
    depth = applied.shape[-1]
    place_x = lax.axis_index("gx") * rows
    place_y = lax.axis_index("gy") * cols
    local_x = load_x[...] - place_x
    local_y = load_y[...] - place_y
    owned = (local_x >= 0) & (local_x < rows) & (local_y >= 0) & (local_y < cols)
    target = jnp.where(owned, local_x * cols + local_y, -1)
    loads = target.shape[1]
    lanes = lax.broadcasted_iota(jnp.int32, (depth, loads), 0)
    hit_z = lanes == load_z[...]
    right = [[], []]
    for c in range(3):
        value = force[c : c + 1, :]
        coarse = value.astype(jnp.bfloat16).astype(jnp.float32)
        for part, piece in zip(right, (coarse, value - coarse)):
            part.append(jnp.where(hit_z, piece, 0.0).astype(jnp.bfloat16))
    place = lax.broadcasted_iota(jnp.int32, (rows * cols, loads), 0)
    left = jnp.where(place == target, 1.0, 0.0).astype(jnp.bfloat16)
    product = None
    for part in right:
        piece = lax.dot_general(
            left, jnp.concatenate(part, axis=0), (((1,), (1,)), ((), ())), preferred_element_type=jnp.float32
        )
        product = piece if product is None else product + piece
    for c in range(3):
        applied[c] = product[:, c * depth : (c + 1) * depth]

    wide = cols + HALO
    total_x, total_y = rows * count_x, cols * count_y
    sublane = lax.broadcasted_iota(jnp.int32, (wide, depth), 0)
    node_y = jnp.where(sublane >= wide - RADIUS, sublane - wide, sublane) + place_y
    inside_y = {
        shift: ((node_y + shift >= 0) & (node_y + shift < total_y)).astype(jnp.float32)
        for shift in range(-RADIUS, RADIUS + 1)
    }
    for kind in range(2 * RADIUS + 1):
        row = kind if kind <= RADIUS else rows - 2 * RADIUS - 1 + kind
        result = jnp.zeros((wide, depth), jnp.float32)
        for shift_y in range(-RADIUS, RADIUS + 1):
            line = jnp.zeros((1, depth), jnp.float32)
            for shift_x in range(-RADIUS, RADIUS + 1):
                square = shift_x * shift_x + shift_y * shift_y
                if square in CLASSES:
                    at = place_x + (row + shift_x)
                    inside = ((at >= 0) & (at < total_x)).astype(jnp.float32)
                    rank = CLASSES.index(square)
                    line = line + inside * sums[rank : rank + 1, :]
            result = result + inside_y[shift_y] * line
        inverse[kind] = 1.0 / jnp.where(result > 0.0, result, 1.0)


def waves_of(here, there, lane, depth):
    result = [[[None] * 3 for _ in range(2)] for _ in range(2)]
    for c in range(3):
        for q, along in enumerate((here[c] + there[c], there[c] - here[c])):
            beyond = jnp.where(lane == depth - 1, 0.0, pltpu.roll(along, depth - 1, 1))
            result[q][0][c] = along + beyond
            result[q][1][c] = beyond - along
    return tuple(result[q][r][c] for q in range(2) for r in range(2) for c in range(3))


def modal(before, after, stiff, constants):
    shear, normal_off, normal_own, pair_off, pair_own, trio, last = constants
    u = [None] * 24
    for low in range(12):
        if low >= 3:
            u[low] = before[low] + after[low]
        u[12 + low] = after[low] - before[low]
    f = [None] * 24
    terms = []

    def take(degree, pull):
        terms.append(pull * u[degree])
        f[degree] = pull * stiff

    for first, second in SHEARS:
        both = u[first] + u[second]
        pull = shear * both
        terms.append(pull * both)
        f[first] = f[second] = pull * stiff
    common = normal_off * (u[5] + u[7] + u[12])
    for degree in NORMALS:
        take(degree, common + normal_own * u[degree])
    for first, second in PAIRS:
        common = pair_off * (u[first] + u[second])
        take(first, common + pair_own * u[first])
        take(second, common + pair_own * u[second])
    common = u[9] + u[16] + u[20]
    for degree in TRIO:
        take(degree, trio * (common + u[degree]))
    for degree in LASTS:
        take(degree, last * u[degree])
    while len(terms) > 1:
        terms = [sum(terms[k : k + 2][1:], terms[k]) for k in range(0, len(terms), 2)]
    return terms[0], f


def lower_of(f):
    return tuple(f[12 + k] * -1.0 if f[k] is None else f[k] - f[12 + k] for k in range(12))


def upper_of(f):
    return tuple(f[12 + k] if f[k] is None else f[k] + f[12 + k] for k in range(12))


def along_z(g, lane):
    result = []
    for c in range(3):
        lines = []
        for q in range(2):
            first, second = g[6 * q + c], g[6 * q + 3 + c]
            lines.append((first - second) + jnp.where(lane == 0, 0.0, pltpu.roll(first + second, 1, 1)))
        result.append((lines[0] - lines[1], lines[0] + lines[1]))
    return result


def inner_elements(
    rows, cols,
    disp, dens, kind, edge_u, edge_f, edge_s, applied, inverse,
    resid, scaled, sums, ring, carry_y,
):
    depth = disp.shape[-1]
    constants = modal_constants()
    blocks = cols // HALO
    lane = lax.broadcasted_iota(jnp.int32, (HALO, depth), 1)

    def gather(step, nothing):
        for c in range(3):
            at = c * rows + step
            ring[c, step, :HALO, :] = disp[pl.ds(pl.multiple_of(at * cols + cols - HALO, 8), HALO), :]
            ring[c, step, HALO : 2 * HALO, :] = edge_u[pl.ds(pl.multiple_of(at * HALO, 8), HALO), :]
            ring[c, step, 2 * HALO :, :] = disp[pl.ds(pl.multiple_of(at * cols, 8), HALO), :]
        return nothing

    lax.fori_loop(0, rows, gather, 0, unroll=4)
    total = jnp.zeros((HALO, depth), jnp.float32)
    filled = jnp.zeros((HALO, depth), jnp.float32)

    for block in (blocks, *range(blocks)):
        own = block < blocks

        def nodes(row, block=block):
            if block < blocks - 1:
                start = [(c * rows + row) * cols + block * HALO for c in range(3)]
                return waves_of(
                    [disp[pl.ds(v, HALO), :] for v in start], [disp[pl.ds(v + 1, HALO), :] for v in start], lane, depth
                )
            start = (block - (blocks - 1)) * HALO
            return waves_of(
                [ring[c, row, start : start + HALO, :] for c in range(3)],
                [ring[c, row, start + 1 : start + 1 + HALO, :] for c in range(3)],
                lane,
                depth,
            )

        def finish(row, g, block=block, own=own):
            for c, (near, far) in enumerate(along_z(g, lane)):
                if own:
                    carry_y[c, row, 8 * block + 9 : 8 * block + 17, :] = far
                    at = pl.ds(row * cols + 8 * block, HALO)
                    resid[c, at, :] = applied[c, at, :] - (near + carry_y[c, row, 8 * block + 8 : 8 * block + 16, :])
                else:
                    carry_y[c, row, 1:9, :] = far

        def step(row, carry, block=block, own=own, nodes=nodes, finish=finish):
            before, held, total, filled = carry
            after = nodes(row + 1)
            where = jnp.where(
                row < RADIUS, row, jnp.where(row >= rows - RADIUS, row - (rows - 2 * RADIUS - 1), RADIUS)
            )
            if own:
                at = pl.ds(row * cols + block * HALO, HALO)
                code = kind[at, :]
                physical = physical_of(dens[at, :], code)
                stiff, factor = stiffness_of(physical), factor_of(physical, code)
                filled = filled + physical
            else:
                at = pl.ds(row * HALO, HALO)
                stiff, factor = edge_s[at, :], edge_f[at, :]
            energy, f = modal(before, after, stiff, constants)
            value = factor * energy * inverse[where, 8 * block : 8 * block + 8, :]
            if own:
                scaled[row, 8 * block + 8 : 8 * block + 16, :] = value
                total = total + stiff * energy
            else:
                scaled[row, :HALO, :] = value
                scaled[row, cols + HALO :, :] = value
            finish(row, tuple(a + b for a, b in zip(held, lower_of(f))))
            return after, upper_of(f), total, filled

        zero = jnp.zeros((HALO, depth), jnp.float32)
        carry = (nodes(0), (zero,) * 12, total, filled)
        carry = lax.fori_loop(0, rows - 2, step, carry, unroll=2)
        carry = step(rows - 2, carry)
        _, held, total, filled = carry
        finish(rows - 1, held)
        if own:
            at = pl.ds((rows - 1) * cols + block * HALO, HALO)
            filled = filled + physical_of(dens[at, :], kind[at, :])
    sums[0] = total
    sums[1] = filled


def outer_elements(
    rows, cols, count_x, devices,
    disp, dens, kind, edge_u, edge_f, edge_s, got_a, got_b, inner, scaled, sums, inverse,
    resid, final, out_a, out_b, parts, ring, carry_y,
):
    depth = disp.shape[-1]
    constants = modal_constants()
    wide = cols + HALO
    blocks = wide // HALO
    lane = lax.broadcasted_iota(jnp.int32, (HALO, depth), 1)
    here = lax.axis_index("gx")
    has_low = here > 0
    has_high = here < count_x - 1
    odd = here % 2

    def take(low, high):
        for c in range(3):
            ring[0, c, :wide, :] = low[c]
            ring[0, c, wide:, :] = low[c, :HALO, :]
            ring[3, c, :wide, :] = jnp.where(has_high, high[c], 0.0)
            ring[3, c, wide:, :] = jnp.where(has_high, high[c, :HALO, :], 0.0)
        ring[4, 0, :wide, :] = jnp.where(has_low, low[3], 0.0)

    @pl.when(odd == 0)
    def _():
        take(got_b, got_a)

    @pl.when(odd == 1)
    def _():
        take(got_a, got_b)

    for index, row in ((1, 0), (2, rows - 1)):
        for c in range(3):
            at = c * rows + row
            ring[index, c, :cols, :] = disp[pl.ds(at * cols, cols), :]
            ring[index, c, cols:wide, :] = edge_u[pl.ds(at * HALO, HALO), :]
            ring[index, c, wide:, :] = disp[pl.ds(at * cols, HALO), :]

    total = sums[0]
    for block in (blocks - 1, *range(blocks - 1)):
        own = block < blocks - 1
        first = 8 * block
        line = [
            waves_of(
                [ring[index, c, first : first + 8, :] for c in range(3)],
                [ring[index, c, first + 1 : first + 9, :] for c in range(3)],
                lane,
                depth,
            )
            for index in range(4)
        ]
        _, f_low = modal(line[0], line[1], ring[4, 0, first : first + 8, :], constants)
        row = rows - 1
        if own:
            at = pl.ds(row * cols + first, HALO)
            code = kind[at, :]
            physical = physical_of(dens[at, :], code)
            stiff, factor = stiffness_of(physical), factor_of(physical, code)
        else:
            at = pl.ds(row * HALO, HALO)
            stiff, factor = edge_s[at, :], edge_f[at, :]
        energy, f_high = modal(line[2], line[3], stiff, constants)
        value = factor * energy * inverse[2 * RADIUS, first : first + 8, :]
        if own:
            total = total + stiff * energy
            final[first + 8 : first + 16, :] = value
        else:
            final[:HALO, :] = value
            final[wide:, :] = value
        for index, (row, g) in enumerate(((0, upper_of(f_low)), (rows - 1, lower_of(f_high)))):
            for c, (near, far) in enumerate(along_z(g, lane)):
                if own:
                    carry_y[index, c, first + 9 : first + 17, :] = far
                    resid[index, c, first : first + 8, :] = inner[c, pl.ds(row * cols + first, HALO), :] - (
                        near + carry_y[index, c, first + 8 : first + 16, :]
                    )
                else:
                    carry_y[index, c, 1:9, :] = far

    half = depth // 2
    pieces = []
    for value in (total, sums[1]):
        line = jnp.sum(value, axis=0, keepdims=True)
        pieces.append(line + pltpu.roll(line, half, 1))
    line = jnp.where(lax.broadcasted_iota(jnp.int32, (1, depth), 1) < half, pieces[0], pieces[1])
    parts[...] = jnp.broadcast_to(line, (devices, depth))

    def send(up, down):
        for index in range(RADIUS - 1):
            up[index] = scaled[rows - RADIUS + index, :wide, :]
        up[RADIUS - 1] = final[:wide, :]
        for index in range(RADIUS):
            down[index] = scaled[index, :wide, :]

    @pl.when(odd == 0)
    def _():
        send(out_a, out_b)

    @pl.when(odd == 1)
    def _():
        send(out_b, out_a)


def filter_rows(
    rows, cols, count_x, cells,
    scaled, final, got_a, got_b, parts, inner, outer,
    sens, resid, comp, vol, near, ends, result_v, sems,
):
    depth = sens.shape[-1]
    wide = cols + HALO
    copies = [
        pltpu.make_async_copy(
            inner.at[:, pl.ds(cols, (rows - 2) * cols), :], resid.at[:, pl.ds(cols, (rows - 2) * cols), :], sems.at[0]
        )
    ]
    for index, row in enumerate((0, rows - 1)):
        copies.append(
            pltpu.make_async_copy(outer.at[index], resid.at[:, pl.ds(row * cols, cols), :], sems.at[1 + index])
        )
    for copy in copies:
        copy.start()
    here = lax.axis_index("gx")
    has_low = here > 0
    has_high = here < count_x - 1
    odd = here % 2
    half = depth // 2
    line = jnp.sum(parts[...], axis=0, keepdims=True)
    first = lax.broadcasted_iota(jnp.int32, (1, depth), 1) < half
    compliance = jnp.sum(jnp.where(first, line, 0.0))
    volume = jnp.sum(jnp.where(first, 0.0, line))
    comp[0, 0] = compliance
    vol[0, 0] = volume / cells
    scale = cells / jnp.broadcast_to(compliance, (8, depth))

    def along_y(row, load):
        for block in range(cols // 8):
            start = 8 + 8 * block
            near[0, row, 8 * block : 8 * block + 8, :] = load(start)
            for shift in range(1, RADIUS + 1):
                near[shift, row, 8 * block : 8 * block + 8, :] = load(start + shift) + load(start - shift)

    def take(low, high):
        for index in range(RADIUS):
            for source, has, at in ((low, has_low, index), (high, has_high, RADIUS + index)):
                value = jnp.where(has, source[index], 0.0)
                ends[at, :wide, :] = value
                ends[at, wide:, :] = value[:HALO]

    @pl.when(odd == 0)
    def _():
        take(got_b, got_a)

    @pl.when(odd == 1)
    def _():
        take(got_a, got_b)

    for index in range(RADIUS):
        along_y(index, lambda start, at=index: ends[at, start : start + 8, :])
        along_y(rows + RADIUS + index, lambda start, at=RADIUS + index: ends[at, start : start + 8, :])
    along_y(rows + RADIUS - 1, lambda start: final[start : start + 8, :])

    def own(row, carry):
        along_y(row + RADIUS, lambda start: scaled[row, start : start + 8, :])
        return carry

    lax.fori_loop(0, rows - 1, own, 0)
    lane = lax.broadcasted_iota(jnp.int32, (8, depth), 1)

    def out_row(row, carry):
        for block in range(cols // 8):
            at = pl.ds(block * 8, 8)
            classes = {}
            for shift_x in range(RADIUS + 1):
                for shift_y in range(RADIUS + 1):
                    square = shift_x * shift_x + shift_y * shift_y
                    if square not in CLASSES:
                        continue
                    value = near[shift_y, row + (RADIUS + shift_x), at, :]
                    if shift_x:
                        value = value + near[shift_y, row + (RADIUS - shift_x), at, :]
                    classes[square] = value if square not in classes else classes[square] + value
            result = None
            for shift_z in range(RADIUS + 1):
                line = None
                for square, value in classes.items():
                    weight = weight_of(square + shift_z * shift_z)
                    if weight > 0.0:
                        line = weight * value if line is None else line + weight * value
                if shift_z:
                    up = jnp.where(lane < shift_z, 0.0, pltpu.roll(line, shift_z, 1))
                    down = jnp.where(lane >= depth - shift_z, 0.0, pltpu.roll(line, depth - shift_z, 1))
                    line = up + down
                result = line if result is None else result + line
            result_v[row, at, :] = result * scale
        return carry

    pieces = 4
    for piece in range(pieces):
        size = rows // pieces
        lax.fori_loop(piece * size, (piece + 1) * size, out_row, 0, unroll=2)
        at = pl.ds(piece * size, size)
        copies.append(pltpu.make_async_copy(result_v.at[at], sens.at[at], sems.at[3 + piece]))
        copies[-1].start()
    for copy in copies:
        copy.wait()


def call(body, shapes, inputs, scratch=(), places=None, out_places=None, flops=0, limit=24):
    places, out_places = places or {}, out_places or {}
    in_specs = [pl.BlockSpec(memory_space=places.get(rank, pltpu.VMEM)) for rank in range(len(inputs))]
    out_specs = [pl.BlockSpec(memory_space=out_places.get(rank, pltpu.VMEM)) for rank in range(len(shapes))]
    moved = sum(int(np.prod(v.shape)) * 4 for v in list(inputs) + list(shapes))
    return pl.pallas_call(
        body,
        out_shape=[FULL(v.shape, v.dtype) for v in shapes],
        in_specs=in_specs,
        out_specs=out_specs,
        scratch_shapes=list(scratch),
        cost_estimate=pl.CostEstimate(flops=flops, bytes_accessed=moved, transcendentals=0),
        compiler_params=pltpu.CompilerParams(vmem_limit_bytes=limit * 1024 * 1024),
    )(*inputs)


def f32(*shape):
    return FULL(shape, jnp.float32)


def vmem(*shape, dtype=jnp.float32):
    return pltpu.VMEM(shape, dtype)


def on_device(count_x, count_y, displacement, density, element_kind, load_x, load_y, load_z, load_force):
    rows, cols, depth = density.shape
    wide = cols + HALO
    devices = count_x * count_y
    cells = float(rows * cols * depth * devices)

    pairs_ya = [(k, k ^ 1) for k in range(count_y)]
    pairs_xa = [(k, k ^ 1) for k in range(count_x)]
    pairs_yb, pairs_xb = [], []
    for i in range(count_x):
        for j in range(count_y):
            here = i * count_y + j
            inside_y, inside_x = 0 < j < count_y - 1, 0 < i < count_x - 1
            pairs_yb.append((here, i * count_y + ((j + 1) ^ 1) - 1 if inside_y else (i ^ 1) * count_y + j))
            pairs_xb.append((here, (((i + 1) ^ 1) - 1) * count_y + j if inside_x else i * count_y + (j ^ 1)))

    disp = displacement.reshape(3 * rows * cols, depth)
    dens = density.reshape(rows * cols, depth)
    kind = element_kind.reshape(rows * cols, depth)

    slots = 4 * RADIUS + RADIUS
    send_a, send_b = call(
        functools.partial(pack_y, rows, cols),
        [f32(slots * rows, depth)] * 2,
        [displacement, density, element_kind],
        scratch=[
            vmem(3, rows, HALO, depth),
            vmem(rows, HALO, depth),
            vmem(rows, HALO, depth, dtype=jnp.int32),
            pltpu.SemaphoreType.DMA((6,)),
        ],
        places={0: pltpu.HBM, 1: pltpu.HBM, 2: pltpu.HBM},
    )
    got_a = lax.ppermute(send_a, "gy", pairs_ya)
    got_b = lax.ppermute(send_b, BOTH, pairs_yb)

    sums = np.zeros((8, depth), np.float32)
    for rank, square in enumerate(CLASSES):
        for z in range(depth):
            sums[rank, z] = sum(
                weight_of(square + s * s) for s in range(-RADIUS, RADIUS + 1) if 0 <= z + s < depth
            )
    count = load_x.shape[0]
    applied, inverse = call(
        functools.partial(loads_and_weights, rows, cols, count_x, count_y),
        [f32(3, rows * cols, depth), f32(2 * RADIUS + 1, wide, depth)],
        [send_b, load_x.reshape(1, count), load_y.reshape(1, count), load_z.reshape(1, count), load_force, jnp.asarray(sums)],
        places={0: pl.ANY},
        flops=2 * rows * cols * count * 6 * depth,
    )

    edge_u, edge_f, edge_s, send_a, send_b = call(
        functools.partial(unpack_y, rows, cols, count_y),
        [f32(3 * rows * HALO, depth), f32(rows * HALO, depth), f32(rows * HALO, depth)] + [f32(4, wide, depth)] * 2,
        [inverse, disp, dens, kind, got_a, got_b],
        places={0: pl.ANY},
    )
    got_a = lax.ppermute(send_a, "gx", pairs_xa)
    got_b = lax.ppermute(send_b, BOTH, pairs_xb)

    inner, scaled, sums = call(
        functools.partial(inner_elements, rows, cols),
        [f32(3, rows * cols, depth), f32(rows, wide + HALO, depth), f32(2, 8, depth)],
        [disp, dens, kind, edge_u, edge_f, edge_s, applied, inverse],
        scratch=[vmem(3, rows, 3 * HALO, depth), vmem(3, rows, wide + 2 * HALO, depth)],
        flops=250 * rows * wide * depth,
    )
    outer, final, send_a, send_b, parts = call(
        functools.partial(outer_elements, rows, cols, count_x, devices),
        [f32(2, 3, cols, depth), f32(wide + HALO, depth)] + [f32(RADIUS, wide, depth)] * 2 + [f32(devices, depth)],
        [disp, dens, kind, edge_u, edge_f, edge_s, got_a, got_b, inner, scaled, sums, inverse],
        scratch=[vmem(5, 3, wide + HALO, depth), vmem(2, 3, wide + 2 * HALO, depth)],
        flops=500 * wide * depth,
    )
    got_a = lax.ppermute(send_a, "gx", pairs_xa)
    got_b = lax.ppermute(send_b, BOTH, pairs_xb)
    parts = lax.all_to_all(parts, BOTH, 0, 0, tiled=True)

    sens, resid, comp, volume = call(
        functools.partial(filter_rows, rows, cols, count_x, cells),
        [f32(rows, cols, depth), f32(3, rows * cols, depth), f32(1, 1), f32(1, 1)],
        [scaled, final, got_a, got_b, parts, inner, outer],
        scratch=[
            vmem(RADIUS + 1, rows + 2 * RADIUS, cols, depth),
            vmem(2 * RADIUS, wide + HALO, depth),
            vmem(rows, cols, depth),
            pltpu.SemaphoreType.DMA((7,)),
        ],
        out_places={0: pltpu.HBM, 1: pltpu.HBM, 2: pltpu.SMEM, 3: pltpu.SMEM},
        flops=60 * rows * cols * depth,
    )
    return (
        sens,
        resid.reshape(3, rows, cols, depth),
        comp.reshape(()),
        volume.reshape(()),
    )


def solution(mesh):
    placed = (
        P(None, "gx", "gy", None),
        P("gx", "gy", None),
        P("gx", "gy", None),
        P(),
        P(),
        P(),
        P(),
    )
    return jax.shard_map(
        functools.partial(on_device, mesh.shape["gx"], mesh.shape["gy"]),
        mesh=mesh,
        in_specs=placed,
        out_specs=(P("gx", "gy", None), P(None, "gx", "gy", None), P(), P()),
        check_vma=False,
    )
```

```python
import functools

import jax
import jax.numpy as jnp
import numpy as np
from jax import lax
from jax.experimental import pallas as pl
from jax.experimental.pallas import tpu as pltpu
from jax.sharding import PartitionSpec as P

RADIUS = 3
PENALTY = 3.0
STIFF_FLOOR = 0.001
POISSON = 0.3
HALO = 8
BOTH = ("gx", "gy")
FULL = jax.ShapeDtypeStruct
UNROLL = 5


def element_matrix():
    lame_first = POISSON / ((1.0 + POISSON) * (1.0 - 2.0 * POISSON))
    shear_modulus = 0.5 / (1.0 + POISSON)
    material = np.zeros((6, 6))
    material[:3, :3] = lame_first
    for diagonal in range(3):
        material[diagonal, diagonal] += 2.0 * shear_modulus
        material[diagonal + 3, diagonal + 3] = shear_modulus
    points = [0.5 - 0.5 / np.sqrt(3.0), 0.5 + 0.5 / np.sqrt(3.0)]
    corners = [(a, b, e) for a in (0, 1) for b in (0, 1) for e in (0, 1)]
    result = np.zeros((24, 24))
    for point_x in points:
        for point_y in points:
            for point_z in points:
                strain = np.zeros((6, 24))
                for corner, (side_x, side_y, side_z) in enumerate(corners):
                    value_x = point_x if side_x else 1.0 - point_x
                    value_y = point_y if side_y else 1.0 - point_y
                    value_z = point_z if side_z else 1.0 - point_z
                    slope_x = (1.0 if side_x else -1.0) * value_y * value_z
                    slope_y = value_x * (1.0 if side_y else -1.0) * value_z
                    slope_z = value_x * value_y * (1.0 if side_z else -1.0)
                    column = 3 * corner
                    strain[0, column] = slope_x
                    strain[1, column + 1] = slope_y
                    strain[2, column + 2] = slope_z
                    strain[3, column] = slope_y
                    strain[3, column + 1] = slope_x
                    strain[4, column + 1] = slope_z
                    strain[4, column + 2] = slope_y
                    strain[5, column + 2] = slope_x
                    strain[5, column] = slope_z
                result += strain.T @ material @ strain / 8.0
    return result


def modal_matrix():
    pair = np.array([[1.0, 1.0], [-1.0, 1.0]])
    turn = np.kron(np.kron(np.kron(pair, pair), pair), np.eye(3))
    return turn @ element_matrix() @ turn.T / 64.0


SHEARS = ((3, 14), (4, 8), (6, 13))
NORMALS = (5, 7, 12)
PAIRS = ((10, 15), (11, 18), (17, 19))
TRIO = (9, 16, 20)
LASTS = (21, 22, 23)


def modal_constants():
    modal = modal_matrix()
    known = np.zeros((24, 24))
    shear = modal[3, 3]
    for first, second in SHEARS:
        known[np.ix_((first, second), (first, second))] = shear
    normal_off = modal[5, 7]
    normal_own = modal[5, 5] - normal_off
    known[np.ix_(NORMALS, NORMALS)] = normal_off
    pair_off = modal[10, 15]
    pair_own = modal[10, 10] - pair_off
    for both in PAIRS:
        known[np.ix_(both, both)] = pair_off
    trio = modal[9, 16]
    known[np.ix_(TRIO, TRIO)] = trio
    last = modal[21, 21]
    for group, own in ((NORMALS, normal_own), (sum(PAIRS, ()), pair_own), (TRIO, trio), (LASTS, last)):
        for degree in group:
            known[degree, degree] += own
    assert np.abs(known - modal).max() < 1e-12
    return tuple(float(v) for v in (shear, normal_off, normal_own, pair_off, pair_own, trio, last))


def weight_of(square):
    return max(0.0, RADIUS + 0.5 - float(np.sqrt(square)))


CLASSES = (0, 1, 2, 4, 5, 8, 9, 10)


def stiffness_of(physical):
    return STIFF_FLOOR + (1.0 - STIFF_FLOOR) * (physical * physical * physical)


def physical_of(density, kind):
    return jnp.where(kind == 1, 0.0, jnp.where(kind == 2, 1.0, density))


def factor_of(physical, kind):
    design = (kind != 1) & (kind != 2)
    return jnp.where(design, (-PENALTY * (1.0 - STIFF_FLOOR)) * (physical * physical), 0.0)


def pack_y(rows, cols, disp, dens, kind, out_a, out_b, mark, edge_d, edge_p, edge_k, sems):
    half = HALO // 2
    copies = []
    for side, start in ((0, 0), (half, cols - half)):
        for source, target in ((disp, edge_d), (dens, edge_p), (kind, edge_k)):
            lead = (slice(None),) * (len(source.shape) - 2)
            copies.append(
                pltpu.make_async_copy(
                    source.at[(*lead, pl.ds(start, half), slice(None))],
                    target.at[(*lead, pl.ds(side, half), slice(None))],
                    sems.at[len(copies)],
                )
            )
    for copy in copies:
        copy.start()
    for copy in copies:
        copy.wait()
    depth = disp.shape[-1]
    flat_d = edge_d.reshape(3 * rows * HALO, depth)
    flat_p = edge_p.reshape(rows * HALO, depth)
    flat_k = edge_k.reshape(rows * HALO, depth)

    def state(index):
        code = flat_k[pl.ds(index, rows, stride=HALO), :]
        return physical_of(flat_p[pl.ds(index, rows, stride=HALO), :], code), code

    def fill(low, high):
        slot = 0
        for c in range(3):
            for index in range(RADIUS + 1):
                low[pl.ds(slot * rows, rows), :] = flat_d[pl.ds(c * rows * HALO + index, rows, stride=HALO), :]
                slot += 1
        for index in range(RADIUS):
            low[pl.ds(slot * rows, rows), :] = factor_of(*state(index))
            slot += 1
        slot = 0
        for c in range(3):
            for index in range(HALO - RADIUS, HALO):
                high[pl.ds(slot * rows, rows), :] = flat_d[pl.ds(c * rows * HALO + index, rows, stride=HALO), :]
                slot += 1
        for index in range(HALO - RADIUS, HALO):
            physical, code = state(index)
            high[pl.ds(slot * rows, rows), :] = factor_of(physical, code)
            slot += 1
        high[pl.ds(slot * rows, rows), :] = stiffness_of(physical)

    mark[...] = jnp.zeros_like(mark)
    odd = lax.axis_index("gy") % 2

    @pl.when(odd == 0)
    def _():
        fill(out_b, out_a)

    @pl.when(odd == 1)
    def _():
        fill(out_a, out_b)


def unpack_y(rows, cols, count_y, after, disp, dens, kind, got_a, got_b, edge_u, edge_f, edge_s, out_a, out_b):
    del after
    here = lax.axis_index("gy")
    depth = disp.shape[-1]
    has_low = here > 0
    has_high = here < count_y - 1

    def fill(low, high):
        def put(ref, start, sublane, value):
            ref[pl.ds(start + sublane, rows, stride=HALO), :] = value

        zero = jnp.zeros((rows, depth), jnp.float32)
        slot = 0
        for c in range(3):
            for index in range(RADIUS + 1):
                put(edge_u, c * rows * HALO, index, jnp.where(has_high, high[pl.ds(slot * rows, rows), :], 0.0))
                slot += 1
        for index in range(RADIUS):
            put(edge_f, 0, index, jnp.where(has_high, high[pl.ds(slot * rows, rows), :], 0.0))
            slot += 1
        slot = 0
        for c in range(3):
            put(edge_u, c * rows * HALO, RADIUS + 1, zero)
            for index in range(HALO - RADIUS, HALO):
                put(edge_u, c * rows * HALO, index, low[pl.ds(slot * rows, rows), :])
                slot += 1
        for index in range(RADIUS, HALO - RADIUS):
            put(edge_f, 0, index, zero)
        for index in range(HALO - RADIUS, HALO):
            put(edge_f, 0, index, jnp.where(has_low, low[pl.ds(slot * rows, rows), :], 0.0))
            slot += 1
        edge_s[...] = jnp.zeros_like(edge_s)
        put(edge_s, 0, HALO - 1, jnp.where(has_low, low[pl.ds(slot * rows, rows), :], 0.0))

    odd = here % 2

    @pl.when(odd == 0)
    def _():
        fill(got_b, got_a)

    @pl.when(odd == 1)
    def _():
        fill(got_a, got_b)

    def send(out, row, with_stiff):
        for c in range(3):
            out[c, :cols, :] = disp[pl.ds((c * rows + row) * cols, cols), :]
            out[c, cols:, :] = edge_u[pl.ds((c * rows + row) * HALO, HALO), :]
        if with_stiff:
            at = pl.ds(row * cols, cols)
            out[3, :cols, :] = stiffness_of(physical_of(dens[at, :], kind[at, :]))
            out[3, cols:, :] = edge_s[pl.ds(row * HALO, HALO), :]
        else:
            out[3] = jnp.zeros_like(out[3])

    odd_x = lax.axis_index("gx") % 2

    @pl.when(odd_x == 0)
    def _():
        send(out_a, rows - 1, True)
        send(out_b, 0, False)

    @pl.when(odd_x == 1)
    def _():
        send(out_a, 0, False)
        send(out_b, rows - 1, True)


def loads_and_weights(rows, cols, count_x, count_y, after, load_x, load_y, load_z, force, sums, applied, inverse):
    del after
    depth = applied.shape[-1]
    place_x = lax.axis_index("gx") * rows
    place_y = lax.axis_index("gy") * cols
    local_x = load_x[...] - place_x
    local_y = load_y[...] - place_y
    owned = (local_x >= 0) & (local_x < rows) & (local_y >= 0) & (local_y < cols)
    target = jnp.where(owned, local_x * cols + local_y, -1)
    loads = target.shape[1]
    lanes = lax.broadcasted_iota(jnp.int32, (depth, loads), 0)
    hit_z = lanes == load_z[...]
    right = [[], []]
    for c in range(3):
        value = force[c : c + 1, :]
        coarse = value.astype(jnp.bfloat16).astype(jnp.float32)
        for part, piece in zip(right, (coarse, value - coarse)):
            part.append(jnp.where(hit_z, piece, 0.0).astype(jnp.bfloat16))
    place = lax.broadcasted_iota(jnp.int32, (rows * cols, loads), 0)
    left = jnp.where(place == target, 1.0, 0.0).astype(jnp.bfloat16)
    product = None
    for part in right:
        piece = lax.dot_general(
            left, jnp.concatenate(part, axis=0), (((1,), (1,)), ((), ())), preferred_element_type=jnp.float32
        )
        product = piece if product is None else product + piece
    for c in range(3):
        applied[c] = product[:, c * depth : (c + 1) * depth]

    wide = cols + HALO
    total_x, total_y = rows * count_x, cols * count_y
    sublane = lax.broadcasted_iota(jnp.int32, (wide, depth), 0)
    node_y = jnp.where(sublane >= wide - RADIUS, sublane - wide, sublane) + place_y
    inside_y = {
        shift: ((node_y + shift >= 0) & (node_y + shift < total_y)).astype(jnp.float32)
        for shift in range(-RADIUS, RADIUS + 1)
    }
    for kind in range(2 * RADIUS + 1):
        row = kind if kind <= RADIUS else rows - 2 * RADIUS - 1 + kind
        result = jnp.zeros((wide, depth), jnp.float32)
        for shift_y in range(-RADIUS, RADIUS + 1):
            line = jnp.zeros((1, depth), jnp.float32)
            for shift_x in range(-RADIUS, RADIUS + 1):
                square = shift_x * shift_x + shift_y * shift_y
                if square in CLASSES:
                    at = place_x + (row + shift_x)
                    inside = ((at >= 0) & (at < total_x)).astype(jnp.float32)
                    rank = CLASSES.index(square)
                    line = line + inside * sums[rank : rank + 1, :]
            result = result + inside_y[shift_y] * line
        inverse[kind] = 1.0 / jnp.where(result > 0.0, result, 1.0)


def shifted_z(value, lane, depth):
    beyond = jnp.where(lane == depth - 1, 0.0, pltpu.roll(value, depth - 1, 1))
    return value + beyond, beyond - value


def waves_of(here, there):
    return tuple(a + b for a, b in zip(here, there)) + tuple(b - a for a, b in zip(here, there))


def modal(before, after, stiff, constants):
    shear, normal_off, normal_own, pair_off, pair_own, trio, last = constants
    u = [None] * 24
    for low in range(12):
        if low >= 3:
            u[low] = before[low] + after[low]
        u[12 + low] = after[low] - before[low]
    f = [None] * 24
    terms = []

    def take(degree, pull):
        terms.append(pull * u[degree])
        f[degree] = pull * stiff

    for first, second in SHEARS:
        both = u[first] + u[second]
        pull = shear * both
        terms.append(pull * both)
        f[first] = f[second] = pull * stiff
    common = normal_off * (u[5] + u[7] + u[12])
    for degree in NORMALS:
        take(degree, common + normal_own * u[degree])
    for first, second in PAIRS:
        common = pair_off * (u[first] + u[second])
        take(first, common + pair_own * u[first])
        take(second, common + pair_own * u[second])
    common = u[9] + u[16] + u[20]
    for degree in TRIO:
        take(degree, trio * (common + u[degree]))
    for degree in LASTS:
        take(degree, last * u[degree])
    while len(terms) > 1:
        terms = [sum(terms[k : k + 2][1:], terms[k]) for k in range(0, len(terms), 2)]
    return terms[0], f


def lower_of(f):
    return tuple(f[12 + k] * -1.0 if f[k] is None else f[k] - f[12 + k] for k in range(12))


def upper_of(f):
    return tuple(f[12 + k] if f[k] is None else f[k] + f[12 + k] for k in range(12))


def along_y(g):
    return tuple(g[k] - g[6 + k] for k in range(6)), tuple(g[k] + g[6 + k] for k in range(6))


def along_z(g, lane):
    return [
        (g[c] - g[3 + c]) + jnp.where(lane == 0, 0.0, pltpu.roll(g[c] + g[3 + c], 1, 1)) for c in range(3)
    ]


def class_of(row, rows):
    return jnp.where(row < RADIUS, row, jnp.where(row >= rows - RADIUS, row - (rows - 2 * RADIUS - 1), RADIUS))


def march(rows, block, waves, state, inverse, near, far, put, own):
    constants = modal_constants()
    depth = waves.shape[-1]
    first = 8 * block
    zero = jnp.zeros((HALO, depth), jnp.float32)

    def nodes(row):
        return waves_of(
            [waves[k, row, first : first + 8, :] for k in range(6)],
            [waves[k, row, first + 1 : first + 9, :] for k in range(6)],
        )

    def finish(row, g):
        low, high = along_y(g)
        for k in range(6):
            if near is not None:
                near(k, row, low[k])
            far(k, row, high[k])

    def step(row, carry):
        before, held, total, filled = carry
        after = nodes(row + 1)
        physical, stiff, factor = state(row)
        energy, f = modal(before, after, stiff, constants)
        put(row, factor * energy * inverse[class_of(row, rows), first : first + 8, :])
        if own:
            total = total + stiff * energy
            filled = filled + physical
        finish(row, tuple(a + b for a, b in zip(held, lower_of(f))))
        return after, upper_of(f), total, filled

    carry = (nodes(0), (zero,) * 12, zero, zero)
    carry = lax.fori_loop(0, rows - 2, step, carry, unroll=UNROLL)
    _, held, total, filled = step(rows - 2, carry)
    finish(rows - 1, held)
    if own:
        filled = filled + state(rows - 1)[0]
    return total, filled


def own_state(dens, kind, cols, first):
    def state(row):
        at = pl.ds(pl.multiple_of(row * cols + first, 8), HALO)
        code = kind[at, :]
        physical = physical_of(dens[at, :], code)
        return physical, stiffness_of(physical), factor_of(physical, code)

    return state


def early_elements(rows, cols, disp, dens, kind, inverse, waves, near, far, scaled, sums):
    depth = disp.shape[-1]
    lane = lax.broadcasted_iota(jnp.int32, (HALO, depth), 1)

    def turn(row, nothing):
        for c in range(3):
            for block in range(cols // 8):
                at = pl.ds(pl.multiple_of((c * rows + row) * cols + 8 * block, 8), HALO)
                for r, value in enumerate(shifted_z(disp[at, :], lane, depth)):
                    waves[3 * r + c, row, 8 * block : 8 * block + 8, :] = value
                    if block == 0:
                        waves[3 * r + c, row, cols + HALO :, :] = value
        return nothing

    lax.fori_loop(0, rows, turn, 0, unroll=4)
    total = filled = jnp.zeros((HALO, depth), jnp.float32)
    for block in range(cols // 8 - 1):
        first = 8 * block

        def put_near(k, row, value, first=first):
            near[k, row, first : first + 8, :] = value

        def put_far(k, row, value, first=first):
            far[k, row, first + 1 : first + 9, :] = value

        def put(row, value, first=first):
            scaled[row, first : first + 8, :] = value

        state = own_state(dens, kind, cols, first)
        more = march(rows, block, waves, state, inverse, put_near, put_far, put, True)
        total, filled = total + more[0], filled + more[1]
    sums[0] = total
    sums[1] = filled


def late_elements(
    rows, cols,
    waves_in, dens, kind, edge_u, edge_f, edge_s, applied, inverse, near_a, far_a, scaled_a, sums_a,
    waves, resid, scaled, sums, near, far_h, far,
):
    depth = dens.shape[-1]
    del waves_in
    wide = cols + HALO
    lane = lax.broadcasted_iota(jnp.int32, (HALO, depth), 1)
    sublane = lax.broadcasted_iota(jnp.int32, (HALO, depth), 0)

    def turn(row, nothing):
        for c in range(3):
            at = pl.ds(pl.multiple_of((c * rows + row) * HALO, 8), HALO)
            for r, value in enumerate(shifted_z(edge_u[at, :], lane, depth)):
                waves[3 * r + c, row, cols:wide, :] = value
        return nothing

    lax.fori_loop(0, rows, turn, 0, unroll=8)

    def edge_state(row):
        at = pl.ds(pl.multiple_of(row * HALO, 8), HALO)
        return None, edge_s[at, :], edge_f[at, :]

    def put_edge(row, value):
        scaled[row, :HALO, :] = value
        scaled[row, wide:, :] = value

    def far_edge(k, row, value):
        far_h[k, row, 1:9, :] = value

    march(rows, cols // 8, waves, edge_state, inverse, None, far_edge, put_edge, False)
    last = cols // 8 - 1

    def put_near(k, row, value):
        near[k, row] = value

    def put_far(k, row, value):
        far[k, row, 1:9, :] = value

    def put(row, value):
        scaled[row, cols:wide, :] = value

    state = own_state(dens, kind, cols, 8 * last)
    total, filled = march(rows, last, waves, state, inverse, put_near, put_far, put, True)
    sums[0] = sums_a[0] + total
    sums[1] = sums_a[1] + filled

    def join(row, nothing):
        for block in range(last + 1):
            first = 8 * block
            parts = []
            for k in range(6):
                if block < last:
                    low, high = near_a[k, row, first : first + 8, :], far_a[k, row, first : first + 8, :]
                    if block == 0:
                        high = jnp.where(sublane == 0, far_h[k, row, 8:16, :], high)
                else:
                    low = near[k, row]
                    high = jnp.where(sublane == 0, far_a[k, row, first : first + 8, :], far[k, row, :8, :])
                parts.append(low + high)
            at = pl.ds(pl.multiple_of(row * cols + first, 8), HALO)
            for c, value in enumerate(along_z(parts, lane)):
                resid[c, at, :] = applied[c, at, :] - value
            if block < last:
                scaled[row, first + 8 : first + 16, :] = scaled_a[row, first : first + 8, :]
        return nothing

    lax.fori_loop(0, rows, join, 0, unroll=4)


def outer_elements(
    rows, cols, count_x, devices,
    waves, dens, kind, edge_f, edge_s, got_a, got_b, inner, scaled, sums, inverse,
    resid, final, out_a, out_b, parts, ring, stiff_low, carry_y,
):
    depth = dens.shape[-1]
    constants = modal_constants()
    wide = cols + HALO
    blocks = wide // HALO
    lane = lax.broadcasted_iota(jnp.int32, (HALO, depth), 1)
    here = lax.axis_index("gx")
    has_low = here > 0
    has_high = here < count_x - 1
    odd = here % 2

    def take(low, high):
        for block in range(blocks):
            first = 8 * block
            for c in range(3):
                for side, value in enumerate((low[c, first : first + 8, :], high[c, first : first + 8, :])):
                    if side:
                        value = jnp.where(has_high, value, 0.0)
                    for r, wave in enumerate(shifted_z(value, lane, depth)):
                        ring[side, 3 * r + c, first : first + 8, :] = wave
                        if block == 0:
                            ring[side, 3 * r + c, wide:, :] = wave
        stiff_low[...] = jnp.where(has_low, low[3], 0.0)

    @pl.when(odd == 0)
    def _():
        take(got_b, got_a)

    @pl.when(odd == 1)
    def _():
        take(got_a, got_b)

    total = sums[0]
    for block in (blocks - 1, *range(blocks - 1)):
        own = block < blocks - 1
        first = 8 * block

        def nodes(load):
            return waves_of(
                [load(k)[first : first + 8, :] for k in range(6)], [load(k)[first + 1 : first + 9, :] for k in range(6)]
            )

        line = [
            nodes(lambda k: ring.at[0, k]),
            nodes(lambda k: waves.at[k, 0]),
            nodes(lambda k: waves.at[k, rows - 1]),
            nodes(lambda k: ring.at[1, k]),
        ]
        _, f_low = modal(line[0], line[1], stiff_low[first : first + 8, :], constants)
        if own:
            _, stiff, factor = own_state(dens, kind, cols, first)(rows - 1)
        else:
            at = pl.ds((rows - 1) * HALO, HALO)
            stiff, factor = edge_s[at, :], edge_f[at, :]
        energy, f_high = modal(line[2], line[3], stiff, constants)
        value = factor * energy * inverse[2 * RADIUS, first : first + 8, :]
        if own:
            total = total + stiff * energy
            final[first + 8 : first + 16, :] = value
        else:
            final[:HALO, :] = value
            final[wide:, :] = value
        for index, (row, g) in enumerate(((0, upper_of(f_low)), (rows - 1, lower_of(f_high)))):
            low, high = along_y(g)
            if own:
                joined = []
                for k in range(6):
                    carry_y[index, k, first + 9 : first + 17, :] = high[k]
                    joined.append(low[k] + carry_y[index, k, first + 8 : first + 16, :])
                for c, value in enumerate(along_z(joined, lane)):
                    resid[index, c, first : first + 8, :] = inner[c, pl.ds(row * cols + first, HALO), :] - value
            else:
                for k in range(6):
                    carry_y[index, k, 1:9, :] = high[k]

    half = depth // 2
    pieces = []
    for value in (total, sums[1]):
        line = jnp.sum(value, axis=0, keepdims=True)
        pieces.append(line + pltpu.roll(line, half, 1))
    line = jnp.where(lax.broadcasted_iota(jnp.int32, (1, depth), 1) < half, pieces[0], pieces[1])
    parts[...] = jnp.broadcast_to(line, (devices, depth))

    def send(up, down):
        for index in range(RADIUS - 1):
            up[index] = scaled[rows - RADIUS + index, :wide, :]
        up[RADIUS - 1] = final[:wide, :]
        for index in range(RADIUS):
            down[index] = scaled[index, :wide, :]

    @pl.when(odd == 0)
    def _():
        send(out_a, out_b)

    @pl.when(odd == 1)
    def _():
        send(out_b, out_a)


def filter_rows(
    rows, cols, count_x, cells,
    scaled, final, got_a, got_b, parts, inner, outer,
    sens, resid, comp, vol, near, ends, result_v, sems,
):
    depth = sens.shape[-1]
    wide = cols + HALO
    copies = [
        pltpu.make_async_copy(
            inner.at[:, pl.ds(cols, (rows - 2) * cols), :], resid.at[:, pl.ds(cols, (rows - 2) * cols), :], sems.at[0]
        )
    ]
    for index, row in enumerate((0, rows - 1)):
        copies.append(
            pltpu.make_async_copy(outer.at[index], resid.at[:, pl.ds(row * cols, cols), :], sems.at[1 + index])
        )
    for copy in copies:
        copy.start()
    here = lax.axis_index("gx")
    has_low = here > 0
    has_high = here < count_x - 1
    odd = here % 2
    half = depth // 2
    line = jnp.sum(parts[...], axis=0, keepdims=True)
    first = lax.broadcasted_iota(jnp.int32, (1, depth), 1) < half
    compliance = jnp.sum(jnp.where(first, line, 0.0))
    volume = jnp.sum(jnp.where(first, 0.0, line))
    comp[0, 0] = compliance
    vol[0, 0] = volume / cells
    scale = cells / jnp.broadcast_to(compliance, (8, depth))

    def lines_y(row, load):
        for block in range(cols // 8):
            start = 8 + 8 * block
            near[0, row, 8 * block : 8 * block + 8, :] = load(start)
            for shift in range(1, RADIUS + 1):
                near[shift, row, 8 * block : 8 * block + 8, :] = load(start + shift) + load(start - shift)

    def take(low, high):
        for index in range(RADIUS):
            for source, has, at in ((low, has_low, index), (high, has_high, RADIUS + index)):
                value = jnp.where(has, source[index], 0.0)
                ends[at, :wide, :] = value
                ends[at, wide:, :] = value[:HALO]

    @pl.when(odd == 0)
    def _():
        take(got_b, got_a)

    @pl.when(odd == 1)
    def _():
        take(got_a, got_b)

    for index in range(RADIUS):
        lines_y(index, lambda start, at=index: ends[at, start : start + 8, :])
        lines_y(rows + RADIUS + index, lambda start, at=RADIUS + index: ends[at, start : start + 8, :])
    lines_y(rows + RADIUS - 1, lambda start: final[start : start + 8, :])

    def own(row, carry):
        lines_y(row + RADIUS, lambda start: scaled[row, start : start + 8, :])
        return carry

    lax.fori_loop(0, rows - 1, own, 0)
    lane = lax.broadcasted_iota(jnp.int32, (8, depth), 1)
    blocks = cols // 8

    def lines_of(row):
        lines = []
        for block in range(blocks):
            at = pl.ds(block * 8, 8)
            classes = {}
            for shift_x in range(RADIUS + 1):
                for shift_y in range(RADIUS + 1):
                    square = shift_x * shift_x + shift_y * shift_y
                    if square not in CLASSES:
                        continue
                    value = near[shift_y, row + (RADIUS + shift_x), at, :]
                    if shift_x:
                        value = value + near[shift_y, row + (RADIUS - shift_x), at, :]
                    classes[square] = value if square not in classes else classes[square] + value
            for shift_z in range(RADIUS + 1):
                line = None
                for square, value in classes.items():
                    weight = weight_of(square + shift_z * shift_z)
                    if weight > 0.0:
                        line = weight * value if line is None else line + weight * value
                lines.append(line)
        return tuple(lines)

    def write(row, lines):
        for block in range(blocks):
            result, *rest = lines[(RADIUS + 1) * block : (RADIUS + 1) * (block + 1)]
            for shift_z, line in enumerate(rest, 1):
                up = jnp.where(lane < shift_z, 0.0, pltpu.roll(line, shift_z, 1))
                down = jnp.where(lane >= depth - shift_z, 0.0, pltpu.roll(line, depth - shift_z, 1))
                result = result + (up + down)
            result_v[row, 8 * block : 8 * block + 8, :] = result * scale

    def out_row(row, lines):
        more = lines_of(row + 1)
        write(row, lines)
        return more

    pieces = 4
    size = rows // pieces
    lines = lines_of(0)
    for piece in range(pieces):
        last = piece == pieces - 1
        lines = lax.fori_loop(piece * size, (piece + 1) * size - (1 if last else 0), out_row, lines)
        if last:
            write(rows - 1, lines)
        at = pl.ds(piece * size, size)
        copies.append(pltpu.make_async_copy(result_v.at[at], sens.at[at], sems.at[3 + piece]))
        copies[-1].start()
    for copy in copies:
        copy.wait()


def call(body, shapes, inputs, scratch=(), places=None, out_places=None, flops=0, limit=24, aliases=None):
    places, out_places = places or {}, out_places or {}
    in_specs = [pl.BlockSpec(memory_space=places.get(rank, pltpu.VMEM)) for rank in range(len(inputs))]
    out_specs = [pl.BlockSpec(memory_space=out_places.get(rank, pltpu.VMEM)) for rank in range(len(shapes))]
    moved = sum(int(np.prod(v.shape)) * 4 for v in list(inputs) + list(shapes))
    return pl.pallas_call(
        body,
        out_shape=[FULL(v.shape, v.dtype) for v in shapes],
        in_specs=in_specs,
        out_specs=out_specs,
        scratch_shapes=list(scratch),
        input_output_aliases=aliases or {},
        cost_estimate=pl.CostEstimate(flops=flops, bytes_accessed=moved, transcendentals=0),
        compiler_params=pltpu.CompilerParams(vmem_limit_bytes=int(limit * 1024 * 1024)),
    )(*inputs)


def f32(*shape):
    return FULL(shape, jnp.float32)


def vmem(*shape, dtype=jnp.float32):
    return pltpu.VMEM(shape, dtype)


def on_device(count_x, count_y, displacement, density, element_kind, load_x, load_y, load_z, load_force):
    rows, cols, depth = density.shape
    wide = cols + HALO
    devices = count_x * count_y
    cells = float(rows * cols * depth * devices)

    pairs_ya = [(k, k ^ 1) for k in range(count_y)]
    pairs_xa = [(k, k ^ 1) for k in range(count_x)]
    pairs_yb, pairs_xb = [], []
    for i in range(count_x):
        for j in range(count_y):
            here = i * count_y + j
            inside_y, inside_x = 0 < j < count_y - 1, 0 < i < count_x - 1
            pairs_yb.append((here, i * count_y + ((j + 1) ^ 1) - 1 if inside_y else (i ^ 1) * count_y + j))
            pairs_xb.append((here, (((i + 1) ^ 1) - 1) * count_y + j if inside_x else i * count_y + (j ^ 1)))

    disp = displacement.reshape(3 * rows * cols, depth)
    dens = density.reshape(rows * cols, depth)
    kind = element_kind.reshape(rows * cols, depth)

    slots = 4 * RADIUS + RADIUS
    send_a, send_b, mark = call(
        functools.partial(pack_y, rows, cols),
        [f32(slots * rows, depth)] * 2 + [f32(8, depth)],
        [displacement, density, element_kind],
        scratch=[
            vmem(3, rows, HALO, depth),
            vmem(rows, HALO, depth),
            vmem(rows, HALO, depth, dtype=jnp.int32),
            pltpu.SemaphoreType.DMA((6,)),
        ],
        places={0: pltpu.HBM, 1: pltpu.HBM, 2: pltpu.HBM},
        limit=53.25,
    )
    got_a = lax.ppermute(send_a, "gy", pairs_ya)
    got_b = lax.ppermute(send_b, BOTH, pairs_yb)

    sums = np.zeros((8, depth), np.float32)
    for rank, square in enumerate(CLASSES):
        for z in range(depth):
            sums[rank, z] = sum(
                weight_of(square + s * s) for s in range(-RADIUS, RADIUS + 1) if 0 <= z + s < depth
            )
    count = load_x.shape[0]
    applied, inverse = call(
        functools.partial(loads_and_weights, rows, cols, count_x, count_y),
        [f32(3, rows * cols, depth), f32(2 * RADIUS + 1, wide, depth)],
        [mark, load_x.reshape(1, count), load_y.reshape(1, count), load_z.reshape(1, count), load_force, jnp.asarray(sums)],
        places={0: pl.ANY},
        flops=2 * rows * cols * count * 6 * depth,
    )

    early = cols - HALO
    waves, near_a, far_a, scaled_a, sums_a = call(
        functools.partial(early_elements, rows, cols),
        [
            f32(6, rows, wide + HALO, depth),
            f32(6, rows, early, depth),
            f32(6, rows, cols, depth),
            f32(rows, early, depth),
            f32(2, 8, depth),
        ],
        [disp, dens, kind, inverse],
        flops=250 * rows * early * depth,
    )

    edge_u, edge_f, edge_s, send_a, send_b = call(
        functools.partial(unpack_y, rows, cols, count_y),
        [f32(3 * rows * HALO, depth), f32(rows * HALO, depth), f32(rows * HALO, depth)] + [f32(4, wide, depth)] * 2,
        [sums_a, disp, dens, kind, got_a, got_b],
        places={0: pl.ANY},
    )
    got_a = lax.ppermute(send_a, "gx", pairs_xa)
    got_b = lax.ppermute(send_b, BOTH, pairs_xb)

    waves, inner, scaled, sums = call(
        functools.partial(late_elements, rows, cols),
        [f32(6, rows, wide + HALO, depth), f32(3, rows * cols, depth), f32(rows, wide + HALO, depth), f32(2, 8, depth)],
        [waves, dens, kind, edge_u, edge_f, edge_s, applied, inverse, near_a, far_a, scaled_a, sums_a],
        scratch=[vmem(6, rows, HALO, depth), vmem(6, rows, 2 * HALO, depth), vmem(6, rows, 2 * HALO, depth)],
        flops=250 * rows * 2 * HALO * depth,
        aliases={0: 0},
    )
    outer, final, send_a, send_b, parts = call(
        functools.partial(outer_elements, rows, cols, count_x, devices),
        [f32(2, 3, cols, depth), f32(wide + HALO, depth)] + [f32(RADIUS, wide, depth)] * 2 + [f32(devices, depth)],
        [waves, dens, kind, edge_f, edge_s, got_a, got_b, inner, scaled, sums, inverse],
        scratch=[vmem(2, 6, wide + HALO, depth), vmem(wide, depth), vmem(2, 6, wide + 2 * HALO, depth)],
        flops=500 * wide * depth,
    )
    got_a = lax.ppermute(send_a, "gx", pairs_xa)
    got_b = lax.ppermute(send_b, BOTH, pairs_xb)
    parts = lax.all_to_all(parts, BOTH, 0, 0, tiled=True)

    sens, resid, comp, volume = call(
        functools.partial(filter_rows, rows, cols, count_x, cells),
        [f32(rows, cols, depth), f32(3, rows * cols, depth), f32(1, 1), f32(1, 1)],
        [scaled, final, got_a, got_b, parts, inner, outer],
        scratch=[
            vmem(RADIUS + 1, rows + 2 * RADIUS, cols, depth),
            vmem(2 * RADIUS, wide + HALO, depth),
            vmem(rows, cols, depth),
            pltpu.SemaphoreType.DMA((7,)),
        ],
        out_places={0: pltpu.HBM, 1: pltpu.HBM, 2: pltpu.SMEM, 3: pltpu.SMEM},
        flops=60 * rows * cols * depth,
    )
    return (
        sens,
        resid.reshape(3, rows, cols, depth),
        comp.reshape(()),
        volume.reshape(()),
    )


def solution(mesh):
    placed = (
        P(None, "gx", "gy", None),
        P("gx", "gy", None),
        P("gx", "gy", None),
        P(),
        P(),
        P(),
        P(),
    )
    return jax.shard_map(
        functools.partial(on_device, mesh.shape["gx"], mesh.shape["gy"]),
        mesh=mesh,
        in_specs=placed,
        out_specs=(P("gx", "gy", None), P(None, "gx", "gy", None), P(), P()),
        check_vma=False,
    )
```

```python
import functools

import jax
import jax.numpy as jnp
import numpy as np
from jax import lax
from jax.experimental import pallas as pl
from jax.experimental.pallas import tpu as pltpu
from jax.sharding import PartitionSpec as P

RADIUS = 3
PENALTY = 3.0
STIFF_FLOOR = 0.001
POISSON = 0.3
HALO = 8
BOTH = ("gx", "gy")
FULL = jax.ShapeDtypeStruct
UNROLL = 5


def element_matrix():
    lame_first = POISSON / ((1.0 + POISSON) * (1.0 - 2.0 * POISSON))
    shear_modulus = 0.5 / (1.0 + POISSON)
    material = np.zeros((6, 6))
    material[:3, :3] = lame_first
    for diagonal in range(3):
        material[diagonal, diagonal] += 2.0 * shear_modulus
        material[diagonal + 3, diagonal + 3] = shear_modulus
    points = [0.5 - 0.5 / np.sqrt(3.0), 0.5 + 0.5 / np.sqrt(3.0)]
    corners = [(a, b, e) for a in (0, 1) for b in (0, 1) for e in (0, 1)]
    result = np.zeros((24, 24))
    for point_x in points:
        for point_y in points:
            for point_z in points:
                strain = np.zeros((6, 24))
                for corner, (side_x, side_y, side_z) in enumerate(corners):
                    value_x = point_x if side_x else 1.0 - point_x
                    value_y = point_y if side_y else 1.0 - point_y
                    value_z = point_z if side_z else 1.0 - point_z
                    slope_x = (1.0 if side_x else -1.0) * value_y * value_z
                    slope_y = value_x * (1.0 if side_y else -1.0) * value_z
                    slope_z = value_x * value_y * (1.0 if side_z else -1.0)
                    column = 3 * corner
                    strain[0, column] = slope_x
                    strain[1, column + 1] = slope_y
                    strain[2, column + 2] = slope_z
                    strain[3, column] = slope_y
                    strain[3, column + 1] = slope_x
                    strain[4, column + 1] = slope_z
                    strain[4, column + 2] = slope_y
                    strain[5, column + 2] = slope_x
                    strain[5, column] = slope_z
                result += strain.T @ material @ strain / 8.0
    return result


def modal_matrix():
    pair = np.array([[1.0, 1.0], [-1.0, 1.0]])
    turn = np.kron(np.kron(np.kron(pair, pair), pair), np.eye(3))
    return turn @ element_matrix() @ turn.T / 64.0


SHEARS = ((3, 14), (4, 8), (6, 13))
NORMALS = (5, 7, 12)
PAIRS = ((10, 15), (11, 18), (17, 19))
TRIO = (9, 16, 20)
LASTS = (21, 22, 23)


def modal_constants():
    modal = modal_matrix()
    known = np.zeros((24, 24))
    shear = modal[3, 3]
    for first, second in SHEARS:
        known[np.ix_((first, second), (first, second))] = shear
    normal_off = modal[5, 7]
    normal_own = modal[5, 5] - normal_off
    known[np.ix_(NORMALS, NORMALS)] = normal_off
    pair_off = modal[10, 15]
    pair_own = modal[10, 10] - pair_off
    for both in PAIRS:
        known[np.ix_(both, both)] = pair_off
    trio = modal[9, 16]
    known[np.ix_(TRIO, TRIO)] = trio
    last = modal[21, 21]
    for group, own in ((NORMALS, normal_own), (sum(PAIRS, ()), pair_own), (TRIO, trio), (LASTS, last)):
        for degree in group:
            known[degree, degree] += own
    assert np.abs(known - modal).max() < 1e-12
    return tuple(float(v) for v in (shear, normal_off, normal_own, pair_off, pair_own, trio, last))


def weight_of(square):
    return max(0.0, RADIUS + 0.5 - float(np.sqrt(square)))


CLASSES = (0, 1, 2, 4, 5, 8, 9, 10)


def stiffness_of(physical):
    return STIFF_FLOOR + (1.0 - STIFF_FLOOR) * (physical * physical * physical)


def physical_of(density, kind):
    return jnp.where(kind == 1, 0.0, jnp.where(kind == 2, 1.0, density))


def factor_of(physical, kind):
    design = (kind != 1) & (kind != 2)
    return jnp.where(design, (-PENALTY * (1.0 - STIFF_FLOOR)) * (physical * physical), 0.0)


def pack_y(rows, cols, disp, dens, kind, out_a, out_b, mark, edge_d, edge_p, edge_k, sems):
    half = HALO // 2
    copies = []
    for side, start in ((0, 0), (half, cols - half)):
        for source, target in ((disp, edge_d), (dens, edge_p), (kind, edge_k)):
            lead = (slice(None),) * (len(source.shape) - 2)
            copies.append(
                pltpu.make_async_copy(
                    source.at[(*lead, pl.ds(start, half), slice(None))],
                    target.at[(*lead, pl.ds(side, half), slice(None))],
                    sems.at[len(copies)],
                )
            )
    for copy in copies:
        copy.start()
    for copy in copies:
        copy.wait()
    depth = disp.shape[-1]
    flat_d = edge_d.reshape(3 * rows * HALO, depth)
    flat_p = edge_p.reshape(rows * HALO, depth)
    flat_k = edge_k.reshape(rows * HALO, depth)

    def state(index):
        code = flat_k[pl.ds(index, rows, stride=HALO), :]
        return physical_of(flat_p[pl.ds(index, rows, stride=HALO), :], code), code

    def fill(low, high):
        slot = 0
        for c in range(3):
            for index in range(RADIUS + 1):
                low[pl.ds(slot * rows, rows), :] = flat_d[pl.ds(c * rows * HALO + index, rows, stride=HALO), :]
                slot += 1
        for index in range(RADIUS):
            low[pl.ds(slot * rows, rows), :] = factor_of(*state(index))
            slot += 1
        slot = 0
        for c in range(3):
            for index in range(HALO - RADIUS, HALO):
                high[pl.ds(slot * rows, rows), :] = flat_d[pl.ds(c * rows * HALO + index, rows, stride=HALO), :]
                slot += 1
        for index in range(HALO - RADIUS, HALO):
            physical, code = state(index)
            high[pl.ds(slot * rows, rows), :] = factor_of(physical, code)
            slot += 1
        high[pl.ds(slot * rows, rows), :] = stiffness_of(physical)

    mark[...] = jnp.zeros_like(mark)
    odd = lax.axis_index("gy") % 2

    @pl.when(odd == 0)
    def _():
        fill(out_b, out_a)

    @pl.when(odd == 1)
    def _():
        fill(out_a, out_b)


def unpack_y(rows, cols, count_y, after, disp, dens, kind, got_a, got_b, edge_u, edge_f, edge_s, out_a, out_b):
    del after
    here = lax.axis_index("gy")
    depth = disp.shape[-1]
    has_low = here > 0
    has_high = here < count_y - 1

    def fill(low, high):
        def put(ref, start, sublane, value):
            ref[pl.ds(start + sublane, rows, stride=HALO), :] = value

        zero = jnp.zeros((rows, depth), jnp.float32)
        slot = 0
        for c in range(3):
            for index in range(RADIUS + 1):
                put(edge_u, c * rows * HALO, index, jnp.where(has_high, high[pl.ds(slot * rows, rows), :], 0.0))
                slot += 1
        for index in range(RADIUS):
            put(edge_f, 0, index, jnp.where(has_high, high[pl.ds(slot * rows, rows), :], 0.0))
            slot += 1
        slot = 0
        for c in range(3):
            put(edge_u, c * rows * HALO, RADIUS + 1, zero)
            for index in range(HALO - RADIUS, HALO):
                put(edge_u, c * rows * HALO, index, low[pl.ds(slot * rows, rows), :])
                slot += 1
        for index in range(RADIUS, HALO - RADIUS):
            put(edge_f, 0, index, zero)
        for index in range(HALO - RADIUS, HALO):
            put(edge_f, 0, index, jnp.where(has_low, low[pl.ds(slot * rows, rows), :], 0.0))
            slot += 1
        edge_s[...] = jnp.zeros_like(edge_s)
        put(edge_s, 0, HALO - 1, jnp.where(has_low, low[pl.ds(slot * rows, rows), :], 0.0))

    odd = here % 2

    @pl.when(odd == 0)
    def _():
        fill(got_b, got_a)

    @pl.when(odd == 1)
    def _():
        fill(got_a, got_b)

    def send(out, row, with_stiff):
        for c in range(3):
            out[c, :cols, :] = disp[pl.ds((c * rows + row) * cols, cols), :]
            out[c, cols:, :] = edge_u[pl.ds((c * rows + row) * HALO, HALO), :]
        if with_stiff:
            at = pl.ds(row * cols, cols)
            out[3, :cols, :] = stiffness_of(physical_of(dens[at, :], kind[at, :]))
            out[3, cols:, :] = edge_s[pl.ds(row * HALO, HALO), :]
        else:
            out[3] = jnp.zeros_like(out[3])

    odd_x = lax.axis_index("gx") % 2

    @pl.when(odd_x == 0)
    def _():
        send(out_a, rows - 1, True)
        send(out_b, 0, False)

    @pl.when(odd_x == 1)
    def _():
        send(out_a, 0, False)
        send(out_b, rows - 1, True)


def loads_and_weights(rows, cols, count_x, count_y, after, load_x, load_y, load_z, force, sums, applied, inverse):
    del after
    depth = applied.shape[-1]
    place_x = lax.axis_index("gx") * rows
    place_y = lax.axis_index("gy") * cols
    local_x = load_x[...] - place_x
    local_y = load_y[...] - place_y
    owned = (local_x >= 0) & (local_x < rows) & (local_y >= 0) & (local_y < cols)
    target = jnp.where(owned, local_x * cols + local_y, -1)
    loads = target.shape[1]
    lanes = lax.broadcasted_iota(jnp.int32, (depth, loads), 0)
    hit_z = lanes == load_z[...]
    right = [[], []]
    for c in range(3):
        value = force[c : c + 1, :]
        coarse = value.astype(jnp.bfloat16).astype(jnp.float32)
        for part, piece in zip(right, (coarse, value - coarse)):
            part.append(jnp.where(hit_z, piece, 0.0).astype(jnp.bfloat16))
    place = lax.broadcasted_iota(jnp.int32, (rows * cols, loads), 0)
    left = jnp.where(place == target, 1.0, 0.0).astype(jnp.bfloat16)
    product = None
    for part in right:
        piece = lax.dot_general(
            left, jnp.concatenate(part, axis=0), (((1,), (1,)), ((), ())), preferred_element_type=jnp.float32
        )
        product = piece if product is None else product + piece
    for c in range(3):
        applied[c] = product[:, c * depth : (c + 1) * depth]

    wide = cols + HALO
    total_x, total_y = rows * count_x, cols * count_y
    sublane = lax.broadcasted_iota(jnp.int32, (wide, depth), 0)
    node_y = jnp.where(sublane >= wide - RADIUS, sublane - wide, sublane) + place_y
    inside_y = {
        shift: ((node_y + shift >= 0) & (node_y + shift < total_y)).astype(jnp.float32)
        for shift in range(-RADIUS, RADIUS + 1)
    }
    for kind in range(2 * RADIUS + 1):
        row = kind if kind <= RADIUS else rows - 2 * RADIUS - 1 + kind
        result = jnp.zeros((wide, depth), jnp.float32)
        for shift_y in range(-RADIUS, RADIUS + 1):
            line = jnp.zeros((1, depth), jnp.float32)
            for shift_x in range(-RADIUS, RADIUS + 1):
                square = shift_x * shift_x + shift_y * shift_y
                if square in CLASSES:
                    at = place_x + (row + shift_x)
                    inside = ((at >= 0) & (at < total_x)).astype(jnp.float32)
                    rank = CLASSES.index(square)
                    line = line + inside * sums[rank : rank + 1, :]
            result = result + inside_y[shift_y] * line
        inverse[kind] = 1.0 / jnp.where(result > 0.0, result, 1.0)


def shifted_z(value, lane, depth):
    beyond = jnp.where(lane == depth - 1, 0.0, pltpu.roll(value, depth - 1, 1))
    return value + beyond, beyond - value


def waves_of(here, there):
    return tuple(a + b for a, b in zip(here, there)) + tuple(b - a for a, b in zip(here, there))


def modal(before, after, stiff, constants):
    shear, normal_off, normal_own, pair_off, pair_own, trio, last = constants
    u = [None] * 24
    for low in range(12):
        if low >= 3:
            u[low] = before[low] + after[low]
        u[12 + low] = after[low] - before[low]
    f = [None] * 24
    terms = []

    def take(degree, pull):
        terms.append(pull * u[degree])
        f[degree] = pull * stiff

    for first, second in SHEARS:
        both = u[first] + u[second]
        pull = shear * both
        terms.append(pull * both)
        f[first] = f[second] = pull * stiff
    common = normal_off * (u[5] + u[7] + u[12])
    for degree in NORMALS:
        take(degree, common + normal_own * u[degree])
    for first, second in PAIRS:
        common = pair_off * (u[first] + u[second])
        take(first, common + pair_own * u[first])
        take(second, common + pair_own * u[second])
    common = u[9] + u[16] + u[20]
    for degree in TRIO:
        take(degree, trio * (common + u[degree]))
    for degree in LASTS:
        take(degree, last * u[degree])
    while len(terms) > 1:
        terms = [sum(terms[k : k + 2][1:], terms[k]) for k in range(0, len(terms), 2)]
    return terms[0], f


def lower_of(f):
    return tuple(f[12 + k] * -1.0 if f[k] is None else f[k] - f[12 + k] for k in range(12))


def upper_of(f):
    return tuple(f[12 + k] if f[k] is None else f[k] + f[12 + k] for k in range(12))


def along_y(g):
    return tuple(g[k] - g[6 + k] for k in range(6)), tuple(g[k] + g[6 + k] for k in range(6))


def along_z(g, lane):
    return [
        (g[c] - g[3 + c]) + jnp.where(lane == 0, 0.0, pltpu.roll(g[c] + g[3 + c], 1, 1)) for c in range(3)
    ]


def class_of(row, rows):
    return jnp.where(row < RADIUS, row, jnp.where(row >= rows - RADIUS, row - (rows - 2 * RADIUS - 1), RADIUS))


def march(rows, block, waves, state, inverse, near, far, put, own, beside=None):
    constants = modal_constants()
    depth = waves.shape[-1]
    first = 8 * block
    zero = jnp.zeros((HALO, depth), jnp.float32)

    def nodes(row):
        return waves_of(
            [waves[k, row, first : first + 8, :] for k in range(6)],
            [waves[k, row, first + 1 : first + 9, :] for k in range(6)],
        )

    def finish(row, g):
        low, high = along_y(g)
        for k in range(6):
            if near is not None:
                near(k, row, low[k])
            far(k, row, high[k])

    def step(row, carry):
        before, held, total, filled = carry
        if beside is not None:
            beside(row)
        after = nodes(row + 1)
        physical, stiff, factor = state(row)
        energy, f = modal(before, after, stiff, constants)
        put(row, factor * energy * inverse[class_of(row, rows), first : first + 8, :])
        if own:
            total = total + stiff * energy
            filled = filled + physical
        finish(row, tuple(a + b for a, b in zip(held, lower_of(f))))
        return after, upper_of(f), total, filled

    carry = (nodes(0), (zero,) * 12, zero, zero)
    carry = lax.fori_loop(0, rows - 2, step, carry, unroll=UNROLL)
    _, held, total, filled = step(rows - 2, carry)
    finish(rows - 1, held)
    if own:
        filled = filled + state(rows - 1)[0]
    return total, filled


def own_state(dens, kind, cols, first):
    def state(row):
        at = pl.ds(pl.multiple_of(row * cols + first, 8), HALO)
        code = kind[at, :]
        physical = physical_of(dens[at, :], code)
        return physical, stiffness_of(physical), factor_of(physical, code)

    return state


def joiner(rows, cols, block, near, far, applied, resid, lane):
    first = 8 * block

    def put_near(k, row, value):
        near[k, row] = value

    def put_far(k, row, value):
        far[k, row, first + 1 : first + 9, :] = value

    def join(row):
        parts = [near[k, row] + far[k, row, first : first + 8, :] for k in range(6)]
        at = pl.ds(pl.multiple_of(row * cols + first, 8), HALO)
        for c, value in enumerate(along_z(parts, lane)):
            resid[c, at, :] = applied[c, at, :] - value

    def finish():
        join(rows - 2)
        join(rows - 1)

    return put_near, put_far, lambda row: join(jnp.maximum(row - 1, 0)), finish


def early_elements(
    rows, cols, disp, dens, kind, inverse, applied, waves, far, resid, scaled, sums, near
):
    depth = disp.shape[-1]
    lane = lax.broadcasted_iota(jnp.int32, (HALO, depth), 1)

    def turn(row, nothing):
        for c in range(3):
            for block in range(cols // 8):
                at = pl.ds(pl.multiple_of((c * rows + row) * cols + 8 * block, 8), HALO)
                for r, value in enumerate(shifted_z(disp[at, :], lane, depth)):
                    waves[3 * r + c, row, 8 * block : 8 * block + 8, :] = value
                    if block == 0:
                        waves[3 * r + c, row, cols + HALO :, :] = value
        for k in range(6):
            far[k, row, :8, :] = jnp.zeros((HALO, depth), jnp.float32)
        return nothing

    lax.fori_loop(0, rows, turn, 0, unroll=8)
    total = filled = jnp.zeros((HALO, depth), jnp.float32)
    for block in range(cols // 8 - 1):
        first = 8 * block

        def put(row, value, first=first):
            scaled[row, first + 8 : first + 16, :] = value

        put_near, put_far, beside, finish = joiner(rows, cols, block, near, far, applied, resid, lane)
        state = own_state(dens, kind, cols, first)
        more = march(rows, block, waves, state, inverse, put_near, put_far, put, True, beside=beside)
        finish()
        total, filled = total + more[0], filled + more[1]
    sums[0] = total
    sums[1] = filled


def late_elements(
    rows, cols,
    waves_in, far_in, resid_in, scaled_in, dens, kind, edge_u, edge_f, edge_s, applied, inverse, sums_a,
    waves, far, resid, scaled, sums, near, far_h,
):
    depth = dens.shape[-1]
    del waves_in, far_in, resid_in, scaled_in
    wide = cols + HALO
    lane = lax.broadcasted_iota(jnp.int32, (HALO, depth), 1)

    def turn(row, nothing):
        for c in range(3):
            at = pl.ds(pl.multiple_of((c * rows + row) * HALO, 8), HALO)
            for r, value in enumerate(shifted_z(edge_u[at, :], lane, depth)):
                waves[3 * r + c, row, cols:wide, :] = value
        return nothing

    lax.fori_loop(0, rows, turn, 0, unroll=16)

    def edge_state(row):
        at = pl.ds(pl.multiple_of(row * HALO, 8), HALO)
        return None, edge_s[at, :], edge_f[at, :]

    def put_edge(row, value):
        scaled[row, :HALO, :] = value
        scaled[row, wide:, :] = value

    def far_edge(k, row, value):
        far_h[pl.ds(pl.multiple_of((k * rows + row) * HALO, 8), HALO), :] = value

    march(rows, cols // 8, waves, edge_state, inverse, None, far_edge, put_edge, False)
    last = cols // 8 - 1

    def put(row, value):
        scaled[row, cols:wide, :] = value

    put_near, put_far, beside, finish = joiner(rows, cols, last, near, far, applied, resid, lane)
    state = own_state(dens, kind, cols, 8 * last)
    total, filled = march(rows, last, waves, state, inverse, put_near, put_far, put, True, beside=beside)
    finish()
    sums[0] = sums_a[0] + total
    sums[1] = sums_a[1] + filled

    parts = [far_h[pl.ds(k * rows * HALO + HALO - 1, rows, stride=HALO), :] for k in range(6)]
    at = pl.ds(0, rows, stride=cols)
    for c, value in enumerate(along_z(parts, lax.broadcasted_iota(jnp.int32, (rows, depth), 1))):
        resid[c, at, :] = resid[c, at, :] - value


def outer_elements(
    rows, cols, count_x, devices,
    waves, dens, kind, edge_f, edge_s, got_a, got_b, inner, scaled, sums, inverse,
    resid, final, out_a, out_b, parts, ring, stiff_low, carry_y,
):
    depth = dens.shape[-1]
    constants = modal_constants()
    wide = cols + HALO
    blocks = wide // HALO
    lane = lax.broadcasted_iota(jnp.int32, (HALO, depth), 1)
    here = lax.axis_index("gx")
    has_low = here > 0
    has_high = here < count_x - 1
    odd = here % 2

    def take(low, high):
        for block in range(blocks):
            first = 8 * block
            for c in range(3):
                for side, value in enumerate((low[c, first : first + 8, :], high[c, first : first + 8, :])):
                    if side:
                        value = jnp.where(has_high, value, 0.0)
                    for r, wave in enumerate(shifted_z(value, lane, depth)):
                        ring[side, 3 * r + c, first : first + 8, :] = wave
                        if block == 0:
                            ring[side, 3 * r + c, wide:, :] = wave
        stiff_low[...] = jnp.where(has_low, low[3], 0.0)

    @pl.when(odd == 0)
    def _():
        take(got_b, got_a)

    @pl.when(odd == 1)
    def _():
        take(got_a, got_b)

    total = sums[0]
    for block in (blocks - 1, *range(blocks - 1)):
        own = block < blocks - 1
        first = 8 * block

        def nodes(load):
            return waves_of(
                [load(k)[first : first + 8, :] for k in range(6)], [load(k)[first + 1 : first + 9, :] for k in range(6)]
            )

        line = [
            nodes(lambda k: ring.at[0, k]),
            nodes(lambda k: waves.at[k, 0]),
            nodes(lambda k: waves.at[k, rows - 1]),
            nodes(lambda k: ring.at[1, k]),
        ]
        _, f_low = modal(line[0], line[1], stiff_low[first : first + 8, :], constants)
        if own:
            _, stiff, factor = own_state(dens, kind, cols, first)(rows - 1)
        else:
            at = pl.ds((rows - 1) * HALO, HALO)
            stiff, factor = edge_s[at, :], edge_f[at, :]
        energy, f_high = modal(line[2], line[3], stiff, constants)
        value = factor * energy * inverse[2 * RADIUS, first : first + 8, :]
        if own:
            total = total + stiff * energy
            final[first + 8 : first + 16, :] = value
        else:
            final[:HALO, :] = value
            final[wide:, :] = value
        for index, (row, g) in enumerate(((0, upper_of(f_low)), (rows - 1, lower_of(f_high)))):
            low, high = along_y(g)
            if own:
                joined = []
                for k in range(6):
                    carry_y[index, k, first + 9 : first + 17, :] = high[k]
                    joined.append(low[k] + carry_y[index, k, first + 8 : first + 16, :])
                for c, value in enumerate(along_z(joined, lane)):
                    resid[index, c, first : first + 8, :] = inner[c, pl.ds(row * cols + first, HALO), :] - value
            else:
                for k in range(6):
                    carry_y[index, k, 1:9, :] = high[k]

    half = depth // 2
    pieces = []
    for value in (total, sums[1]):
        line = jnp.sum(value, axis=0, keepdims=True)
        pieces.append(line + pltpu.roll(line, half, 1))
    line = jnp.where(lax.broadcasted_iota(jnp.int32, (1, depth), 1) < half, pieces[0], pieces[1])
    parts[...] = jnp.broadcast_to(line, (devices, depth))

    def send(up, down):
        for index in range(RADIUS - 1):
            up[index] = scaled[rows - RADIUS + index, :wide, :]
        up[RADIUS - 1] = final[:wide, :]
        for index in range(RADIUS):
            down[index] = scaled[index, :wide, :]

    @pl.when(odd == 0)
    def _():
        send(out_a, out_b)

    @pl.when(odd == 1)
    def _():
        send(out_b, out_a)


def filter_rows(
    rows, cols, count_x, cells,
    scaled, final, got_a, got_b, parts, inner, outer,
    sens, resid, comp, vol, near, ends, result_v, sems,
):
    depth = sens.shape[-1]
    wide = cols + HALO
    copies = [
        pltpu.make_async_copy(
            inner.at[:, pl.ds(cols, (rows - 2) * cols), :], resid.at[:, pl.ds(cols, (rows - 2) * cols), :], sems.at[0]
        )
    ]
    for index, row in enumerate((0, rows - 1)):
        copies.append(
            pltpu.make_async_copy(outer.at[index], resid.at[:, pl.ds(row * cols, cols), :], sems.at[1 + index])
        )
    for copy in copies:
        copy.start()
    here = lax.axis_index("gx")
    has_low = here > 0
    has_high = here < count_x - 1
    odd = here % 2
    half = depth // 2
    line = jnp.sum(parts[...], axis=0, keepdims=True)
    first = lax.broadcasted_iota(jnp.int32, (1, depth), 1) < half
    compliance = jnp.sum(jnp.where(first, line, 0.0))
    volume = jnp.sum(jnp.where(first, 0.0, line))
    comp[0, 0] = compliance
    vol[0, 0] = volume / cells
    scale = cells / jnp.broadcast_to(compliance, (8, depth))

    def lines_y(row, load):
        for block in range(cols // 8):
            start = 8 + 8 * block
            near[0, row, 8 * block : 8 * block + 8, :] = load(start)
            for shift in range(1, RADIUS + 1):
                near[shift, row, 8 * block : 8 * block + 8, :] = load(start + shift) + load(start - shift)

    def take(low, high):
        for index in range(RADIUS):
            for source, has, at in ((low, has_low, index), (high, has_high, RADIUS + index)):
                value = jnp.where(has, source[index], 0.0)
                ends[at, :wide, :] = value
                ends[at, wide:, :] = value[:HALO]

    @pl.when(odd == 0)
    def _():
        take(got_b, got_a)

    @pl.when(odd == 1)
    def _():
        take(got_a, got_b)

    for index in range(RADIUS):
        lines_y(index, lambda start, at=index: ends[at, start : start + 8, :])
        lines_y(rows + RADIUS + index, lambda start, at=RADIUS + index: ends[at, start : start + 8, :])
    lines_y(rows + RADIUS - 1, lambda start: final[start : start + 8, :])

    def own(row, carry):
        lines_y(row + RADIUS, lambda start: scaled[row, start : start + 8, :])
        return carry

    lax.fori_loop(0, rows - 1, own, 0, unroll=True)
    lane = lax.broadcasted_iota(jnp.int32, (8, depth), 1)
    blocks = cols // 8

    def lines_of(row):
        lines = []
        for block in range(blocks):
            at = pl.ds(block * 8, 8)
            classes = {}
            for shift_x in range(RADIUS + 1):
                for shift_y in range(RADIUS + 1):
                    square = shift_x * shift_x + shift_y * shift_y
                    if square not in CLASSES:
                        continue
                    value = near[shift_y, row + (RADIUS + shift_x), at, :]
                    if shift_x:
                        value = value + near[shift_y, row + (RADIUS - shift_x), at, :]
                    classes[square] = value if square not in classes else classes[square] + value
            for shift_z in range(RADIUS + 1):
                line = None
                for square, value in classes.items():
                    weight = weight_of(square + shift_z * shift_z)
                    if weight > 0.0:
                        line = weight * value if line is None else line + weight * value
                lines.append(line)
        return tuple(lines)

    def write(row, lines):
        for block in range(blocks):
            result, *rest = lines[(RADIUS + 1) * block : (RADIUS + 1) * (block + 1)]
            for shift_z, line in enumerate(rest, 1):
                up = jnp.where(lane < shift_z, 0.0, pltpu.roll(line, shift_z, 1))
                down = jnp.where(lane >= depth - shift_z, 0.0, pltpu.roll(line, depth - shift_z, 1))
                result = result + (up + down)
            result_v[row, 8 * block : 8 * block + 8, :] = result * scale

    def out_row(row, nothing):
        write(row, lines_of(row))
        return nothing

    pieces = 4
    size = rows // pieces
    for piece in range(pieces):
        lax.fori_loop(piece * size, (piece + 1) * size, out_row, 0, unroll=size)
        at = pl.ds(piece * size, size)
        copies.append(pltpu.make_async_copy(result_v.at[at], sens.at[at], sems.at[3 + piece]))
        copies[-1].start()
    for copy in copies:
        copy.wait()


def call(body, shapes, inputs, scratch=(), places=None, out_places=None, flops=0, limit=24, aliases=None):
    places, out_places = places or {}, out_places or {}
    in_specs = [pl.BlockSpec(memory_space=places.get(rank, pltpu.VMEM)) for rank in range(len(inputs))]
    out_specs = [pl.BlockSpec(memory_space=out_places.get(rank, pltpu.VMEM)) for rank in range(len(shapes))]
    moved = sum(int(np.prod(v.shape)) * 4 for v in list(inputs) + list(shapes))
    return pl.pallas_call(
        body,
        out_shape=[FULL(v.shape, v.dtype) for v in shapes],
        in_specs=in_specs,
        out_specs=out_specs,
        scratch_shapes=list(scratch),
        input_output_aliases=aliases or {},
        cost_estimate=pl.CostEstimate(flops=flops, bytes_accessed=moved, transcendentals=0),
        compiler_params=pltpu.CompilerParams(vmem_limit_bytes=int(limit * 1024 * 1024)),
    )(*inputs)


def f32(*shape):
    return FULL(shape, jnp.float32)


def vmem(*shape, dtype=jnp.float32):
    return pltpu.VMEM(shape, dtype)


def on_device(count_x, count_y, displacement, density, element_kind, load_x, load_y, load_z, load_force):
    rows, cols, depth = density.shape
    wide = cols + HALO
    devices = count_x * count_y
    cells = float(rows * cols * depth * devices)

    pairs_ya = [(k, k ^ 1) for k in range(count_y)]
    pairs_xa = [(k, k ^ 1) for k in range(count_x)]
    pairs_yb, pairs_xb = [], []
    for i in range(count_x):
        for j in range(count_y):
            here = i * count_y + j
            inside_y, inside_x = 0 < j < count_y - 1, 0 < i < count_x - 1
            pairs_yb.append((here, i * count_y + ((j + 1) ^ 1) - 1 if inside_y else (i ^ 1) * count_y + j))
            pairs_xb.append((here, (((i + 1) ^ 1) - 1) * count_y + j if inside_x else i * count_y + (j ^ 1)))

    disp = displacement.reshape(3 * rows * cols, depth)
    dens = density.reshape(rows * cols, depth)
    kind = element_kind.reshape(rows * cols, depth)

    slots = 4 * RADIUS + RADIUS
    send_a, send_b, mark = call(
        functools.partial(pack_y, rows, cols),
        [f32(slots * rows, depth)] * 2 + [f32(8, depth)],
        [displacement, density, element_kind],
        scratch=[
            vmem(3, rows, HALO, depth),
            vmem(rows, HALO, depth),
            vmem(rows, HALO, depth, dtype=jnp.int32),
            pltpu.SemaphoreType.DMA((6,)),
        ],
        places={0: pltpu.HBM, 1: pltpu.HBM, 2: pltpu.HBM},
        limit=53.25,
    )
    got_a = lax.ppermute(send_a, "gy", pairs_ya)
    got_b = lax.ppermute(send_b, BOTH, pairs_yb)

    sums = np.zeros((8, depth), np.float32)
    for rank, square in enumerate(CLASSES):
        for z in range(depth):
            sums[rank, z] = sum(
                weight_of(square + s * s) for s in range(-RADIUS, RADIUS + 1) if 0 <= z + s < depth
            )
    count = load_x.shape[0]
    applied, inverse = call(
        functools.partial(loads_and_weights, rows, cols, count_x, count_y),
        [f32(3, rows * cols, depth), f32(2 * RADIUS + 1, wide, depth)],
        [mark, load_x.reshape(1, count), load_y.reshape(1, count), load_z.reshape(1, count), load_force, jnp.asarray(sums)],
        places={0: pl.ANY},
        flops=2 * rows * cols * count * 6 * depth,
    )

    early = cols - HALO
    waves, far, inner, scaled, sums = call(
        functools.partial(early_elements, rows, cols),
        [
            f32(6, rows, wide + HALO, depth),
            f32(6, rows, wide, depth),
            f32(3, rows * cols, depth),
            f32(rows, wide + HALO, depth),
            f32(2, 8, depth),
        ],
        [disp, dens, kind, inverse, applied],
        scratch=[vmem(6, rows, HALO, depth)],
        flops=250 * rows * early * depth,
    )

    edge_u, edge_f, edge_s, send_a, send_b = call(
        functools.partial(unpack_y, rows, cols, count_y),
        [f32(3 * rows * HALO, depth), f32(rows * HALO, depth), f32(rows * HALO, depth)] + [f32(4, wide, depth)] * 2,
        [sums, disp, dens, kind, got_a, got_b],
        places={0: pl.ANY},
    )
    got_a = lax.ppermute(send_a, "gx", pairs_xa)
    got_b = lax.ppermute(send_b, BOTH, pairs_xb)

    waves, far, inner, scaled, sums = call(
        functools.partial(late_elements, rows, cols),
        [f32(*v.shape) for v in (waves, far, inner, scaled, sums)],
        [waves, far, inner, scaled, dens, kind, edge_u, edge_f, edge_s, applied, inverse, sums],
        scratch=[vmem(6, rows, HALO, depth), vmem(6 * rows * HALO, depth)],
        flops=250 * rows * 2 * HALO * depth,
        aliases={0: 0, 1: 1, 2: 2, 3: 3},
    )
    outer, final, send_a, send_b, parts = call(
        functools.partial(outer_elements, rows, cols, count_x, devices),
        [f32(2, 3, cols, depth), f32(wide + HALO, depth)] + [f32(RADIUS, wide, depth)] * 2 + [f32(devices, depth)],
        [waves, dens, kind, edge_f, edge_s, got_a, got_b, inner, scaled, sums, inverse],
        scratch=[vmem(2, 6, wide + HALO, depth), vmem(wide, depth), vmem(2, 6, wide + 2 * HALO, depth)],
        flops=500 * wide * depth,
    )
    got_a = lax.ppermute(send_a, "gx", pairs_xa)
    got_b = lax.ppermute(send_b, BOTH, pairs_xb)
    parts = lax.all_to_all(parts, BOTH, 0, 0, tiled=True)

    sens, resid, comp, volume = call(
        functools.partial(filter_rows, rows, cols, count_x, cells),
        [f32(rows, cols, depth), f32(3, rows * cols, depth), f32(1, 1), f32(1, 1)],
        [scaled, final, got_a, got_b, parts, inner, outer],
        scratch=[
            vmem(RADIUS + 1, rows + 2 * RADIUS, cols, depth),
            vmem(2 * RADIUS, wide + HALO, depth),
            vmem(rows, cols, depth),
            pltpu.SemaphoreType.DMA((7,)),
        ],
        out_places={0: pltpu.HBM, 1: pltpu.HBM, 2: pltpu.SMEM, 3: pltpu.SMEM},
        flops=60 * rows * cols * depth,
    )
    return (
        sens,
        resid.reshape(3, rows, cols, depth),
        comp.reshape(()),
        volume.reshape(()),
    )


def solution(mesh):
    placed = (
        P(None, "gx", "gy", None),
        P("gx", "gy", None),
        P("gx", "gy", None),
        P(),
        P(),
        P(),
        P(),
    )
    return jax.shard_map(
        functools.partial(on_device, mesh.shape["gx"], mesh.shape["gy"]),
        mesh=mesh,
        in_specs=placed,
        out_specs=(P("gx", "gy", None), P(None, "gx", "gy", None), P(), P()),
        check_vma=False,
    )
```

```python
import functools

import jax
import jax.numpy as jnp
import numpy as np
from jax import lax
from jax.experimental import pallas as pl
from jax.experimental.pallas import tpu as pltpu
from jax.sharding import PartitionSpec as P

RADIUS = 3
PENALTY = 3.0
STIFF_FLOOR = 0.001
POISSON = 0.3
HALO = 8
BOTH = ("gx", "gy")
FULL = jax.ShapeDtypeStruct


def element_matrix():
    lame_first = POISSON / ((1.0 + POISSON) * (1.0 - 2.0 * POISSON))
    shear_modulus = 0.5 / (1.0 + POISSON)
    material = np.zeros((6, 6))
    material[:3, :3] = lame_first
    for diagonal in range(3):
        material[diagonal, diagonal] += 2.0 * shear_modulus
        material[diagonal + 3, diagonal + 3] = shear_modulus
    points = [0.5 - 0.5 / np.sqrt(3.0), 0.5 + 0.5 / np.sqrt(3.0)]
    corners = [(a, b, e) for a in (0, 1) for b in (0, 1) for e in (0, 1)]
    result = np.zeros((24, 24))
    for point_x in points:
        for point_y in points:
            for point_z in points:
                strain = np.zeros((6, 24))
                for corner, (side_x, side_y, side_z) in enumerate(corners):
                    value_x = point_x if side_x else 1.0 - point_x
                    value_y = point_y if side_y else 1.0 - point_y
                    value_z = point_z if side_z else 1.0 - point_z
                    slope_x = (1.0 if side_x else -1.0) * value_y * value_z
                    slope_y = value_x * (1.0 if side_y else -1.0) * value_z
                    slope_z = value_x * value_y * (1.0 if side_z else -1.0)
                    column = 3 * corner
                    strain[0, column] = slope_x
                    strain[1, column + 1] = slope_y
                    strain[2, column + 2] = slope_z
                    strain[3, column] = slope_y
                    strain[3, column + 1] = slope_x
                    strain[4, column + 1] = slope_z
                    strain[4, column + 2] = slope_y
                    strain[5, column + 2] = slope_x
                    strain[5, column] = slope_z
                result += strain.T @ material @ strain / 8.0
    return result


def modal_matrix():
    pair = np.array([[1.0, 1.0], [-1.0, 1.0]])
    turn = np.kron(np.kron(np.kron(pair, pair), pair), np.eye(3))
    return turn @ element_matrix() @ turn.T / 64.0


SHEARS = ((3, 14), (4, 8), (6, 13))
NORMALS = (5, 7, 12)
PAIRS = ((10, 15), (11, 18), (17, 19))
TRIO = (9, 16, 20)
LASTS = (21, 22, 23)


def modal_constants():
    modal = modal_matrix()
    known = np.zeros((24, 24))
    shear = modal[3, 3]
    for first, second in SHEARS:
        known[np.ix_((first, second), (first, second))] = shear
    normal_off = modal[5, 7]
    normal_own = modal[5, 5] - normal_off
    known[np.ix_(NORMALS, NORMALS)] = normal_off
    pair_off = modal[10, 15]
    pair_own = modal[10, 10] - pair_off
    for both in PAIRS:
        known[np.ix_(both, both)] = pair_off
    trio = modal[9, 16]
    known[np.ix_(TRIO, TRIO)] = trio
    last = modal[21, 21]
    for group, own in ((NORMALS, normal_own), (sum(PAIRS, ()), pair_own), (TRIO, trio), (LASTS, last)):
        for degree in group:
            known[degree, degree] += own
    assert np.abs(known - modal).max() < 1e-12
    return tuple(float(v) for v in (shear, normal_off, normal_own, pair_off, pair_own, trio, last))


def weight_of(square):
    return max(0.0, RADIUS + 0.5 - float(np.sqrt(square)))


CLASSES = (0, 1, 2, 4, 5, 8, 9, 10)


def stiffness_of(physical):
    return STIFF_FLOOR + (1.0 - STIFF_FLOOR) * (physical * physical * physical)


def physical_of(density, kind):
    return jnp.where(kind == 1, 0.0, jnp.where(kind == 2, 1.0, density))


def factor_of(physical, kind):
    design = (kind != 1) & (kind != 2)
    return jnp.where(design, (-PENALTY * (1.0 - STIFF_FLOOR)) * (physical * physical), 0.0)


def pack_y(rows, cols, disp, dens, kind, out_a, out_b, mark, edge_d, edge_p, edge_k, sems):
    half = HALO // 2
    copies = []
    for side, start in ((0, 0), (half, cols - half)):
        for source, target in ((disp, edge_d), (dens, edge_p), (kind, edge_k)):
            lead = (slice(None),) * (len(source.shape) - 2)
            copies.append(
                pltpu.make_async_copy(
                    source.at[(*lead, pl.ds(start, half), slice(None))],
                    target.at[(*lead, pl.ds(side, half), slice(None))],
                    sems.at[len(copies)],
                )
            )
    for copy in copies:
        copy.start()
    for copy in copies:
        copy.wait()
    depth = disp.shape[-1]
    flat_d = edge_d.reshape(3 * rows * HALO, depth)
    flat_p = edge_p.reshape(rows * HALO, depth)
    flat_k = edge_k.reshape(rows * HALO, depth)

    def state(index):
        code = flat_k[pl.ds(index, rows, stride=HALO), :]
        return physical_of(flat_p[pl.ds(index, rows, stride=HALO), :], code), code

    def fill(low, high):
        slot = 0
        for c in range(3):
            for index in range(RADIUS + 1):
                low[pl.ds(slot * rows, rows), :] = flat_d[pl.ds(c * rows * HALO + index, rows, stride=HALO), :]
                slot += 1
        for index in range(RADIUS):
            low[pl.ds(slot * rows, rows), :] = factor_of(*state(index))
            slot += 1
        slot = 0
        for c in range(3):
            for index in range(HALO - RADIUS, HALO):
                high[pl.ds(slot * rows, rows), :] = flat_d[pl.ds(c * rows * HALO + index, rows, stride=HALO), :]
                slot += 1
        for index in range(HALO - RADIUS, HALO):
            physical, code = state(index)
            high[pl.ds(slot * rows, rows), :] = factor_of(physical, code)
            slot += 1
        high[pl.ds(slot * rows, rows), :] = stiffness_of(physical)

    mark[...] = jnp.zeros_like(mark)
    odd = lax.axis_index("gy") % 2

    @pl.when(odd == 0)
    def _():
        fill(out_b, out_a)

    @pl.when(odd == 1)
    def _():
        fill(out_a, out_b)


def unpack_y(rows, cols, count_y, after, disp, dens, kind, got_a, got_b, edge_u, edge_f, edge_s, out_a, out_b):
    del after
    here = lax.axis_index("gy")
    depth = disp.shape[-1]
    has_low = here > 0
    has_high = here < count_y - 1

    def fill(low, high):
        def put(ref, start, sublane, value):
            ref[pl.ds(start + sublane, rows, stride=HALO), :] = value

        zero = jnp.zeros((rows, depth), jnp.float32)
        slot = 0
        for c in range(3):
            for index in range(RADIUS + 1):
                put(edge_u, c * rows * HALO, index, jnp.where(has_high, high[pl.ds(slot * rows, rows), :], 0.0))
                slot += 1
        for index in range(RADIUS):
            put(edge_f, 0, index, jnp.where(has_high, high[pl.ds(slot * rows, rows), :], 0.0))
            slot += 1
        slot = 0
        for c in range(3):
            put(edge_u, c * rows * HALO, RADIUS + 1, zero)
            for index in range(HALO - RADIUS, HALO):
                put(edge_u, c * rows * HALO, index, low[pl.ds(slot * rows, rows), :])
                slot += 1
        for index in range(RADIUS, HALO - RADIUS):
            put(edge_f, 0, index, zero)
        for index in range(HALO - RADIUS, HALO):
            put(edge_f, 0, index, jnp.where(has_low, low[pl.ds(slot * rows, rows), :], 0.0))
            slot += 1
        edge_s[...] = jnp.zeros_like(edge_s)
        put(edge_s, 0, HALO - 1, jnp.where(has_low, low[pl.ds(slot * rows, rows), :], 0.0))

    odd = here % 2

    @pl.when(odd == 0)
    def _():
        fill(got_b, got_a)

    @pl.when(odd == 1)
    def _():
        fill(got_a, got_b)

    def send(out, row, with_stiff):
        for c in range(3):
            out[c, :cols, :] = disp[pl.ds((c * rows + row) * cols, cols), :]
            out[c, cols:, :] = edge_u[pl.ds((c * rows + row) * HALO, HALO), :]
        if with_stiff:
            at = pl.ds(row * cols, cols)
            out[3, :cols, :] = stiffness_of(physical_of(dens[at, :], kind[at, :]))
            out[3, cols:, :] = edge_s[pl.ds(row * HALO, HALO), :]
        else:
            out[3] = jnp.zeros_like(out[3])

    odd_x = lax.axis_index("gx") % 2

    @pl.when(odd_x == 0)
    def _():
        send(out_a, rows - 1, True)
        send(out_b, 0, False)

    @pl.when(odd_x == 1)
    def _():
        send(out_a, 0, False)
        send(out_b, rows - 1, True)


def loads_and_weights(rows, cols, count_x, count_y, after, load_x, load_y, load_z, force, sums, applied, inverse):
    del after
    depth = applied.shape[-1]
    place_x = lax.axis_index("gx") * rows
    place_y = lax.axis_index("gy") * cols
    local_x = load_x[...] - place_x
    local_y = load_y[...] - place_y
    owned = (local_x >= 0) & (local_x < rows) & (local_y >= 0) & (local_y < cols)
    target = jnp.where(owned, local_x * cols + local_y, -1)
    loads = target.shape[1]
    lanes = lax.broadcasted_iota(jnp.int32, (depth, loads), 0)
    hit_z = lanes == load_z[...]
    right = [[], []]
    for c in range(3):
        value = force[c : c + 1, :]
        coarse = value.astype(jnp.bfloat16).astype(jnp.float32)
        for part, piece in zip(right, (coarse, value - coarse)):
            part.append(jnp.where(hit_z, piece, 0.0).astype(jnp.bfloat16))
    place = lax.broadcasted_iota(jnp.int32, (rows * cols, loads), 0)
    left = jnp.where(place == target, 1.0, 0.0).astype(jnp.bfloat16)
    product = None
    for part in right:
        piece = lax.dot_general(
            left, jnp.concatenate(part, axis=0), (((1,), (1,)), ((), ())), preferred_element_type=jnp.float32
        )
        product = piece if product is None else product + piece
    for c in range(3):
        applied[c] = product[:, c * depth : (c + 1) * depth]

    wide = cols + HALO
    total_x, total_y = rows * count_x, cols * count_y
    sublane = lax.broadcasted_iota(jnp.int32, (wide, depth), 0)
    node_y = jnp.where(sublane >= wide - RADIUS, sublane - wide, sublane) + place_y
    inside_y = {
        shift: ((node_y + shift >= 0) & (node_y + shift < total_y)).astype(jnp.float32)
        for shift in range(-RADIUS, RADIUS + 1)
    }
    for kind in range(2 * RADIUS + 1):
        row = kind if kind <= RADIUS else rows - 2 * RADIUS - 1 + kind
        result = jnp.zeros((wide, depth), jnp.float32)
        for shift_y in range(-RADIUS, RADIUS + 1):
            line = jnp.zeros((1, depth), jnp.float32)
            for shift_x in range(-RADIUS, RADIUS + 1):
                square = shift_x * shift_x + shift_y * shift_y
                if square in CLASSES:
                    at = place_x + (row + shift_x)
                    inside = ((at >= 0) & (at < total_x)).astype(jnp.float32)
                    rank = CLASSES.index(square)
                    line = line + inside * sums[rank : rank + 1, :]
            result = result + inside_y[shift_y] * line
        inverse[kind] = 1.0 / jnp.where(result > 0.0, result, 1.0)


def shifted_z(value, lane, depth):
    beyond = jnp.where(lane == depth - 1, 0.0, pltpu.roll(value, depth - 1, 1))
    return value + beyond, beyond - value


def waves_of(here, there):
    return tuple(a + b for a, b in zip(here, there)) + tuple(b - a for a, b in zip(here, there))


def modal(before, after, stiff, constants):
    shear, normal_off, normal_own, pair_off, pair_own, trio, last = constants
    u = [None] * 24
    for low in range(12):
        if low >= 3:
            u[low] = before[low] + after[low]
        u[12 + low] = after[low] - before[low]
    f = [None] * 24
    terms = []

    def take(degree, pull):
        terms.append(pull * u[degree])
        f[degree] = pull * stiff

    for first, second in SHEARS:
        both = u[first] + u[second]
        pull = shear * both
        terms.append(pull * both)
        f[first] = f[second] = pull * stiff
    common = normal_off * (u[5] + u[7] + u[12])
    for degree in NORMALS:
        take(degree, common + normal_own * u[degree])
    for first, second in PAIRS:
        common = pair_off * (u[first] + u[second])
        take(first, common + pair_own * u[first])
        take(second, common + pair_own * u[second])
    common = u[9] + u[16] + u[20]
    for degree in TRIO:
        take(degree, trio * (common + u[degree]))
    for degree in LASTS:
        take(degree, last * u[degree])
    while len(terms) > 1:
        terms = [sum(terms[k : k + 2][1:], terms[k]) for k in range(0, len(terms), 2)]
    return terms[0], f


def lower_of(f):
    return tuple(f[12 + k] * -1.0 if f[k] is None else f[k] - f[12 + k] for k in range(12))


def upper_of(f):
    return tuple(f[12 + k] if f[k] is None else f[k] + f[12 + k] for k in range(12))


def along_y(g):
    return tuple(g[k] - g[6 + k] for k in range(6)), tuple(g[k] + g[6 + k] for k in range(6))


def along_z(g, lane):
    return [
        (g[c] - g[3 + c]) + jnp.where(lane == 0, 0.0, pltpu.roll(g[c] + g[3 + c], 1, 1)) for c in range(3)
    ]


def class_of(row, rows):
    return jnp.where(row < RADIUS, row, jnp.where(row >= rows - RADIUS, row - (rows - 2 * RADIUS - 1), RADIUS))


def march(rows, block, waves, state, inverse, emit, put, own):
    constants = modal_constants()
    depth = waves.shape[-1]
    first = 8 * block
    zero = jnp.zeros((HALO, depth), jnp.float32)

    def nodes(row):
        return waves_of(
            [waves[k, row, first : first + 8, :] for k in range(6)],
            [waves[k, row, first + 1 : first + 9, :] for k in range(6)],
        )

    def step(row, carry):
        before, held, total, filled = carry
        after = nodes(row + 1)
        physical, stiff, factor = state(row)
        energy, f = modal(before, after, stiff, constants)
        put(row, factor * energy * inverse[class_of(row, rows), first : first + 8, :])
        if own:
            total = total + stiff * energy
            filled = filled + physical
        emit(row, *along_y(tuple(a + b for a, b in zip(held, lower_of(f)))))
        return after, upper_of(f), total, filled

    carry = (nodes(0), (zero,) * 12, zero, zero)
    carry = lax.fori_loop(0, rows - 2, step, carry, unroll=True)
    _, held, total, filled = step(rows - 2, carry)
    emit(rows - 1, *along_y(held))
    if own:
        filled = filled + state(rows - 1)[0]
    return total, filled


def own_state(dens, kind, cols, first):
    def state(row):
        at = pl.ds(pl.multiple_of(row * cols + first, 8), HALO)
        code = kind[at, :]
        physical = physical_of(dens[at, :], code)
        return physical, stiffness_of(physical), factor_of(physical, code)

    return state


def joiner(cols, block, tail_in, tail_out, applied, resid):
    first = 8 * block
    depth = resid.shape[-1]
    lane = lax.broadcasted_iota(jnp.int32, (HALO, depth), 1)
    sublane = lax.broadcasted_iota(jnp.int32, (HALO, depth), 0)

    def emit(row, low, high):
        parts = []
        for k in range(6):
            turned = pltpu.roll(high[k], 1, 0)
            if tail_out is not None:
                tail_out[k, row] = turned
            before = 0.0 if tail_in is None else tail_in[k, row]
            parts.append(low[k] + jnp.where(sublane == 0, before, turned))
        at = pl.ds(pl.multiple_of(row * cols + first, 8), HALO)
        for c, value in enumerate(along_z(parts, lane)):
            resid[c, at, :] = applied[c, at, :] - value

    return emit


def early_elements(
    rows, cols, disp, dens, kind, inverse, applied, waves, tail, resid, scaled, sums, *tails
):
    depth = disp.shape[-1]
    lane = lax.broadcasted_iota(jnp.int32, (HALO, depth), 1)

    def turn(row, nothing):
        for c in range(3):
            for block in range(cols // 8):
                at = pl.ds(pl.multiple_of((c * rows + row) * cols + 8 * block, 8), HALO)
                for r, value in enumerate(shifted_z(disp[at, :], lane, depth)):
                    waves[3 * r + c, row, 8 * block : 8 * block + 8, :] = value
                    if block == 0:
                        waves[3 * r + c, row, cols + HALO :, :] = value
        return nothing

    lax.fori_loop(0, rows, turn, 0, unroll=8)
    total = filled = jnp.zeros((HALO, depth), jnp.float32)
    chain = (None, *tails, tail)
    for block in range(cols // 8 - 1):
        first = 8 * block

        def put(row, value, first=first):
            scaled[row, first + 8 : first + 16, :] = value

        emit = joiner(cols, block, chain[block], chain[block + 1], applied, resid)
        state = own_state(dens, kind, cols, first)
        more = march(rows, block, waves, state, inverse, emit, put, True)
        total, filled = total + more[0], filled + more[1]
    sums[0] = total
    sums[1] = filled


def late_elements(
    rows, cols,
    waves_in, resid_in, scaled_in, tail, dens, kind, edge_u, edge_f, edge_s, applied, inverse, sums_a,
    waves, resid, scaled, sums, resid_out, near, filtered, far_h, sem,
):
    depth = dens.shape[-1]
    del waves_in, resid_in, scaled_in
    wide = cols + HALO
    lane = lax.broadcasted_iota(jnp.int32, (HALO, depth), 1)

    def turn(row, nothing):
        for c in range(3):
            at = pl.ds(pl.multiple_of((c * rows + row) * HALO, 8), HALO)
            for r, value in enumerate(shifted_z(edge_u[at, :], lane, depth)):
                waves[3 * r + c, row, cols:wide, :] = value
        return nothing

    lax.fori_loop(0, rows, turn, 0, unroll=16)

    def edge_state(row):
        at = pl.ds(pl.multiple_of(row * HALO, 8), HALO)
        return None, edge_s[at, :], edge_f[at, :]

    def put_edge(row, value):
        scaled[row, :HALO, :] = value
        scaled[row, wide:, :] = value

    def emit_edge(row, low, high):
        for k in range(6):
            far_h[pl.ds(pl.multiple_of((k * rows + row) * HALO, 8), HALO), :] = high[k]

    march(rows, cols // 8, waves, edge_state, inverse, emit_edge, put_edge, False)
    last = cols // 8 - 1

    def put(row, value):
        scaled[row, cols:wide, :] = value

    emit = joiner(cols, last, tail, None, applied, resid)
    state = own_state(dens, kind, cols, 8 * last)
    total, filled = march(rows, last, waves, state, inverse, emit, put, True)
    sums[0] = sums_a[0] + total
    sums[1] = sums_a[1] + filled

    parts = [far_h[pl.ds(k * rows * HALO + HALO - 1, rows, stride=HALO), :] for k in range(6)]
    at = pl.ds(0, rows, stride=cols)
    for c, value in enumerate(along_z(parts, lax.broadcasted_iota(jnp.int32, (rows, depth), 1))):
        resid[c, at, :] = resid[c, at, :] - value
    middle = pl.ds(cols, (rows - 2) * cols)
    copy = pltpu.make_async_copy(resid.at[:, middle, :], resid_out.at[:, middle, :], sem)
    copy.start()

    def own(row, nothing):
        lines_y(near, row + RADIUS, cols, lambda start: scaled[row, start : start + 8, :])
        return nothing

    lax.fori_loop(0, rows - 1, own, 0, unroll=True)
    for row in range(RADIUS, rows - RADIUS - 1):
        for block in range(last + 1):
            filtered[row, 8 * block : 8 * block + 8, :] = filter_row(near, row, block, lane)
    copy.wait()


def outer_elements(
    rows, cols, count_x, devices,
    waves, dens, kind, edge_f, edge_s, got_a, got_b, inner, scaled, sums, inverse,
    resid, final, out_a, out_b, parts, ring, stiff_low, carry_y,
):
    depth = dens.shape[-1]
    constants = modal_constants()
    wide = cols + HALO
    blocks = wide // HALO
    lane = lax.broadcasted_iota(jnp.int32, (HALO, depth), 1)
    here = lax.axis_index("gx")
    has_low = here > 0
    has_high = here < count_x - 1
    odd = here % 2

    def take(low, high):
        for block in range(blocks):
            first = 8 * block
            for c in range(3):
                for side, value in enumerate((low[c, first : first + 8, :], high[c, first : first + 8, :])):
                    if side:
                        value = jnp.where(has_high, value, 0.0)
                    for r, wave in enumerate(shifted_z(value, lane, depth)):
                        ring[side, 3 * r + c, first : first + 8, :] = wave
                        if block == 0:
                            ring[side, 3 * r + c, wide:, :] = wave
        stiff_low[...] = jnp.where(has_low, low[3], 0.0)

    @pl.when(odd == 0)
    def _():
        take(got_b, got_a)

    @pl.when(odd == 1)
    def _():
        take(got_a, got_b)

    total = sums[0]
    for block in (blocks - 1, *range(blocks - 1)):
        own = block < blocks - 1
        first = 8 * block

        def nodes(load):
            return waves_of(
                [load(k)[first : first + 8, :] for k in range(6)], [load(k)[first + 1 : first + 9, :] for k in range(6)]
            )

        line = [
            nodes(lambda k: ring.at[0, k]),
            nodes(lambda k: waves.at[k, 0]),
            nodes(lambda k: waves.at[k, rows - 1]),
            nodes(lambda k: ring.at[1, k]),
        ]
        _, f_low = modal(line[0], line[1], stiff_low[first : first + 8, :], constants)
        if own:
            _, stiff, factor = own_state(dens, kind, cols, first)(rows - 1)
        else:
            at = pl.ds((rows - 1) * HALO, HALO)
            stiff, factor = edge_s[at, :], edge_f[at, :]
        energy, f_high = modal(line[2], line[3], stiff, constants)
        value = factor * energy * inverse[2 * RADIUS, first : first + 8, :]
        if own:
            total = total + stiff * energy
            final[first + 8 : first + 16, :] = value
        else:
            final[:HALO, :] = value
            final[wide:, :] = value
        for index, (row, g) in enumerate(((0, upper_of(f_low)), (rows - 1, lower_of(f_high)))):
            low, high = along_y(g)
            if own:
                joined = []
                for k in range(6):
                    carry_y[index, k, first + 9 : first + 17, :] = high[k]
                    joined.append(low[k] + carry_y[index, k, first + 8 : first + 16, :])
                for c, value in enumerate(along_z(joined, lane)):
                    resid[index, c, first : first + 8, :] = inner[c, pl.ds(row * cols + first, HALO), :] - value
            else:
                for k in range(6):
                    carry_y[index, k, 1:9, :] = high[k]

    half = depth // 2
    pieces = []
    for value in (total, sums[1]):
        line = jnp.sum(value, axis=0, keepdims=True)
        pieces.append(line + pltpu.roll(line, half, 1))
    line = jnp.where(lax.broadcasted_iota(jnp.int32, (1, depth), 1) < half, pieces[0], pieces[1])
    parts[...] = jnp.broadcast_to(line, (devices, depth))

    def send(up, down):
        for index in range(RADIUS - 1):
            up[index] = scaled[rows - RADIUS + index, :wide, :]
        up[RADIUS - 1] = final[:wide, :]
        for index in range(RADIUS):
            down[index] = scaled[index, :wide, :]

    @pl.when(odd == 0)
    def _():
        send(out_a, out_b)

    @pl.when(odd == 1)
    def _():
        send(out_b, out_a)


def lines_y(near, row, cols, load):
    for block in range(cols // 8):
        start = HALO + 8 * block
        near[0, row, 8 * block : 8 * block + 8, :] = load(start)
        for shift in range(1, RADIUS + 1):
            near[shift, row, 8 * block : 8 * block + 8, :] = load(start + shift) + load(start - shift)


def filter_row(near, row, block, lane):
    depth = near.shape[-1]
    at = pl.ds(block * 8, 8)
    classes = {}
    for shift_x in range(RADIUS + 1):
        for shift_y in range(RADIUS + 1):
            square = shift_x * shift_x + shift_y * shift_y
            if square not in CLASSES:
                continue
            value = near[shift_y, row + (RADIUS + shift_x), at, :]
            if shift_x:
                value = value + near[shift_y, row + (RADIUS - shift_x), at, :]
            classes[square] = value if square not in classes else classes[square] + value
    result = None
    for shift_z in range(RADIUS + 1):
        line = None
        for square, value in classes.items():
            weight = weight_of(square + shift_z * shift_z)
            if weight > 0.0:
                line = weight * value if line is None else line + weight * value
        if shift_z:
            up = jnp.where(lane < shift_z, 0.0, pltpu.roll(line, shift_z, 1))
            down = jnp.where(lane >= depth - shift_z, 0.0, pltpu.roll(line, depth - shift_z, 1))
            line = up + down
        result = line if result is None else result + line
    return result


def filter_rest(
    rows, cols, count_x, cells,
    near_in, inner, final, got_a, got_b, parts, outer, resid_in,
    sens, resid, comp, vol, near, ends, result_v, sems,
):
    depth = sens.shape[-1]
    del near_in, resid_in
    wide = cols + HALO
    copies = [
        pltpu.make_async_copy(outer.at[index], resid.at[:, pl.ds(row * cols, cols), :], sems.at[index])
        for index, row in enumerate((0, rows - 1))
    ]
    for copy in copies:
        copy.start()
    here = lax.axis_index("gx")
    has_low = here > 0
    has_high = here < count_x - 1
    odd = here % 2
    half = depth // 2
    line = jnp.sum(parts[...], axis=0, keepdims=True)
    first = lax.broadcasted_iota(jnp.int32, (1, depth), 1) < half
    compliance = jnp.sum(jnp.where(first, line, 0.0))
    volume = jnp.sum(jnp.where(first, 0.0, line))
    comp[0, 0] = compliance
    vol[0, 0] = volume / cells
    scale = cells / jnp.broadcast_to(compliance, (8, depth))

    def send(start, size):
        at = pl.ds(start, size)
        copies.append(pltpu.make_async_copy(result_v.at[at], sens.at[at], sems.at[len(copies)]))
        copies[-1].start()

    low_end, high_start = RADIUS, rows - RADIUS - 1
    for row in range(low_end, high_start):
        for block in range(cols // 8):
            at = pl.ds(block * 8, 8)
            result_v[row, at, :] = inner[row, at, :] * scale
    send(low_end, high_start - low_end)

    def take(low, high):
        for index in range(RADIUS):
            for source, has, at in ((low, has_low, index), (high, has_high, RADIUS + index)):
                value = jnp.where(has, source[index], 0.0)
                ends[at, :wide, :] = value
                ends[at, wide:, :] = value[:HALO]

    @pl.when(odd == 0)
    def _():
        take(got_b, got_a)

    @pl.when(odd == 1)
    def _():
        take(got_a, got_b)

    for index in range(RADIUS):
        lines_y(near, index, cols, lambda start, at=index: ends[at, start : start + 8, :])
        lines_y(near, rows + RADIUS + index, cols, lambda start, at=RADIUS + index: ends[at, start : start + 8, :])
    lines_y(near, rows + RADIUS - 1, cols, lambda start: final[start : start + 8, :])
    lane = lax.broadcasted_iota(jnp.int32, (8, depth), 1)
    for start, stop in ((0, low_end), (high_start, rows)):
        for row in range(start, stop):
            for block in range(cols // 8):
                result_v[row, 8 * block : 8 * block + 8, :] = filter_row(near, row, block, lane) * scale
        send(start, stop - start)
    for copy in copies:
        copy.wait()


def call(body, shapes, inputs, scratch=(), places=None, out_places=None, flops=0, limit=24, aliases=None):
    places, out_places = places or {}, out_places or {}
    in_specs = [pl.BlockSpec(memory_space=places.get(rank, pltpu.VMEM)) for rank in range(len(inputs))]
    out_specs = [pl.BlockSpec(memory_space=out_places.get(rank, pltpu.VMEM)) for rank in range(len(shapes))]
    moved = sum(int(np.prod(v.shape)) * 4 for v in list(inputs) + list(shapes))
    return pl.pallas_call(
        body,
        out_shape=[FULL(v.shape, v.dtype) for v in shapes],
        in_specs=in_specs,
        out_specs=out_specs,
        scratch_shapes=list(scratch),
        input_output_aliases=aliases or {},
        cost_estimate=pl.CostEstimate(flops=flops, bytes_accessed=moved, transcendentals=0),
        compiler_params=pltpu.CompilerParams(vmem_limit_bytes=int(limit * 1024 * 1024)),
    )(*inputs)


def f32(*shape):
    return FULL(shape, jnp.float32)


def vmem(*shape, dtype=jnp.float32):
    return pltpu.VMEM(shape, dtype)


def on_device(count_x, count_y, displacement, density, element_kind, load_x, load_y, load_z, load_force):
    rows, cols, depth = density.shape
    wide = cols + HALO
    devices = count_x * count_y
    cells = float(rows * cols * depth * devices)

    pairs_ya = [(k, k ^ 1) for k in range(count_y)]
    pairs_xa = [(k, k ^ 1) for k in range(count_x)]
    pairs_yb, pairs_xb = [], []
    for i in range(count_x):
        for j in range(count_y):
            here = i * count_y + j
            inside_y, inside_x = 0 < j < count_y - 1, 0 < i < count_x - 1
            pairs_yb.append((here, i * count_y + ((j + 1) ^ 1) - 1 if inside_y else (i ^ 1) * count_y + j))
            pairs_xb.append((here, (((i + 1) ^ 1) - 1) * count_y + j if inside_x else i * count_y + (j ^ 1)))

    disp = displacement.reshape(3 * rows * cols, depth)
    dens = density.reshape(rows * cols, depth)
    kind = element_kind.reshape(rows * cols, depth)

    slots = 4 * RADIUS + RADIUS
    send_a, send_b, mark = call(
        functools.partial(pack_y, rows, cols),
        [f32(slots * rows, depth)] * 2 + [f32(8, depth)],
        [displacement, density, element_kind],
        scratch=[
            vmem(3, rows, HALO, depth),
            vmem(rows, HALO, depth),
            vmem(rows, HALO, depth, dtype=jnp.int32),
            pltpu.SemaphoreType.DMA((6,)),
        ],
        places={0: pltpu.HBM, 1: pltpu.HBM, 2: pltpu.HBM},
        limit=53.25,
    )
    got_a = lax.ppermute(send_a, "gy", pairs_ya)
    got_b = lax.ppermute(send_b, BOTH, pairs_yb)

    sums = np.zeros((8, depth), np.float32)
    for rank, square in enumerate(CLASSES):
        for z in range(depth):
            sums[rank, z] = sum(
                weight_of(square + s * s) for s in range(-RADIUS, RADIUS + 1) if 0 <= z + s < depth
            )
    count = load_x.shape[0]
    applied, inverse = call(
        functools.partial(loads_and_weights, rows, cols, count_x, count_y),
        [f32(3, rows * cols, depth), f32(2 * RADIUS + 1, wide, depth)],
        [mark, load_x.reshape(1, count), load_y.reshape(1, count), load_z.reshape(1, count), load_force, jnp.asarray(sums)],
        places={0: pl.ANY},
        flops=2 * rows * cols * count * 6 * depth,
    )

    early = cols - HALO
    waves, tail, inner, scaled, sums = call(
        functools.partial(early_elements, rows, cols),
        [
            f32(6, rows, wide + HALO, depth),
            f32(6, rows, HALO, depth),
            f32(3, rows * cols, depth),
            f32(rows, wide + HALO, depth),
            f32(2, 8, depth),
        ],
        [disp, dens, kind, inverse, applied],
        scratch=[vmem(6, rows, HALO, depth)] * (cols // HALO - 2),
        flops=250 * rows * early * depth,
    )

    edge_u, edge_f, edge_s, send_a, send_b = call(
        functools.partial(unpack_y, rows, cols, count_y),
        [f32(3 * rows * HALO, depth), f32(rows * HALO, depth), f32(rows * HALO, depth)] + [f32(4, wide, depth)] * 2,
        [sums, disp, dens, kind, got_a, got_b],
        places={0: pl.ANY},
    )
    got_a = lax.ppermute(send_a, "gx", pairs_xa)
    got_b = lax.ppermute(send_b, BOTH, pairs_xb)

    waves, inner, scaled, sums, resid, near, filtered = call(
        functools.partial(late_elements, rows, cols),
        [f32(*v.shape) for v in (waves, inner, scaled, sums)]
        + [f32(3, rows * cols, depth), f32(RADIUS + 1, rows + 2 * RADIUS, cols, depth), f32(rows, cols, depth)],
        [waves, inner, scaled, tail, dens, kind, edge_u, edge_f, edge_s, applied, inverse, sums],
        scratch=[vmem(6 * rows * HALO, depth), pltpu.SemaphoreType.DMA],
        out_places={4: pltpu.HBM},
        flops=250 * rows * 2 * HALO * depth,
        aliases={0: 0, 1: 1, 2: 2},
    )
    outer, final, send_a, send_b, parts = call(
        functools.partial(outer_elements, rows, cols, count_x, devices),
        [f32(2, 3, cols, depth), f32(wide + HALO, depth)] + [f32(RADIUS, wide, depth)] * 2 + [f32(devices, depth)],
        [waves, dens, kind, edge_f, edge_s, got_a, got_b, inner, scaled, sums, inverse],
        scratch=[vmem(2, 6, wide + HALO, depth), vmem(wide, depth), vmem(2, 6, wide + 2 * HALO, depth)],
        flops=500 * wide * depth,
    )
    got_a = lax.ppermute(send_a, "gx", pairs_xa)
    got_b = lax.ppermute(send_b, BOTH, pairs_xb)
    parts = lax.all_to_all(parts, BOTH, 0, 0, tiled=True)

    sens, resid, comp, volume, _ = call(
        functools.partial(filter_rest, rows, cols, count_x, cells),
        [f32(rows, cols, depth), f32(3, rows * cols, depth), f32(1, 1), f32(1, 1), f32(*near.shape)],
        [near, filtered, final, got_a, got_b, parts, outer, resid],
        scratch=[vmem(2 * RADIUS, wide + HALO, depth), vmem(rows, cols, depth), pltpu.SemaphoreType.DMA((5,))],
        places={7: pltpu.HBM},
        out_places={0: pltpu.HBM, 1: pltpu.HBM, 2: pltpu.SMEM, 3: pltpu.SMEM},
        flops=20 * rows * cols * depth,
        aliases={0: 4, 7: 1},
    )
    return (
        sens,
        resid.reshape(3, rows, cols, depth),
        comp.reshape(()),
        volume.reshape(()),
    )


def solution(mesh):
    placed = (
        P(None, "gx", "gy", None),
        P("gx", "gy", None),
        P("gx", "gy", None),
        P(),
        P(),
        P(),
        P(),
    )
    return jax.shard_map(
        functools.partial(on_device, mesh.shape["gx"], mesh.shape["gy"]),
        mesh=mesh,
        in_specs=placed,
        out_specs=(P("gx", "gy", None), P(None, "gx", "gy", None), P(), P()),
        check_vma=False,
    )
```

```python
import functools

import jax
import jax.numpy as jnp
import numpy as np
from jax import lax
from jax.experimental import pallas as pl
from jax.experimental.pallas import tpu as pltpu
from jax.sharding import PartitionSpec as P

RADIUS = 3
PENALTY = 3.0
STIFF_FLOOR = 0.001
POISSON = 0.3
HALO = 8
BOTH = ("gx", "gy")
FULL = jax.ShapeDtypeStruct
FILTER_ROWS = 12


def element_matrix():
    lame_first = POISSON / ((1.0 + POISSON) * (1.0 - 2.0 * POISSON))
    shear_modulus = 0.5 / (1.0 + POISSON)
    material = np.zeros((6, 6))
    material[:3, :3] = lame_first
    for diagonal in range(3):
        material[diagonal, diagonal] += 2.0 * shear_modulus
        material[diagonal + 3, diagonal + 3] = shear_modulus
    points = [0.5 - 0.5 / np.sqrt(3.0), 0.5 + 0.5 / np.sqrt(3.0)]
    corners = [(a, b, e) for a in (0, 1) for b in (0, 1) for e in (0, 1)]
    result = np.zeros((24, 24))
    for point_x in points:
        for point_y in points:
            for point_z in points:
                strain = np.zeros((6, 24))
                for corner, (side_x, side_y, side_z) in enumerate(corners):
                    value_x = point_x if side_x else 1.0 - point_x
                    value_y = point_y if side_y else 1.0 - point_y
                    value_z = point_z if side_z else 1.0 - point_z
                    slope_x = (1.0 if side_x else -1.0) * value_y * value_z
                    slope_y = value_x * (1.0 if side_y else -1.0) * value_z
                    slope_z = value_x * value_y * (1.0 if side_z else -1.0)
                    column = 3 * corner
                    strain[0, column] = slope_x
                    strain[1, column + 1] = slope_y
                    strain[2, column + 2] = slope_z
                    strain[3, column] = slope_y
                    strain[3, column + 1] = slope_x
                    strain[4, column + 1] = slope_z
                    strain[4, column + 2] = slope_y
                    strain[5, column + 2] = slope_x
                    strain[5, column] = slope_z
                result += strain.T @ material @ strain / 8.0
    return result


def modal_matrix():
    pair = np.array([[1.0, 1.0], [-1.0, 1.0]])
    turn = np.kron(np.kron(np.kron(pair, pair), pair), np.eye(3))
    return turn @ element_matrix() @ turn.T / 64.0


SHEARS = ((3, 14), (4, 8), (6, 13))
NORMALS = (5, 7, 12)
PAIRS = ((10, 15), (11, 18), (17, 19))
TRIO = (9, 16, 20)
LASTS = (21, 22, 23)


def modal_constants():
    modal = modal_matrix()
    known = np.zeros((24, 24))
    shear = modal[3, 3]
    for first, second in SHEARS:
        known[np.ix_((first, second), (first, second))] = shear
    normal_off = modal[5, 7]
    normal_own = modal[5, 5] - normal_off
    known[np.ix_(NORMALS, NORMALS)] = normal_off
    pair_off = modal[10, 15]
    pair_own = modal[10, 10] - pair_off
    for both in PAIRS:
        known[np.ix_(both, both)] = pair_off
    trio = modal[9, 16]
    known[np.ix_(TRIO, TRIO)] = trio
    last = modal[21, 21]
    for group, own in ((NORMALS, normal_own), (sum(PAIRS, ()), pair_own), (TRIO, trio), (LASTS, last)):
        for degree in group:
            known[degree, degree] += own
    assert np.abs(known - modal).max() < 1e-12
    return tuple(float(v) for v in (shear, normal_off, normal_own, pair_off, pair_own, trio, last))


def weight_of(square):
    return max(0.0, RADIUS + 0.5 - float(np.sqrt(square)))


CLASSES = (0, 1, 2, 4, 5, 8, 9, 10)


def stiffness_of(physical):
    return STIFF_FLOOR + (1.0 - STIFF_FLOOR) * (physical * physical * physical)


def physical_of(density, kind):
    return jnp.where(kind == 1, 0.0, jnp.where(kind == 2, 1.0, density))


def factor_of(physical, kind):
    design = (kind != 1) & (kind != 2)
    return jnp.where(design, (-PENALTY * (1.0 - STIFF_FLOOR)) * (physical * physical), 0.0)


def pack_y(rows, cols, disp, dens, kind, out_a, out_b, mark, edge_d, edge_p, edge_k, sems):
    half = HALO // 2
    copies = []
    for side, start in ((0, 0), (half, cols - half)):
        for source, target in ((disp, edge_d), (dens, edge_p), (kind, edge_k)):
            lead = (slice(None),) * (len(source.shape) - 2)
            copies.append(
                pltpu.make_async_copy(
                    source.at[(*lead, pl.ds(start, half), slice(None))],
                    target.at[(*lead, pl.ds(side, half), slice(None))],
                    sems.at[len(copies)],
                )
            )
    for copy in copies:
        copy.start()
    for copy in copies:
        copy.wait()
    depth = disp.shape[-1]
    flat_d = edge_d.reshape(3 * rows * HALO, depth)
    flat_p = edge_p.reshape(rows * HALO, depth)
    flat_k = edge_k.reshape(rows * HALO, depth)

    def state(index):
        code = flat_k[pl.ds(index, rows, stride=HALO), :]
        return physical_of(flat_p[pl.ds(index, rows, stride=HALO), :], code), code

    def fill(low, high):
        slot = 0
        for c in range(3):
            for index in range(RADIUS + 1):
                low[pl.ds(slot * rows, rows), :] = flat_d[pl.ds(c * rows * HALO + index, rows, stride=HALO), :]
                slot += 1
        for index in range(RADIUS):
            low[pl.ds(slot * rows, rows), :] = factor_of(*state(index))
            slot += 1
        slot = 0
        for c in range(3):
            for index in range(HALO - RADIUS, HALO):
                high[pl.ds(slot * rows, rows), :] = flat_d[pl.ds(c * rows * HALO + index, rows, stride=HALO), :]
                slot += 1
        for index in range(HALO - RADIUS, HALO):
            physical, code = state(index)
            high[pl.ds(slot * rows, rows), :] = factor_of(physical, code)
            slot += 1
        high[pl.ds(slot * rows, rows), :] = stiffness_of(physical)

    mark[...] = jnp.zeros_like(mark)
    odd = lax.axis_index("gy") % 2

    @pl.when(odd == 0)
    def _():
        fill(out_b, out_a)

    @pl.when(odd == 1)
    def _():
        fill(out_a, out_b)


def unpack_y(rows, cols, count_y, after, disp, dens, kind, got_a, got_b, edge_u, edge_f, edge_s, out_a, out_b):
    del after
    here = lax.axis_index("gy")
    depth = disp.shape[-1]
    has_low = here > 0
    has_high = here < count_y - 1

    def fill(low, high):
        def put(ref, start, sublane, value):
            ref[pl.ds(start + sublane, rows, stride=HALO), :] = value

        zero = jnp.zeros((rows, depth), jnp.float32)
        slot = 0
        for c in range(3):
            for index in range(RADIUS + 1):
                put(edge_u, c * rows * HALO, index, jnp.where(has_high, high[pl.ds(slot * rows, rows), :], 0.0))
                slot += 1
        for index in range(RADIUS):
            put(edge_f, 0, index, jnp.where(has_high, high[pl.ds(slot * rows, rows), :], 0.0))
            slot += 1
        slot = 0
        for c in range(3):
            put(edge_u, c * rows * HALO, RADIUS + 1, zero)
            for index in range(HALO - RADIUS, HALO):
                put(edge_u, c * rows * HALO, index, low[pl.ds(slot * rows, rows), :])
                slot += 1
        for index in range(RADIUS, HALO - RADIUS):
            put(edge_f, 0, index, zero)
        for index in range(HALO - RADIUS, HALO):
            put(edge_f, 0, index, jnp.where(has_low, low[pl.ds(slot * rows, rows), :], 0.0))
            slot += 1
        edge_s[...] = jnp.zeros_like(edge_s)
        put(edge_s, 0, HALO - 1, jnp.where(has_low, low[pl.ds(slot * rows, rows), :], 0.0))

    odd = here % 2

    @pl.when(odd == 0)
    def _():
        fill(got_b, got_a)

    @pl.when(odd == 1)
    def _():
        fill(got_a, got_b)

    def send(out, row, with_stiff):
        for c in range(3):
            out[c, :cols, :] = disp[pl.ds((c * rows + row) * cols, cols), :]
            out[c, cols:, :] = edge_u[pl.ds((c * rows + row) * HALO, HALO), :]
        if with_stiff:
            at = pl.ds(row * cols, cols)
            out[3, :cols, :] = stiffness_of(physical_of(dens[at, :], kind[at, :]))
            out[3, cols:, :] = edge_s[pl.ds(row * HALO, HALO), :]
        else:
            out[3] = jnp.zeros_like(out[3])

    odd_x = lax.axis_index("gx") % 2

    @pl.when(odd_x == 0)
    def _():
        send(out_a, rows - 1, True)
        send(out_b, 0, False)

    @pl.when(odd_x == 1)
    def _():
        send(out_a, 0, False)
        send(out_b, rows - 1, True)


def loads_and_weights(rows, cols, count_x, count_y, after, load_x, load_y, load_z, force, sums, applied, inverse):
    del after
    depth = applied.shape[-1]
    place_x = lax.axis_index("gx") * rows
    place_y = lax.axis_index("gy") * cols
    local_x = load_x[...] - place_x
    local_y = load_y[...] - place_y
    owned = (local_x >= 0) & (local_x < rows) & (local_y >= 0) & (local_y < cols)
    target = jnp.where(owned, local_x * cols + local_y, -1)
    loads = target.shape[1]
    lanes = lax.broadcasted_iota(jnp.int32, (depth, loads), 0)
    hit_z = lanes == load_z[...]
    right = [[], []]
    for c in range(3):
        value = force[c : c + 1, :]
        coarse = value.astype(jnp.bfloat16).astype(jnp.float32)
        for part, piece in zip(right, (coarse, value - coarse)):
            part.append(jnp.where(hit_z, piece, 0.0).astype(jnp.bfloat16))
    place = lax.broadcasted_iota(jnp.int32, (rows * cols, loads), 0)
    left = jnp.where(place == target, 1.0, 0.0).astype(jnp.bfloat16)
    product = lax.dot_general(
        left, jnp.concatenate(right[0] + right[1], axis=0), (((1,), (1,)), ((), ())), preferred_element_type=jnp.float32
    )
    for c in range(3):
        applied[c] = product[:, c * depth : (c + 1) * depth] + product[:, (3 + c) * depth : (4 + c) * depth]

    wide = cols + HALO
    total_x, total_y = rows * count_x, cols * count_y
    sublane = lax.broadcasted_iota(jnp.int32, (wide, depth), 0)
    node_y = jnp.where(sublane >= wide - RADIUS, sublane - wide, sublane) + place_y
    inside_y = {
        shift: ((node_y + shift >= 0) & (node_y + shift < total_y)).astype(jnp.float32)
        for shift in range(-RADIUS, RADIUS + 1)
    }
    for kind in range(2 * RADIUS + 1):
        row = kind if kind <= RADIUS else rows - 2 * RADIUS - 1 + kind
        result = jnp.zeros((wide, depth), jnp.float32)
        for shift_y in range(-RADIUS, RADIUS + 1):
            line = jnp.zeros((1, depth), jnp.float32)
            for shift_x in range(-RADIUS, RADIUS + 1):
                square = shift_x * shift_x + shift_y * shift_y
                if square in CLASSES:
                    at = place_x + (row + shift_x)
                    inside = ((at >= 0) & (at < total_x)).astype(jnp.float32)
                    rank = CLASSES.index(square)
                    line = line + inside * sums[rank : rank + 1, :]
            result = result + inside_y[shift_y] * line
        inverse[kind] = 1.0 / jnp.where(result > 0.0, result, 1.0)


def shifted_z(value, lane, depth):
    beyond = jnp.where(lane == depth - 1, 0.0, pltpu.roll(value, depth - 1, 1))
    return value + beyond, beyond - value


def waves_of(here, there):
    return tuple(a + b for a, b in zip(here, there)) + tuple(b - a for a, b in zip(here, there))


def modal(before, after, stiff, constants):
    shear, normal_off, normal_own, pair_off, pair_own, trio, last = constants
    u = [None] * 24
    for low in range(12):
        if low >= 3:
            u[low] = before[low] + after[low]
        u[12 + low] = after[low] - before[low]
    f = [None] * 24
    terms = []

    def take(degree, pull):
        terms.append(pull * u[degree])
        f[degree] = pull * stiff

    for first, second in SHEARS:
        both = u[first] + u[second]
        pull = shear * both
        terms.append(pull * both)
        f[first] = f[second] = pull * stiff
    common = normal_off * (u[5] + u[7] + u[12])
    for degree in NORMALS:
        take(degree, common + normal_own * u[degree])
    for first, second in PAIRS:
        common = pair_off * (u[first] + u[second])
        take(first, common + pair_own * u[first])
        take(second, common + pair_own * u[second])
    common = u[9] + u[16] + u[20]
    for degree in TRIO:
        take(degree, trio * (common + u[degree]))
    for degree in LASTS:
        take(degree, last * u[degree])
    while len(terms) > 1:
        terms = [sum(terms[k : k + 2][1:], terms[k]) for k in range(0, len(terms), 2)]
    return terms[0], f


def lower_of(f):
    return tuple(f[12 + k] * -1.0 if f[k] is None else f[k] - f[12 + k] for k in range(12))


def upper_of(f):
    return tuple(f[12 + k] if f[k] is None else f[k] + f[12 + k] for k in range(12))


def along_y(g):
    return tuple(g[k] - g[6 + k] for k in range(6)), tuple(g[k] + g[6 + k] for k in range(6))


def along_z(g, lane):
    return [
        (g[c] - g[3 + c]) + jnp.where(lane == 0, 0.0, pltpu.roll(g[c] + g[3 + c], 1, 1)) for c in range(3)
    ]


def class_of(row, rows):
    return jnp.where(row < RADIUS, row, jnp.where(row >= rows - RADIUS, row - (rows - 2 * RADIUS - 1), RADIUS))


def march(rows, block, waves, state, inverse, emit, put, own):
    constants = modal_constants()
    depth = waves.shape[-1]
    first = 8 * block
    zero = jnp.zeros((HALO, depth), jnp.float32)

    def nodes(row):
        return waves_of(
            [waves[k, row, first : first + 8, :] for k in range(6)],
            [waves[k, row, first + 1 : first + 9, :] for k in range(6)],
        )

    def step(row, carry):
        before, held, total, filled = carry
        after = nodes(row + 1)
        physical, stiff, factor = state(row)
        energy, f = modal(before, after, stiff, constants)
        put(row, factor * energy * inverse[class_of(row, rows), first : first + 8, :])
        if own:
            total = total + stiff * energy
            filled = filled + physical
        emit(row, *along_y(tuple(a + b for a, b in zip(held, lower_of(f)))))
        return after, upper_of(f), total, filled

    carry = (nodes(0), (zero,) * 12, zero, zero)
    carry = lax.fori_loop(0, rows - 2, step, carry, unroll=True)
    _, held, total, filled = step(rows - 2, carry)
    emit(rows - 1, *along_y(held))
    if own:
        filled = filled + state(rows - 1)[0]
    return total, filled


def own_state(dens, kind, cols, first):
    def state(row):
        at = pl.ds(pl.multiple_of(row * cols + first, 8), HALO)
        code = kind[at, :]
        physical = physical_of(dens[at, :], code)
        return physical, stiffness_of(physical), factor_of(physical, code)

    return state


def joiner(cols, block, tail_in, tail_out, applied, resid):
    first = 8 * block
    depth = resid.shape[-1]
    lane = lax.broadcasted_iota(jnp.int32, (HALO, depth), 1)
    sublane = lax.broadcasted_iota(jnp.int32, (HALO, depth), 0)

    def emit(row, low, high):
        parts = []
        for k in range(6):
            turned = pltpu.roll(high[k], 1, 0)
            if tail_out is not None:
                tail_out[k, row] = turned
            before = 0.0 if tail_in is None else tail_in[k, row]
            parts.append(low[k] + jnp.where(sublane == 0, before, turned))
        at = pl.ds(pl.multiple_of(row * cols + first, 8), HALO)
        for c, value in enumerate(along_z(parts, lane)):
            resid[c, at, :] = applied[c, at, :] - value

    return emit


def early_elements(
    rows, cols, disp, dens, kind, inverse, applied, waves, tail, resid, scaled, sums, *tails
):
    depth = disp.shape[-1]
    lane = lax.broadcasted_iota(jnp.int32, (HALO, depth), 1)

    def turn(row, nothing):
        for c in range(3):
            for block in range(cols // 8):
                at = pl.ds(pl.multiple_of((c * rows + row) * cols + 8 * block, 8), HALO)
                for r, value in enumerate(shifted_z(disp[at, :], lane, depth)):
                    waves[3 * r + c, row, 8 * block : 8 * block + 8, :] = value
                    if block == 0:
                        waves[3 * r + c, row, cols + HALO :, :] = value
        return nothing

    lax.fori_loop(0, rows, turn, 0, unroll=8)
    total = filled = jnp.zeros((HALO, depth), jnp.float32)
    chain = (None, *tails, tail)
    for block in range(cols // 8 - 1):
        first = 8 * block

        def put(row, value, first=first):
            scaled[row, first + 8 : first + 16, :] = value

        emit = joiner(cols, block, chain[block], chain[block + 1], applied, resid)
        state = own_state(dens, kind, cols, first)
        more = march(rows, block, waves, state, inverse, emit, put, True)
        total, filled = total + more[0], filled + more[1]
    sums[0] = total
    sums[1] = filled


def late_elements(
    rows, cols,
    waves_in, resid_in, scaled_in, tail, dens, kind, edge_u, edge_f, edge_s, applied, inverse, sums_a,
    waves, resid, scaled, sums, resid_out, near, filtered, far_h, lines, sem,
):
    depth = dens.shape[-1]
    del waves_in, resid_in, scaled_in
    wide = cols + HALO
    lane = lax.broadcasted_iota(jnp.int32, (HALO, depth), 1)

    def turn(row, nothing):
        for c in range(3):
            at = pl.ds(pl.multiple_of((c * rows + row) * HALO, 8), HALO)
            for r, value in enumerate(shifted_z(edge_u[at, :], lane, depth)):
                waves[3 * r + c, row, cols:wide, :] = value
        return nothing

    lax.fori_loop(0, rows, turn, 0, unroll=16)

    def edge_state(row):
        at = pl.ds(pl.multiple_of(row * HALO, 8), HALO)
        return None, edge_s[at, :], edge_f[at, :]

    def put_edge(row, value):
        scaled[row, :HALO, :] = value
        scaled[row, wide:, :] = value

    def emit_edge(row, low, high):
        for k in range(6):
            far_h[pl.ds(pl.multiple_of((k * rows + row) * HALO, 8), HALO), :] = high[k]

    march(rows, cols // 8, waves, edge_state, inverse, emit_edge, put_edge, False)
    last = cols // 8 - 1

    def put(row, value):
        scaled[row, cols:wide, :] = value

    emit = joiner(cols, last, tail, None, applied, resid)
    state = own_state(dens, kind, cols, 8 * last)
    total, filled = march(rows, last, waves, state, inverse, emit, put, True)
    sums[0] = sums_a[0] + total
    sums[1] = sums_a[1] + filled

    parts = [far_h[pl.ds(k * rows * HALO + HALO - 1, rows, stride=HALO), :] for k in range(6)]
    at = pl.ds(0, rows, stride=cols)
    for c, value in enumerate(along_z(parts, lax.broadcasted_iota(jnp.int32, (rows, depth), 1))):
        resid[c, at, :] = resid[c, at, :] - value
    middle = pl.ds(cols, (rows - 2) * cols)
    copy = pltpu.make_async_copy(resid.at[:, middle, :], resid_out.at[:, middle, :], sem)
    copy.start()

    def own(row, nothing):
        lines_y(near, row + RADIUS, cols, lambda start: scaled[row, start : start + 8, :])
        return nothing

    lax.fori_loop(0, rows - 1, own, 0, unroll=True)
    band = bands(depth)
    inside = range(RADIUS + 1, rows - RADIUS - 1)
    for start in inside[:: FILTER_ROWS]:
        picks = range(start, min(start + FILTER_ROWS, inside.stop))
        rest = filter_rows(near, lines, filtered, picks, cols, band)
        filtered[picks.start : picks.stop] = filtered[picks.start : picks.stop] + rest
    copy.wait()


def outer_elements(
    rows, cols, count_x, devices,
    waves, dens, kind, edge_f, edge_s, got_a, got_b, inner, scaled, sums, inverse,
    resid, final, out_a, out_b, parts, ring, stiff_low, carry_y,
):
    depth = dens.shape[-1]
    constants = modal_constants()
    wide = cols + HALO
    blocks = wide // HALO
    lane = lax.broadcasted_iota(jnp.int32, (HALO, depth), 1)
    here = lax.axis_index("gx")
    has_low = here > 0
    has_high = here < count_x - 1
    odd = here % 2

    def take(low, high):
        for block in range(blocks):
            first = 8 * block
            for c in range(3):
                for side, value in enumerate((low[c, first : first + 8, :], high[c, first : first + 8, :])):
                    if side:
                        value = jnp.where(has_high, value, 0.0)
                    for r, wave in enumerate(shifted_z(value, lane, depth)):
                        ring[side, 3 * r + c, first : first + 8, :] = wave
                        if block == 0:
                            ring[side, 3 * r + c, wide:, :] = wave
        stiff_low[...] = jnp.where(has_low, low[3], 0.0)

    @pl.when(odd == 0)
    def _():
        take(got_b, got_a)

    @pl.when(odd == 1)
    def _():
        take(got_a, got_b)

    total = sums[0]
    for block in (blocks - 1, *range(blocks - 1)):
        own = block < blocks - 1
        first = 8 * block

        def nodes(load):
            return waves_of(
                [load(k)[first : first + 8, :] for k in range(6)], [load(k)[first + 1 : first + 9, :] for k in range(6)]
            )

        line = [
            nodes(lambda k: ring.at[0, k]),
            nodes(lambda k: waves.at[k, 0]),
            nodes(lambda k: waves.at[k, rows - 1]),
            nodes(lambda k: ring.at[1, k]),
        ]
        _, f_low = modal(line[0], line[1], stiff_low[first : first + 8, :], constants)
        if own:
            _, stiff, factor = own_state(dens, kind, cols, first)(rows - 1)
        else:
            at = pl.ds((rows - 1) * HALO, HALO)
            stiff, factor = edge_s[at, :], edge_f[at, :]
        energy, f_high = modal(line[2], line[3], stiff, constants)
        value = factor * energy * inverse[2 * RADIUS, first : first + 8, :]
        if own:
            total = total + stiff * energy
            final[first + 8 : first + 16, :] = value
        else:
            final[:HALO, :] = value
            final[wide:, :] = value
        for index, (row, g) in enumerate(((0, upper_of(f_low)), (rows - 1, lower_of(f_high)))):
            low, high = along_y(g)
            if own:
                joined = []
                for k in range(6):
                    carry_y[index, k, first + 9 : first + 17, :] = high[k]
                    joined.append(low[k] + carry_y[index, k, first + 8 : first + 16, :])
                for c, value in enumerate(along_z(joined, lane)):
                    resid[index, c, first : first + 8, :] = inner[c, pl.ds(row * cols + first, HALO), :] - value
            else:
                for k in range(6):
                    carry_y[index, k, 1:9, :] = high[k]

    half = depth // 2
    pieces = []
    for value in (total, sums[1]):
        line = jnp.sum(value, axis=0, keepdims=True)
        pieces.append(line + pltpu.roll(line, half, 1))
    line = jnp.where(lax.broadcasted_iota(jnp.int32, (1, depth), 1) < half, pieces[0], pieces[1])
    parts[...] = jnp.broadcast_to(line, (devices, depth))

    def send(up, down):
        for index in range(RADIUS - 1):
            up[index] = scaled[rows - RADIUS + index, :wide, :]
        up[RADIUS - 1] = final[:wide, :]
        for index in range(RADIUS):
            down[index] = scaled[index, :wide, :]

    @pl.when(odd == 0)
    def _():
        send(out_a, out_b)

    @pl.when(odd == 1)
    def _():
        send(out_b, out_a)


def lines_y(near, row, cols, load):
    for block in range(cols // 8):
        start = HALO + 8 * block
        near[0, row, 8 * block : 8 * block + 8, :] = load(start)
        for shift in range(1, RADIUS + 1):
            near[shift, row, 8 * block : 8 * block + 8, :] = load(start + shift) + load(start - shift)


def bands(depth):
    row = lax.broadcasted_iota(jnp.int32, (depth, depth), 0)
    column = lax.broadcasted_iota(jnp.int32, (depth, depth), 1)
    away = jnp.abs(row - column)
    return jnp.concatenate(
        [jnp.where(away == shift, 1.0, 0.0).astype(jnp.bfloat16) for shift in range(1, RADIUS + 1)], axis=0
    )


def filter_rows(near, lines, result, picks, cols, band):
    depth = near.shape[-1]
    for rank, row in enumerate(picks):
        for block in range(cols // 8):
            at = pl.ds(block * 8, 8)
            classes = {}
            for shift_x in range(RADIUS + 1):
                for shift_y in range(RADIUS + 1):
                    square = shift_x * shift_x + shift_y * shift_y
                    if square not in CLASSES:
                        continue
                    value = near[shift_y, row + (RADIUS + shift_x), at, :]
                    if shift_x:
                        value = value + near[shift_y, row + (RADIUS - shift_x), at, :]
                    classes[square] = value if square not in classes else classes[square] + value
            for shift_z in range(RADIUS + 1):
                line = None
                for square, value in classes.items():
                    weight = weight_of(square + shift_z * shift_z)
                    if weight > 0.0:
                        line = weight * value if line is None else line + weight * value
                if shift_z:
                    first = rank * cols + 8 * block
                    lines[first : first + 8, (shift_z - 1) * depth : shift_z * depth] = line
                else:
                    result[row, at, :] = line
    value = lines[: len(picks) * cols, :]
    coarse = value.astype(jnp.bfloat16)
    rest = (value - coarse.astype(jnp.float32)).astype(jnp.bfloat16)
    total = jnp.dot(coarse, band, preferred_element_type=jnp.float32)
    total = total + jnp.dot(rest, band, preferred_element_type=jnp.float32)
    return total.reshape(len(picks), cols, depth)


def filter_rest(
    rows, cols, count_x, cells,
    near_in, inner, final, got_a, got_b, parts, outer, resid_in,
    sens, resid, comp, vol, near, ends, result_v, lines, sems,
):
    depth = sens.shape[-1]
    del near_in, resid_in
    wide = cols + HALO
    copies = [
        pltpu.make_async_copy(outer.at[index], resid.at[:, pl.ds(row * cols, cols), :], sems.at[index])
        for index, row in enumerate((0, rows - 1))
    ]
    for copy in copies:
        copy.start()
    here = lax.axis_index("gx")
    has_low = here > 0
    has_high = here < count_x - 1
    odd = here % 2
    half = depth // 2
    line = jnp.sum(parts[...], axis=0, keepdims=True)
    first = lax.broadcasted_iota(jnp.int32, (1, depth), 1) < half
    compliance = jnp.sum(jnp.where(first, line, 0.0))
    volume = jnp.sum(jnp.where(first, 0.0, line))
    comp[0, 0] = compliance
    vol[0, 0] = volume / cells
    scale = cells / jnp.broadcast_to(compliance, (8, depth))

    def send(start, size):
        at = pl.ds(start, size)
        copies.append(pltpu.make_async_copy(result_v.at[at], sens.at[at], sems.at[len(copies)]))
        copies[-1].start()

    low_end, high_start = RADIUS + 1, rows - RADIUS - 1
    for row in range(low_end, high_start):
        for block in range(cols // 8):
            at = pl.ds(block * 8, 8)
            result_v[row, at, :] = inner[row, at, :] * scale
    send(low_end, high_start - low_end)

    def take(low, high):
        for index in range(RADIUS):
            for source, has, at in ((low, has_low, index), (high, has_high, RADIUS + index)):
                value = jnp.where(has, source[index], 0.0)
                ends[at, :wide, :] = value
                ends[at, wide:, :] = value[:HALO]

    @pl.when(odd == 0)
    def _():
        take(got_b, got_a)

    @pl.when(odd == 1)
    def _():
        take(got_a, got_b)

    for index in range(RADIUS):
        lines_y(near, index, cols, lambda start, at=index: ends[at, start : start + 8, :])
        lines_y(near, rows + RADIUS + index, cols, lambda start, at=RADIUS + index: ends[at, start : start + 8, :])
    lines_y(near, rows + RADIUS - 1, cols, lambda start: final[start : start + 8, :])
    picks = (*range(low_end), *range(high_start, rows))
    rest = filter_rows(near, lines, result_v, picks, cols, bands(depth))
    for start, size, more in ((0, low_end, rest[:low_end]), (high_start, rows - high_start, rest[low_end:])):
        result_v[start : start + size] = (result_v[start : start + size] + more) * scale[:1]
        send(start, size)
    for copy in copies:
        copy.wait()


def call(body, shapes, inputs, scratch=(), places=None, out_places=None, flops=0, limit=24, aliases=None):
    places, out_places = places or {}, out_places or {}
    in_specs = [pl.BlockSpec(memory_space=places.get(rank, pltpu.VMEM)) for rank in range(len(inputs))]
    out_specs = [pl.BlockSpec(memory_space=out_places.get(rank, pltpu.VMEM)) for rank in range(len(shapes))]
    moved = sum(int(np.prod(v.shape)) * 4 for v in list(inputs) + list(shapes))
    return pl.pallas_call(
        body,
        out_shape=[FULL(v.shape, v.dtype) for v in shapes],
        in_specs=in_specs,
        out_specs=out_specs,
        scratch_shapes=list(scratch),
        input_output_aliases=aliases or {},
        cost_estimate=pl.CostEstimate(flops=flops, bytes_accessed=moved, transcendentals=0),
        compiler_params=pltpu.CompilerParams(vmem_limit_bytes=int(limit * 1024 * 1024)),
    )(*inputs)


def f32(*shape):
    return FULL(shape, jnp.float32)


def vmem(*shape, dtype=jnp.float32):
    return pltpu.VMEM(shape, dtype)


def on_device(count_x, count_y, displacement, density, element_kind, load_x, load_y, load_z, load_force):
    rows, cols, depth = density.shape
    wide = cols + HALO
    devices = count_x * count_y
    cells = float(rows * cols * depth * devices)

    pairs_ya = [(k, k ^ 1) for k in range(count_y)]
    pairs_xa = [(k, k ^ 1) for k in range(count_x)]
    pairs_yb, pairs_xb = [], []
    for i in range(count_x):
        for j in range(count_y):
            here = i * count_y + j
            inside_y, inside_x = 0 < j < count_y - 1, 0 < i < count_x - 1
            pairs_yb.append((here, i * count_y + ((j + 1) ^ 1) - 1 if inside_y else (i ^ 1) * count_y + j))
            pairs_xb.append((here, (((i + 1) ^ 1) - 1) * count_y + j if inside_x else i * count_y + (j ^ 1)))

    disp = displacement.reshape(3 * rows * cols, depth)
    dens = density.reshape(rows * cols, depth)
    kind = element_kind.reshape(rows * cols, depth)

    slots = 4 * RADIUS + RADIUS
    send_a, send_b, mark = call(
        functools.partial(pack_y, rows, cols),
        [f32(slots * rows, depth)] * 2 + [f32(8, depth)],
        [displacement, density, element_kind],
        scratch=[
            vmem(3, rows, HALO, depth),
            vmem(rows, HALO, depth),
            vmem(rows, HALO, depth, dtype=jnp.int32),
            pltpu.SemaphoreType.DMA((6,)),
        ],
        places={0: pltpu.HBM, 1: pltpu.HBM, 2: pltpu.HBM},
        limit=53.25,
    )
    got_b = lax.ppermute(send_b, BOTH, pairs_yb)
    got_a = lax.ppermute(send_a, "gy", pairs_ya)

    sums = np.zeros((8, depth), np.float32)
    for rank, square in enumerate(CLASSES):
        for z in range(depth):
            sums[rank, z] = sum(
                weight_of(square + s * s) for s in range(-RADIUS, RADIUS + 1) if 0 <= z + s < depth
            )
    count = load_x.shape[0]
    applied, inverse = call(
        functools.partial(loads_and_weights, rows, cols, count_x, count_y),
        [f32(3, rows * cols, depth), f32(2 * RADIUS + 1, wide, depth)],
        [mark, load_x.reshape(1, count), load_y.reshape(1, count), load_z.reshape(1, count), load_force, jnp.asarray(sums)],
        places={0: pl.ANY},
        flops=2 * rows * cols * count * 6 * depth,
    )

    early = cols - HALO
    waves, tail, inner, scaled, sums = call(
        functools.partial(early_elements, rows, cols),
        [
            f32(6, rows, wide + HALO, depth),
            f32(6, rows, HALO, depth),
            f32(3, rows * cols, depth),
            f32(rows, wide + HALO, depth),
            f32(2, 8, depth),
        ],
        [disp, dens, kind, inverse, applied],
        scratch=[vmem(6, rows, HALO, depth)] * (cols // HALO - 2),
        flops=250 * rows * early * depth,
    )

    edge_u, edge_f, edge_s, send_a, send_b = call(
        functools.partial(unpack_y, rows, cols, count_y),
        [f32(3 * rows * HALO, depth), f32(rows * HALO, depth), f32(rows * HALO, depth)] + [f32(4, wide, depth)] * 2,
        [sums, disp, dens, kind, got_a, got_b],
        places={0: pl.ANY},
    )
    got_b = lax.ppermute(send_b, BOTH, pairs_xb)
    got_a = lax.ppermute(send_a, "gx", pairs_xa)

    waves, inner, scaled, sums, resid, near, filtered = call(
        functools.partial(late_elements, rows, cols),
        [f32(*v.shape) for v in (waves, inner, scaled, sums)]
        + [f32(3, rows * cols, depth), f32(RADIUS + 1, rows + 2 * RADIUS, cols, depth), f32(rows, cols, depth)],
        [waves, inner, scaled, tail, dens, kind, edge_u, edge_f, edge_s, applied, inverse, sums],
        scratch=[
            vmem(6 * rows * HALO, depth),
            vmem(FILTER_ROWS * cols, RADIUS * depth),
            pltpu.SemaphoreType.DMA,
        ],
        out_places={4: pltpu.HBM},
        flops=250 * rows * 2 * HALO * depth,
        aliases={0: 0, 1: 1, 2: 2},
    )
    outer, final, send_a, send_b, parts = call(
        functools.partial(outer_elements, rows, cols, count_x, devices),
        [f32(2, 3, cols, depth), f32(wide + HALO, depth)] + [f32(RADIUS, wide, depth)] * 2 + [f32(devices, depth)],
        [waves, dens, kind, edge_f, edge_s, got_a, got_b, inner, scaled, sums, inverse],
        scratch=[vmem(2, 6, wide + HALO, depth), vmem(wide, depth), vmem(2, 6, wide + 2 * HALO, depth)],
        flops=500 * wide * depth,
    )
    got_b = lax.ppermute(send_b, BOTH, pairs_xb)
    got_a = lax.ppermute(send_a, "gx", pairs_xa)
    parts = lax.all_to_all(parts, BOTH, 0, 0, tiled=True)

    sens, resid, comp, volume, _ = call(
        functools.partial(filter_rest, rows, cols, count_x, cells),
        [f32(rows, cols, depth), f32(3, rows * cols, depth), f32(1, 1), f32(1, 1), f32(*near.shape)],
        [near, filtered, final, got_a, got_b, parts, outer, resid],
        scratch=[
            vmem(2 * RADIUS, wide + HALO, depth),
            vmem(rows, cols, depth),
            vmem(2 * (RADIUS + 1) * cols, RADIUS * depth),
            pltpu.SemaphoreType.DMA((5,)),
        ],
        places={7: pltpu.HBM},
        out_places={0: pltpu.HBM, 1: pltpu.HBM, 2: pltpu.SMEM, 3: pltpu.SMEM},
        flops=20 * rows * cols * depth,
        aliases={0: 4, 7: 1},
    )
    return (
        sens,
        resid.reshape(3, rows, cols, depth),
        comp.reshape(()),
        volume.reshape(()),
    )


def solution(mesh):
    placed = (
        P(None, "gx", "gy", None),
        P("gx", "gy", None),
        P("gx", "gy", None),
        P(),
        P(),
        P(),
        P(),
    )
    return jax.shard_map(
        functools.partial(on_device, mesh.shape["gx"], mesh.shape["gy"]),
        mesh=mesh,
        in_specs=placed,
        out_specs=(P("gx", "gy", None), P(None, "gx", "gy", None), P(), P()),
        check_vma=False,
    )
```

```python
import functools

import jax
import jax.numpy as jnp
import numpy as np
from jax import lax
from jax.experimental import pallas as pl
from jax.experimental.pallas import tpu as pltpu
from jax.sharding import PartitionSpec as P

RADIUS = 3
PENALTY = 3.0
STIFF_FLOOR = 0.001
POISSON = 0.3
HALO = 8
BOTH = ("gx", "gy")
FULL = jax.ShapeDtypeStruct
FILTER_ROWS = 12


def element_matrix():
    lame_first = POISSON / ((1.0 + POISSON) * (1.0 - 2.0 * POISSON))
    shear_modulus = 0.5 / (1.0 + POISSON)
    material = np.zeros((6, 6))
    material[:3, :3] = lame_first
    for diagonal in range(3):
        material[diagonal, diagonal] += 2.0 * shear_modulus
        material[diagonal + 3, diagonal + 3] = shear_modulus
    points = [0.5 - 0.5 / np.sqrt(3.0), 0.5 + 0.5 / np.sqrt(3.0)]
    corners = [(a, b, e) for a in (0, 1) for b in (0, 1) for e in (0, 1)]
    result = np.zeros((24, 24))
    for point_x in points:
        for point_y in points:
            for point_z in points:
                strain = np.zeros((6, 24))
                for corner, (side_x, side_y, side_z) in enumerate(corners):
                    value_x = point_x if side_x else 1.0 - point_x
                    value_y = point_y if side_y else 1.0 - point_y
                    value_z = point_z if side_z else 1.0 - point_z
                    slope_x = (1.0 if side_x else -1.0) * value_y * value_z
                    slope_y = value_x * (1.0 if side_y else -1.0) * value_z
                    slope_z = value_x * value_y * (1.0 if side_z else -1.0)
                    column = 3 * corner
                    strain[0, column] = slope_x
                    strain[1, column + 1] = slope_y
                    strain[2, column + 2] = slope_z
                    strain[3, column] = slope_y
                    strain[3, column + 1] = slope_x
                    strain[4, column + 1] = slope_z
                    strain[4, column + 2] = slope_y
                    strain[5, column + 2] = slope_x
                    strain[5, column] = slope_z
                result += strain.T @ material @ strain / 8.0
    return result


def modal_matrix():
    pair = np.array([[1.0, 1.0], [-1.0, 1.0]])
    turn = np.kron(np.kron(np.kron(pair, pair), pair), np.eye(3))
    return turn @ element_matrix() @ turn.T / 64.0


SHEARS = ((3, 14), (4, 8), (6, 13))
NORMALS = (5, 7, 12)
PAIRS = ((10, 15), (11, 18), (17, 19))
TRIO = (9, 16, 20)
LASTS = (21, 22, 23)


def modal_constants():
    modal = modal_matrix()
    known = np.zeros((24, 24))
    shear = modal[3, 3]
    for first, second in SHEARS:
        known[np.ix_((first, second), (first, second))] = shear
    normal_off = modal[5, 7]
    normal_own = modal[5, 5] - normal_off
    known[np.ix_(NORMALS, NORMALS)] = normal_off
    pair_off = modal[10, 15]
    pair_own = modal[10, 10] - pair_off
    for both in PAIRS:
        known[np.ix_(both, both)] = pair_off
    trio = modal[9, 16]
    known[np.ix_(TRIO, TRIO)] = trio
    last = modal[21, 21]
    for group, own in ((NORMALS, normal_own), (sum(PAIRS, ()), pair_own), (TRIO, trio), (LASTS, last)):
        for degree in group:
            known[degree, degree] += own
    assert np.abs(known - modal).max() < 1e-12
    return tuple(float(v) for v in (shear, normal_off, normal_own, pair_off, pair_own, trio, last))


def weight_of(square):
    return max(0.0, RADIUS + 0.5 - float(np.sqrt(square)))


CLASSES = (0, 1, 2, 4, 5, 8, 9, 10)


def stiffness_of(physical):
    return STIFF_FLOOR + (1.0 - STIFF_FLOOR) * (physical * physical * physical)


def physical_of(density, kind):
    return jnp.where(kind == 1, 0.0, jnp.where(kind == 2, 1.0, density))


def factor_of(physical, kind):
    design = (kind != 1) & (kind != 2)
    return jnp.where(design, (-PENALTY * (1.0 - STIFF_FLOOR)) * (physical * physical), 0.0)


def pack_y(rows, cols, disp, dens, kind, out_a, out_b, mark, edge_d, edge_p, edge_k, sems):
    half = HALO // 2
    copies = []
    for side, start in ((0, 0), (half, cols - half)):
        for source, target in ((disp, edge_d), (dens, edge_p), (kind, edge_k)):
            lead = (slice(None),) * (len(source.shape) - 2)
            copies.append(
                pltpu.make_async_copy(
                    source.at[(*lead, pl.ds(start, half), slice(None))],
                    target.at[(*lead, pl.ds(side, half), slice(None))],
                    sems.at[len(copies)],
                )
            )
    for copy in copies:
        copy.start()
    for copy in copies:
        copy.wait()
    depth = disp.shape[-1]
    flat_d = edge_d.reshape(3 * rows * HALO, depth)
    flat_p = edge_p.reshape(rows * HALO, depth)
    flat_k = edge_k.reshape(rows * HALO, depth)

    def state(index):
        code = flat_k[pl.ds(index, rows, stride=HALO), :]
        return physical_of(flat_p[pl.ds(index, rows, stride=HALO), :], code), code

    def fill(low, high):
        slot = 0
        for c in range(3):
            for index in range(RADIUS + 1):
                low[pl.ds(slot * rows, rows), :] = flat_d[pl.ds(c * rows * HALO + index, rows, stride=HALO), :]
                slot += 1
        for index in range(RADIUS):
            low[pl.ds(slot * rows, rows), :] = factor_of(*state(index))
            slot += 1
        slot = 0
        for c in range(3):
            for index in range(HALO - RADIUS, HALO):
                high[pl.ds(slot * rows, rows), :] = flat_d[pl.ds(c * rows * HALO + index, rows, stride=HALO), :]
                slot += 1
        for index in range(HALO - RADIUS, HALO):
            physical, code = state(index)
            high[pl.ds(slot * rows, rows), :] = factor_of(physical, code)
            slot += 1
        high[pl.ds(slot * rows, rows), :] = stiffness_of(physical)

    mark[...] = jnp.zeros_like(mark)
    odd = lax.axis_index("gy") % 2

    @pl.when(odd == 0)
    def _():
        fill(out_b, out_a)

    @pl.when(odd == 1)
    def _():
        fill(out_a, out_b)


def unpack_y(rows, cols, count_y, after, disp, dens, kind, got_a, got_b, edge_u, edge_f, edge_s, out_a, out_b):
    del after
    here = lax.axis_index("gy")
    depth = disp.shape[-1]
    has_low = here > 0
    has_high = here < count_y - 1

    def fill(low, high):
        def put(ref, start, sublane, value):
            ref[pl.ds(start + sublane, rows, stride=HALO), :] = value

        zero = jnp.zeros((rows, depth), jnp.float32)
        slot = 0
        for c in range(3):
            for index in range(RADIUS + 1):
                put(edge_u, c * rows * HALO, index, jnp.where(has_high, high[pl.ds(slot * rows, rows), :], 0.0))
                slot += 1
        for index in range(RADIUS):
            put(edge_f, 0, index, jnp.where(has_high, high[pl.ds(slot * rows, rows), :], 0.0))
            slot += 1
        slot = 0
        for c in range(3):
            put(edge_u, c * rows * HALO, RADIUS + 1, zero)
            for index in range(HALO - RADIUS, HALO):
                put(edge_u, c * rows * HALO, index, low[pl.ds(slot * rows, rows), :])
                slot += 1
        for index in range(RADIUS, HALO - RADIUS):
            put(edge_f, 0, index, zero)
        for index in range(HALO - RADIUS, HALO):
            put(edge_f, 0, index, jnp.where(has_low, low[pl.ds(slot * rows, rows), :], 0.0))
            slot += 1
        edge_s[...] = jnp.zeros_like(edge_s)
        put(edge_s, 0, HALO - 1, jnp.where(has_low, low[pl.ds(slot * rows, rows), :], 0.0))

    odd = here % 2

    @pl.when(odd == 0)
    def _():
        fill(got_b, got_a)

    @pl.when(odd == 1)
    def _():
        fill(got_a, got_b)

    def send(out, row, with_stiff):
        for c in range(3):
            out[c, :cols, :] = disp[pl.ds((c * rows + row) * cols, cols), :]
            out[c, cols:, :] = edge_u[pl.ds((c * rows + row) * HALO, HALO), :]
        if with_stiff:
            at = pl.ds(row * cols, cols)
            out[3, :cols, :] = stiffness_of(physical_of(dens[at, :], kind[at, :]))
            out[3, cols:, :] = edge_s[pl.ds(row * HALO, HALO), :]
        else:
            out[3] = jnp.zeros_like(out[3])

    odd_x = lax.axis_index("gx") % 2

    @pl.when(odd_x == 0)
    def _():
        send(out_a, rows - 1, True)
        send(out_b, 0, False)

    @pl.when(odd_x == 1)
    def _():
        send(out_a, 0, False)
        send(out_b, rows - 1, True)


def loads_and_weights(rows, cols, count_x, count_y, after, load_x, load_y, load_z, force, sums, applied, inverse):
    del after
    depth = applied.shape[-1]
    place_x = lax.axis_index("gx") * rows
    place_y = lax.axis_index("gy") * cols
    local_x = load_x[...] - place_x
    local_y = load_y[...] - place_y
    owned = (local_x >= 0) & (local_x < rows) & (local_y >= 0) & (local_y < cols)
    target = jnp.where(owned, local_x * cols + local_y, -1)
    loads = target.shape[1]
    lanes = lax.broadcasted_iota(jnp.int32, (depth, loads), 0)
    hit_z = lanes == load_z[...]
    right = [[], []]
    for c in range(3):
        value = force[c : c + 1, :]
        coarse = value.astype(jnp.bfloat16).astype(jnp.float32)
        for part, piece in zip(right, (coarse, value - coarse)):
            part.append(jnp.where(hit_z, piece, 0.0).astype(jnp.bfloat16))
    place = lax.broadcasted_iota(jnp.int32, (rows * cols, loads), 0)
    left = jnp.where(place == target, 1.0, 0.0).astype(jnp.bfloat16)
    product = lax.dot_general(
        left, jnp.concatenate(right[0] + right[1], axis=0), (((1,), (1,)), ((), ())), preferred_element_type=jnp.float32
    )
    for c in range(3):
        applied[c] = product[:, c * depth : (c + 1) * depth] + product[:, (3 + c) * depth : (4 + c) * depth]

    wide = cols + HALO
    total_x, total_y = rows * count_x, cols * count_y
    sublane = lax.broadcasted_iota(jnp.int32, (wide, depth), 0)
    node_y = jnp.where(sublane >= wide - RADIUS, sublane - wide, sublane) + place_y
    inside_y = {
        shift: ((node_y + shift >= 0) & (node_y + shift < total_y)).astype(jnp.float32)
        for shift in range(-RADIUS, RADIUS + 1)
    }
    for kind in range(2 * RADIUS + 1):
        row = kind if kind <= RADIUS else rows - 2 * RADIUS - 1 + kind
        result = jnp.zeros((wide, depth), jnp.float32)
        for shift_y in range(-RADIUS, RADIUS + 1):
            line = jnp.zeros((1, depth), jnp.float32)
            for shift_x in range(-RADIUS, RADIUS + 1):
                square = shift_x * shift_x + shift_y * shift_y
                if square in CLASSES:
                    at = place_x + (row + shift_x)
                    inside = ((at >= 0) & (at < total_x)).astype(jnp.float32)
                    rank = CLASSES.index(square)
                    line = line + inside * sums[rank : rank + 1, :]
            result = result + inside_y[shift_y] * line
        inverse[kind] = 1.0 / jnp.where(result > 0.0, result, 1.0)


def shifted_z(value, lane, depth):
    beyond = jnp.where(lane == depth - 1, 0.0, pltpu.roll(value, depth - 1, 1))
    return value + beyond, beyond - value


def waves_of(here, there):
    return tuple(a + b for a, b in zip(here, there)) + tuple(b - a for a, b in zip(here, there))


def modal(before, after, stiff, constants):
    shear, normal_off, normal_own, pair_off, pair_own, trio, last = constants
    u = [None] * 24
    for low in range(12):
        if low >= 3:
            u[low] = before[low] + after[low]
        u[12 + low] = after[low] - before[low]
    f = [None] * 24
    terms = []

    def take(degree, pull):
        terms.append(pull * u[degree])
        f[degree] = pull * stiff

    for first, second in SHEARS:
        both = u[first] + u[second]
        pull = shear * both
        terms.append(pull * both)
        f[first] = f[second] = pull * stiff
    common = normal_off * (u[5] + u[7] + u[12])
    for degree in NORMALS:
        take(degree, common + normal_own * u[degree])
    for first, second in PAIRS:
        common = pair_off * (u[first] + u[second])
        take(first, common + pair_own * u[first])
        take(second, common + pair_own * u[second])
    common = u[9] + u[16] + u[20]
    for degree in TRIO:
        take(degree, trio * (common + u[degree]))
    for degree in LASTS:
        take(degree, last * u[degree])
    while len(terms) > 1:
        terms = [sum(terms[k : k + 2][1:], terms[k]) for k in range(0, len(terms), 2)]
    return terms[0], f


def lower_of(f):
    return tuple(f[12 + k] * -1.0 if f[k] is None else f[k] - f[12 + k] for k in range(12))


def upper_of(f):
    return tuple(f[12 + k] if f[k] is None else f[k] + f[12 + k] for k in range(12))


def along_y(g):
    return tuple(g[k] - g[6 + k] for k in range(6)), tuple(g[k] + g[6 + k] for k in range(6))


def along_z(g, lane):
    return [
        (g[c] - g[3 + c]) + jnp.where(lane == 0, 0.0, pltpu.roll(g[c] + g[3 + c], 1, 1)) for c in range(3)
    ]


def class_of(row, rows):
    return jnp.where(row < RADIUS, row, jnp.where(row >= rows - RADIUS, row - (rows - 2 * RADIUS - 1), RADIUS))


def march(rows, block, waves, state, inverse, emit, put, own):
    constants = modal_constants()
    depth = waves.shape[-1]
    first = 8 * block
    zero = jnp.zeros((HALO, depth), jnp.float32)

    def nodes(row):
        return waves_of(
            [waves[k, row, first : first + 8, :] for k in range(6)],
            [waves[k, row, first + 1 : first + 9, :] for k in range(6)],
        )

    def step(row, carry):
        before, held, total, filled = carry
        after = nodes(row + 1)
        physical, stiff, factor = state(row)
        energy, f = modal(before, after, stiff, constants)
        put(row, factor * energy * inverse[class_of(row, rows), first : first + 8, :])
        if own:
            total = total + stiff * energy
            filled = filled + physical
        emit(row, *along_y(tuple(a + b for a, b in zip(held, lower_of(f)))))
        return after, upper_of(f), total, filled

    carry = (nodes(0), (zero,) * 12, zero, zero)
    carry = lax.fori_loop(0, rows - 2, step, carry, unroll=True)
    _, held, total, filled = step(rows - 2, carry)
    emit(rows - 1, *along_y(held))
    if own:
        filled = filled + state(rows - 1)[0]
    return total, filled


def own_state(dens, kind, cols, first):
    def state(row):
        at = pl.ds(pl.multiple_of(row * cols + first, 8), HALO)
        code = kind[at, :]
        physical = physical_of(dens[at, :], code)
        return physical, stiffness_of(physical), factor_of(physical, code)

    return state


def joiner(cols, block, tail_in, tail_out, applied, resid):
    first = 8 * block
    depth = resid.shape[-1]
    lane = lax.broadcasted_iota(jnp.int32, (HALO, depth), 1)
    sublane = lax.broadcasted_iota(jnp.int32, (HALO, depth), 0)

    def emit(row, low, high):
        parts = []
        for k in range(6):
            turned = pltpu.roll(high[k], 1, 0)
            if tail_out is not None:
                tail_out[k, row] = turned
            before = 0.0 if tail_in is None else tail_in[k, row]
            parts.append(low[k] + jnp.where(sublane == 0, before, turned))
        at = pl.ds(pl.multiple_of(row * cols + first, 8), HALO)
        for c, value in enumerate(along_z(parts, lane)):
            resid[c, at, :] = applied[c, at, :] - value

    return emit


def early_elements(
    rows, cols, disp, dens, kind, inverse, applied, waves, tail, resid, scaled, sums, *tails
):
    depth = disp.shape[-1]
    lane = lax.broadcasted_iota(jnp.int32, (HALO, depth), 1)

    def turn(row, nothing):
        for c in range(3):
            for block in range(cols // 8):
                at = pl.ds(pl.multiple_of((c * rows + row) * cols + 8 * block, 8), HALO)
                for r, value in enumerate(shifted_z(disp[at, :], lane, depth)):
                    waves[3 * r + c, row, 8 * block : 8 * block + 8, :] = value
                    if block == 0:
                        waves[3 * r + c, row, cols + HALO :, :] = value
        return nothing

    lax.fori_loop(0, rows, turn, 0, unroll=8)
    total = filled = jnp.zeros((HALO, depth), jnp.float32)
    chain = (None, *tails, tail)
    for block in range(cols // 8 - 1):
        first = 8 * block

        def put(row, value, first=first):
            scaled[row, first + 8 : first + 16, :] = value

        emit = joiner(cols, block, chain[block], chain[block + 1], applied, resid)
        state = own_state(dens, kind, cols, first)
        more = march(rows, block, waves, state, inverse, emit, put, True)
        total, filled = total + more[0], filled + more[1]
    sums[0] = total
    sums[1] = filled


def late_elements(
    rows, cols,
    waves_in, resid_in, scaled_in, tail, dens, kind, edge_u, edge_f, edge_s, applied, inverse, sums_a,
    waves, resid, scaled, sums, resid_out, near, filtered, far_h, lines, sems,
):
    depth = dens.shape[-1]
    del waves_in, resid_in, scaled_in
    wide = cols + HALO
    lane = lax.broadcasted_iota(jnp.int32, (HALO, depth), 1)

    def turn(row, nothing):
        for c in range(3):
            at = pl.ds(pl.multiple_of((c * rows + row) * HALO, 8), HALO)
            for r, value in enumerate(shifted_z(edge_u[at, :], lane, depth)):
                waves[3 * r + c, row, cols:wide, :] = value
        return nothing

    lax.fori_loop(0, rows, turn, 0, unroll=16)

    def edge_state(row):
        at = pl.ds(pl.multiple_of(row * HALO, 8), HALO)
        return None, edge_s[at, :], edge_f[at, :]

    def put_edge(row, value):
        scaled[row, :HALO, :] = value
        scaled[row, wide:, :] = value

    def emit_edge(row, low, high):
        for k in range(6):
            far_h[pl.ds(pl.multiple_of((k * rows + row) * HALO, 8), HALO), :] = high[k]

    last = cols // 8 - 1
    source = resid.reshape(3, rows, cols, depth)
    copies = []

    def send(block):
        at = (slice(None), pl.ds(1, rows - 2), pl.ds(8 * block, 8), slice(None))
        copies.append(pltpu.make_async_copy(source.at[at], resid_out.at[at], sems.at[block]))
        copies[-1].start()

    for block in range(1, last):
        send(block)
    march(rows, cols // 8, waves, edge_state, inverse, emit_edge, put_edge, False)
    parts = [far_h[pl.ds(k * rows * HALO + HALO - 1, rows, stride=HALO), :] for k in range(6)]
    at = pl.ds(0, rows, stride=cols)
    for c, value in enumerate(along_z(parts, lax.broadcasted_iota(jnp.int32, (rows, depth), 1))):
        resid[c, at, :] = resid[c, at, :] - value
    send(0)

    def put(row, value):
        scaled[row, cols:wide, :] = value

    emit = joiner(cols, last, tail, None, applied, resid)
    state = own_state(dens, kind, cols, 8 * last)
    total, filled = march(rows, last, waves, state, inverse, emit, put, True)
    send(last)
    sums[0] = sums_a[0] + total
    sums[1] = sums_a[1] + filled

    def own(row, nothing):
        lines_y(near, row + RADIUS, cols, lambda start: scaled[row, start : start + 8, :])
        return nothing

    lax.fori_loop(0, rows - 1, own, 0, unroll=True)
    band = bands(depth)
    inside = range(RADIUS + 1, rows - RADIUS - 1)
    for start in inside[:: FILTER_ROWS]:
        picks = range(start, min(start + FILTER_ROWS, inside.stop))
        rest = filter_rows(near, lines, filtered, picks, cols, band)
        filtered[picks.start : picks.stop] = filtered[picks.start : picks.stop] + rest
    for copy in copies:
        copy.wait()


def outer_elements(
    rows, cols, count_x, devices,
    waves, dens, kind, edge_f, edge_s, got_a, got_b, inner, scaled, sums, inverse,
    resid, final, out_a, out_b, parts, ring, stiff_low, carry_y,
):
    depth = dens.shape[-1]
    constants = modal_constants()
    wide = cols + HALO
    blocks = wide // HALO
    lane = lax.broadcasted_iota(jnp.int32, (HALO, depth), 1)
    here = lax.axis_index("gx")
    has_low = here > 0
    has_high = here < count_x - 1
    odd = here % 2

    def take(low, high):
        for block in range(blocks):
            first = 8 * block
            for c in range(3):
                for side, value in enumerate((low[c, first : first + 8, :], high[c, first : first + 8, :])):
                    if side:
                        value = jnp.where(has_high, value, 0.0)
                    for r, wave in enumerate(shifted_z(value, lane, depth)):
                        ring[side, 3 * r + c, first : first + 8, :] = wave
                        if block == 0:
                            ring[side, 3 * r + c, wide:, :] = wave
        stiff_low[...] = jnp.where(has_low, low[3], 0.0)

    @pl.when(odd == 0)
    def _():
        take(got_b, got_a)

    @pl.when(odd == 1)
    def _():
        take(got_a, got_b)

    total = sums[0]
    for block in (blocks - 1, *range(blocks - 1)):
        own = block < blocks - 1
        first = 8 * block

        def nodes(load):
            return waves_of(
                [load(k)[first : first + 8, :] for k in range(6)], [load(k)[first + 1 : first + 9, :] for k in range(6)]
            )

        line = [
            nodes(lambda k: ring.at[0, k]),
            nodes(lambda k: waves.at[k, 0]),
            nodes(lambda k: waves.at[k, rows - 1]),
            nodes(lambda k: ring.at[1, k]),
        ]
        _, f_low = modal(line[0], line[1], stiff_low[first : first + 8, :], constants)
        if own:
            _, stiff, factor = own_state(dens, kind, cols, first)(rows - 1)
        else:
            at = pl.ds((rows - 1) * HALO, HALO)
            stiff, factor = edge_s[at, :], edge_f[at, :]
        energy, f_high = modal(line[2], line[3], stiff, constants)
        value = factor * energy * inverse[2 * RADIUS, first : first + 8, :]
        if own:
            total = total + stiff * energy
            final[first + 8 : first + 16, :] = value
        else:
            final[:HALO, :] = value
            final[wide:, :] = value
        for index, (row, g) in enumerate(((0, upper_of(f_low)), (rows - 1, lower_of(f_high)))):
            low, high = along_y(g)
            if own:
                joined = []
                for k in range(6):
                    carry_y[index, k, first + 9 : first + 17, :] = high[k]
                    joined.append(low[k] + carry_y[index, k, first + 8 : first + 16, :])
                for c, value in enumerate(along_z(joined, lane)):
                    resid[index, c, first : first + 8, :] = inner[c, pl.ds(row * cols + first, HALO), :] - value
            else:
                for k in range(6):
                    carry_y[index, k, 1:9, :] = high[k]

    half = depth // 2
    pieces = []
    for value in (total, sums[1]):
        line = jnp.sum(value, axis=0, keepdims=True)
        pieces.append(line + pltpu.roll(line, half, 1))
    line = jnp.where(lax.broadcasted_iota(jnp.int32, (1, depth), 1) < half, pieces[0], pieces[1])
    parts[...] = jnp.broadcast_to(line, (devices, depth))

    def send(up, down):
        for index in range(RADIUS - 1):
            up[index] = scaled[rows - RADIUS + index, :wide, :]
        up[RADIUS - 1] = final[:wide, :]
        for index in range(RADIUS):
            down[index] = scaled[index, :wide, :]

    @pl.when(odd == 0)
    def _():
        send(out_a, out_b)

    @pl.when(odd == 1)
    def _():
        send(out_b, out_a)


def lines_y(near, row, cols, load):
    for block in range(cols // 8):
        start = HALO + 8 * block
        near[0, row, 8 * block : 8 * block + 8, :] = load(start)
        for shift in range(1, RADIUS + 1):
            near[shift, row, 8 * block : 8 * block + 8, :] = load(start + shift) + load(start - shift)


def filter_row(near, row, block, lane):
    depth = near.shape[-1]
    at = pl.ds(block * 8, 8)
    classes = {}
    for shift_x in range(RADIUS + 1):
        for shift_y in range(RADIUS + 1):
            square = shift_x * shift_x + shift_y * shift_y
            if square not in CLASSES:
                continue
            value = near[shift_y, row + (RADIUS + shift_x), at, :]
            if shift_x:
                value = value + near[shift_y, row + (RADIUS - shift_x), at, :]
            classes[square] = value if square not in classes else classes[square] + value
    result = None
    for shift_z in range(RADIUS + 1):
        line = None
        for square, value in classes.items():
            weight = weight_of(square + shift_z * shift_z)
            if weight > 0.0:
                line = weight * value if line is None else line + weight * value
        if shift_z:
            up = jnp.where(lane < shift_z, 0.0, pltpu.roll(line, shift_z, 1))
            down = jnp.where(lane >= depth - shift_z, 0.0, pltpu.roll(line, depth - shift_z, 1))
            line = up + down
        result = line if result is None else result + line
    return result


def bands(depth):
    row = lax.broadcasted_iota(jnp.int32, (depth, depth), 0)
    column = lax.broadcasted_iota(jnp.int32, (depth, depth), 1)
    away = jnp.abs(row - column)
    return jnp.concatenate(
        [jnp.where(away == shift, 1.0, 0.0).astype(jnp.bfloat16) for shift in range(1, RADIUS + 1)], axis=0
    )


def filter_rows(near, lines, result, picks, cols, band):
    depth = near.shape[-1]
    for rank, row in enumerate(picks):
        for block in range(cols // 8):
            at = pl.ds(block * 8, 8)
            classes = {}
            for shift_x in range(RADIUS + 1):
                for shift_y in range(RADIUS + 1):
                    square = shift_x * shift_x + shift_y * shift_y
                    if square not in CLASSES:
                        continue
                    value = near[shift_y, row + (RADIUS + shift_x), at, :]
                    if shift_x:
                        value = value + near[shift_y, row + (RADIUS - shift_x), at, :]
                    classes[square] = value if square not in classes else classes[square] + value
            for shift_z in range(RADIUS + 1):
                line = None
                for square, value in classes.items():
                    weight = weight_of(square + shift_z * shift_z)
                    if weight > 0.0:
                        line = weight * value if line is None else line + weight * value
                if shift_z:
                    first = rank * cols + 8 * block
                    lines[first : first + 8, (shift_z - 1) * depth : shift_z * depth] = line
                else:
                    result[row, at, :] = line
    value = lines[: len(picks) * cols, :]
    coarse = value.astype(jnp.bfloat16)
    rest = (value - coarse.astype(jnp.float32)).astype(jnp.bfloat16)
    total = jnp.dot(coarse, band, preferred_element_type=jnp.float32)
    total = total + jnp.dot(rest, band, preferred_element_type=jnp.float32)
    return total.reshape(len(picks), cols, depth)


def filter_rest(
    rows, cols, count_x, cells,
    near_in, inner, final, got_a, got_b, parts, outer, resid_in,
    sens, resid, comp, vol, near, ends, result_v, sems,
):
    depth = sens.shape[-1]
    del near_in, resid_in
    wide = cols + HALO
    copies = [
        pltpu.make_async_copy(outer.at[index], resid.at[:, row], sems.at[index])
        for index, row in enumerate((0, rows - 1))
    ]
    for copy in copies:
        copy.start()
    here = lax.axis_index("gx")
    has_low = here > 0
    has_high = here < count_x - 1
    odd = here % 2
    half = depth // 2
    line = jnp.sum(parts[...], axis=0, keepdims=True)
    first = lax.broadcasted_iota(jnp.int32, (1, depth), 1) < half
    compliance = jnp.sum(jnp.where(first, line, 0.0))
    volume = jnp.sum(jnp.where(first, 0.0, line))
    comp[0, 0] = compliance
    vol[0, 0] = volume / cells
    scale = cells / jnp.broadcast_to(compliance, (8, depth))

    def send(start, size):
        at = pl.ds(start, size)
        copies.append(pltpu.make_async_copy(result_v.at[at], sens.at[at], sems.at[len(copies)]))
        copies[-1].start()

    low_end, high_start = RADIUS + 1, rows - RADIUS - 1
    for row in range(low_end, high_start):
        for block in range(cols // 8):
            at = pl.ds(block * 8, 8)
            result_v[row, at, :] = inner[row, at, :] * scale
    send(low_end, high_start - low_end)

    def take(low, high):
        for index in range(RADIUS):
            for source, has, at in ((low, has_low, index), (high, has_high, RADIUS + index)):
                value = jnp.where(has, source[index], 0.0)
                ends[at, :wide, :] = value
                ends[at, wide:, :] = value[:HALO]

    @pl.when(odd == 0)
    def _():
        take(got_b, got_a)

    @pl.when(odd == 1)
    def _():
        take(got_a, got_b)

    for index in range(RADIUS):
        lines_y(near, index, cols, lambda start, at=index: ends[at, start : start + 8, :])
        lines_y(near, rows + RADIUS + index, cols, lambda start, at=RADIUS + index: ends[at, start : start + 8, :])
    lines_y(near, rows + RADIUS - 1, cols, lambda start: final[start : start + 8, :])
    lane = lax.broadcasted_iota(jnp.int32, (8, depth), 1)
    for start, stop in ((0, low_end), (high_start, rows)):
        for row in range(start, stop):
            for block in range(cols // 8):
                result_v[row, 8 * block : 8 * block + 8, :] = filter_row(near, row, block, lane) * scale
        send(start, stop - start)
    for copy in copies:
        copy.wait()


def call(body, shapes, inputs, scratch=(), places=None, out_places=None, flops=0, limit=24, aliases=None):
    places, out_places = places or {}, out_places or {}
    in_specs = [pl.BlockSpec(memory_space=places.get(rank, pltpu.VMEM)) for rank in range(len(inputs))]
    out_specs = [pl.BlockSpec(memory_space=out_places.get(rank, pltpu.VMEM)) for rank in range(len(shapes))]
    moved = sum(int(np.prod(v.shape)) * 4 for v in list(inputs) + list(shapes))
    return pl.pallas_call(
        body,
        out_shape=[FULL(v.shape, v.dtype) for v in shapes],
        in_specs=in_specs,
        out_specs=out_specs,
        scratch_shapes=list(scratch),
        input_output_aliases=aliases or {},
        cost_estimate=pl.CostEstimate(flops=flops, bytes_accessed=moved, transcendentals=0),
        compiler_params=pltpu.CompilerParams(vmem_limit_bytes=int(limit * 1024 * 1024)),
    )(*inputs)


def f32(*shape):
    return FULL(shape, jnp.float32)


def vmem(*shape, dtype=jnp.float32):
    return pltpu.VMEM(shape, dtype)


def on_device(count_x, count_y, displacement, density, element_kind, load_x, load_y, load_z, load_force):
    rows, cols, depth = density.shape
    wide = cols + HALO
    devices = count_x * count_y
    cells = float(rows * cols * depth * devices)

    pairs_ya = [(k, k ^ 1) for k in range(count_y)]
    pairs_xa = [(k, k ^ 1) for k in range(count_x)]
    pairs_yb, pairs_xb = [], []
    for i in range(count_x):
        for j in range(count_y):
            here = i * count_y + j
            inside_y, inside_x = 0 < j < count_y - 1, 0 < i < count_x - 1
            pairs_yb.append((here, i * count_y + ((j + 1) ^ 1) - 1 if inside_y else (i ^ 1) * count_y + j))
            pairs_xb.append((here, (((i + 1) ^ 1) - 1) * count_y + j if inside_x else i * count_y + (j ^ 1)))

    disp = displacement.reshape(3 * rows * cols, depth)
    dens = density.reshape(rows * cols, depth)
    kind = element_kind.reshape(rows * cols, depth)

    slots = 4 * RADIUS + RADIUS
    send_a, send_b, mark = call(
        functools.partial(pack_y, rows, cols),
        [f32(slots * rows, depth)] * 2 + [f32(8, depth)],
        [displacement, density, element_kind],
        scratch=[
            vmem(3, rows, HALO, depth),
            vmem(rows, HALO, depth),
            vmem(rows, HALO, depth, dtype=jnp.int32),
            pltpu.SemaphoreType.DMA((6,)),
        ],
        places={0: pltpu.HBM, 1: pltpu.HBM, 2: pltpu.HBM},
        limit=53.25,
    )
    got_b = lax.ppermute(send_b, BOTH, pairs_yb)
    got_a = lax.ppermute(send_a, "gy", pairs_ya)

    sums = np.zeros((8, depth), np.float32)
    for rank, square in enumerate(CLASSES):
        for z in range(depth):
            sums[rank, z] = sum(
                weight_of(square + s * s) for s in range(-RADIUS, RADIUS + 1) if 0 <= z + s < depth
            )
    count = load_x.shape[0]
    applied, inverse = call(
        functools.partial(loads_and_weights, rows, cols, count_x, count_y),
        [f32(3, rows * cols, depth), f32(2 * RADIUS + 1, wide, depth)],
        [mark, load_x.reshape(1, count), load_y.reshape(1, count), load_z.reshape(1, count), load_force, jnp.asarray(sums)],
        places={0: pl.ANY},
        flops=2 * rows * cols * count * 6 * depth,
    )

    early = cols - HALO
    waves, tail, inner, scaled, sums = call(
        functools.partial(early_elements, rows, cols),
        [
            f32(6, rows, wide + HALO, depth),
            f32(6, rows, HALO, depth),
            f32(3, rows * cols, depth),
            f32(rows, wide + HALO, depth),
            f32(2, 8, depth),
        ],
        [disp, dens, kind, inverse, applied],
        scratch=[vmem(6, rows, HALO, depth)] * (cols // HALO - 2),
        flops=250 * rows * early * depth,
    )

    edge_u, edge_f, edge_s, send_a, send_b = call(
        functools.partial(unpack_y, rows, cols, count_y),
        [f32(3 * rows * HALO, depth), f32(rows * HALO, depth), f32(rows * HALO, depth)] + [f32(4, wide, depth)] * 2,
        [sums, disp, dens, kind, got_a, got_b],
        places={0: pl.ANY},
    )
    got_b = lax.ppermute(send_b, BOTH, pairs_xb)
    got_a = lax.ppermute(send_a, "gx", pairs_xa)

    waves, inner, scaled, sums, resid, near, filtered = call(
        functools.partial(late_elements, rows, cols),
        [f32(*v.shape) for v in (waves, inner, scaled, sums)]
        + [f32(3, rows, cols, depth), f32(RADIUS + 1, rows + 2 * RADIUS, cols, depth), f32(rows, cols, depth)],
        [waves, inner, scaled, tail, dens, kind, edge_u, edge_f, edge_s, applied, inverse, sums],
        scratch=[
            vmem(6 * rows * HALO, depth),
            vmem(FILTER_ROWS * cols, RADIUS * depth),
            pltpu.SemaphoreType.DMA((cols // HALO,)),
        ],
        out_places={4: pltpu.HBM},
        flops=250 * rows * 2 * HALO * depth,
        aliases={0: 0, 1: 1, 2: 2},
    )
    outer, final, send_a, send_b, parts = call(
        functools.partial(outer_elements, rows, cols, count_x, devices),
        [f32(2, 3, cols, depth), f32(wide + HALO, depth)] + [f32(RADIUS, wide, depth)] * 2 + [f32(devices, depth)],
        [waves, dens, kind, edge_f, edge_s, got_a, got_b, inner, scaled, sums, inverse],
        scratch=[vmem(2, 6, wide + HALO, depth), vmem(wide, depth), vmem(2, 6, wide + 2 * HALO, depth)],
        flops=500 * wide * depth,
    )
    got_b = lax.ppermute(send_b, BOTH, pairs_xb)
    got_a = lax.ppermute(send_a, "gx", pairs_xa)
    parts = lax.all_to_all(parts, BOTH, 0, 0, tiled=True)

    sens, resid, comp, volume, _ = call(
        functools.partial(filter_rest, rows, cols, count_x, cells),
        [f32(rows, cols, depth), f32(3, rows, cols, depth), f32(1, 1), f32(1, 1), f32(*near.shape)],
        [near, filtered, final, got_a, got_b, parts, outer, resid],
        scratch=[
            vmem(2 * RADIUS, wide + HALO, depth),
            vmem(rows, cols, depth),
            pltpu.SemaphoreType.DMA((5,)),
        ],
        places={7: pltpu.HBM},
        out_places={0: pltpu.HBM, 1: pltpu.HBM, 2: pltpu.SMEM, 3: pltpu.SMEM},
        flops=20 * rows * cols * depth,
        aliases={0: 4, 7: 1},
    )
    return (
        sens,
        resid,
        comp.reshape(()),
        volume.reshape(()),
    )


def solution(mesh):
    placed = (
        P(None, "gx", "gy", None),
        P("gx", "gy", None),
        P("gx", "gy", None),
        P(),
        P(),
        P(),
        P(),
    )
    return jax.shard_map(
        functools.partial(on_device, mesh.shape["gx"], mesh.shape["gy"]),
        mesh=mesh,
        in_specs=placed,
        out_specs=(P("gx", "gy", None), P(None, "gx", "gy", None), P(), P()),
        check_vma=False,
    )
```

```python
import functools

import jax
import jax.numpy as jnp
import numpy as np
from jax import lax
from jax.experimental import pallas as pl
from jax.experimental.pallas import tpu as pltpu
from jax.sharding import PartitionSpec as P

RADIUS = 3
PENALTY = 3.0
STIFF_FLOOR = 0.001
POISSON = 0.3
HALO = 8
BOTH = ("gx", "gy")
FULL = jax.ShapeDtypeStruct
FILTER_ROWS = 12


def element_matrix():
    lame_first = POISSON / ((1.0 + POISSON) * (1.0 - 2.0 * POISSON))
    shear_modulus = 0.5 / (1.0 + POISSON)
    material = np.zeros((6, 6))
    material[:3, :3] = lame_first
    for diagonal in range(3):
        material[diagonal, diagonal] += 2.0 * shear_modulus
        material[diagonal + 3, diagonal + 3] = shear_modulus
    points = [0.5 - 0.5 / np.sqrt(3.0), 0.5 + 0.5 / np.sqrt(3.0)]
    corners = [(a, b, e) for a in (0, 1) for b in (0, 1) for e in (0, 1)]
    result = np.zeros((24, 24))
    for point_x in points:
        for point_y in points:
            for point_z in points:
                strain = np.zeros((6, 24))
                for corner, (side_x, side_y, side_z) in enumerate(corners):
                    value_x = point_x if side_x else 1.0 - point_x
                    value_y = point_y if side_y else 1.0 - point_y
                    value_z = point_z if side_z else 1.0 - point_z
                    slope_x = (1.0 if side_x else -1.0) * value_y * value_z
                    slope_y = value_x * (1.0 if side_y else -1.0) * value_z
                    slope_z = value_x * value_y * (1.0 if side_z else -1.0)
                    column = 3 * corner
                    strain[0, column] = slope_x
                    strain[1, column + 1] = slope_y
                    strain[2, column + 2] = slope_z
                    strain[3, column] = slope_y
                    strain[3, column + 1] = slope_x
                    strain[4, column + 1] = slope_z
                    strain[4, column + 2] = slope_y
                    strain[5, column + 2] = slope_x
                    strain[5, column] = slope_z
                result += strain.T @ material @ strain / 8.0
    return result


def modal_matrix():
    pair = np.array([[1.0, 1.0], [-1.0, 1.0]])
    turn = np.kron(np.kron(np.kron(pair, pair), pair), np.eye(3))
    return turn @ element_matrix() @ turn.T / 64.0


SHEARS = ((3, 14), (4, 8), (6, 13))
NORMALS = (5, 7, 12)
PAIRS = ((10, 15), (11, 18), (17, 19))
TRIO = (9, 16, 20)
LASTS = (21, 22, 23)


def modal_constants():
    modal = modal_matrix()
    known = np.zeros((24, 24))
    shear = modal[3, 3]
    for first, second in SHEARS:
        known[np.ix_((first, second), (first, second))] = shear
    normal_off = modal[5, 7]
    normal_own = modal[5, 5] - normal_off
    known[np.ix_(NORMALS, NORMALS)] = normal_off
    pair_off = modal[10, 15]
    pair_own = modal[10, 10] - pair_off
    for both in PAIRS:
        known[np.ix_(both, both)] = pair_off
    trio = modal[9, 16]
    known[np.ix_(TRIO, TRIO)] = trio
    last = modal[21, 21]
    for group, own in ((NORMALS, normal_own), (sum(PAIRS, ()), pair_own), (TRIO, trio), (LASTS, last)):
        for degree in group:
            known[degree, degree] += own
    assert np.abs(known - modal).max() < 1e-12
    return tuple(float(v) for v in (shear, normal_off, normal_own, pair_off, pair_own, trio, last))


def weight_of(square):
    return max(0.0, RADIUS + 0.5 - float(np.sqrt(square)))


CLASSES = (0, 1, 2, 4, 5, 8, 9, 10)


def stiffness_of(physical):
    return STIFF_FLOOR + (1.0 - STIFF_FLOOR) * (physical * physical * physical)


def physical_of(density, kind):
    return jnp.where(kind == 1, 0.0, jnp.where(kind == 2, 1.0, density))


def factor_of(physical, kind):
    design = (kind != 1) & (kind != 2)
    return jnp.where(design, (-PENALTY * (1.0 - STIFF_FLOOR)) * (physical * physical), 0.0)


def pack_y(rows, cols, disp, dens, kind, out_a, out_b, mark, edge_d, edge_p, edge_k, sems):
    half = HALO // 2
    copies = []
    for side, start in ((0, 0), (half, cols - half)):
        for source, target in ((disp, edge_d), (dens, edge_p), (kind, edge_k)):
            lead = (slice(None),) * (len(source.shape) - 2)
            copies.append(
                pltpu.make_async_copy(
                    source.at[(*lead, pl.ds(start, half), slice(None))],
                    target.at[(*lead, pl.ds(side, half), slice(None))],
                    sems.at[len(copies)],
                )
            )
    for copy in copies:
        copy.start()
    for copy in copies:
        copy.wait()
    depth = disp.shape[-1]
    flat_d = edge_d.reshape(3 * rows * HALO, depth)
    flat_p = edge_p.reshape(rows * HALO, depth)
    flat_k = edge_k.reshape(rows * HALO, depth)

    def state(index):
        code = flat_k[pl.ds(index, rows, stride=HALO), :]
        return physical_of(flat_p[pl.ds(index, rows, stride=HALO), :], code), code

    def fill(low, high):
        slot = 0
        for c in range(3):
            for index in range(RADIUS + 1):
                low[pl.ds(slot * rows, rows), :] = flat_d[pl.ds(c * rows * HALO + index, rows, stride=HALO), :]
                slot += 1
        for index in range(RADIUS):
            low[pl.ds(slot * rows, rows), :] = factor_of(*state(index))
            slot += 1
        slot = 0
        for c in range(3):
            for index in range(HALO - RADIUS, HALO):
                high[pl.ds(slot * rows, rows), :] = flat_d[pl.ds(c * rows * HALO + index, rows, stride=HALO), :]
                slot += 1
        for index in range(HALO - RADIUS, HALO):
            physical, code = state(index)
            high[pl.ds(slot * rows, rows), :] = factor_of(physical, code)
            slot += 1
        high[pl.ds(slot * rows, rows), :] = stiffness_of(physical)

    mark[...] = jnp.zeros_like(mark)
    odd = lax.axis_index("gy") % 2

    @pl.when(odd == 0)
    def _():
        fill(out_b, out_a)

    @pl.when(odd == 1)
    def _():
        fill(out_a, out_b)


def unpack_y(rows, cols, count_y, after, disp, dens, kind, got_a, got_b, edge_u, edge_f, edge_s, out_a, out_b):
    del after
    here = lax.axis_index("gy")
    depth = disp.shape[-1]
    has_low = here > 0
    has_high = here < count_y - 1

    def fill(low, high):
        def put(ref, start, sublane, value):
            ref[pl.ds(start + sublane, rows, stride=HALO), :] = value

        zero = jnp.zeros((rows, depth), jnp.float32)
        slot = 0
        for c in range(3):
            for index in range(RADIUS + 1):
                put(edge_u, c * rows * HALO, index, jnp.where(has_high, high[pl.ds(slot * rows, rows), :], 0.0))
                slot += 1
        for index in range(RADIUS):
            put(edge_f, 0, index, jnp.where(has_high, high[pl.ds(slot * rows, rows), :], 0.0))
            slot += 1
        slot = 0
        for c in range(3):
            put(edge_u, c * rows * HALO, RADIUS + 1, zero)
            for index in range(HALO - RADIUS, HALO):
                put(edge_u, c * rows * HALO, index, low[pl.ds(slot * rows, rows), :])
                slot += 1
        for index in range(RADIUS, HALO - RADIUS):
            put(edge_f, 0, index, zero)
        for index in range(HALO - RADIUS, HALO):
            put(edge_f, 0, index, jnp.where(has_low, low[pl.ds(slot * rows, rows), :], 0.0))
            slot += 1
        edge_s[...] = jnp.zeros_like(edge_s)
        put(edge_s, 0, HALO - 1, jnp.where(has_low, low[pl.ds(slot * rows, rows), :], 0.0))

    odd = here % 2

    @pl.when(odd == 0)
    def _():
        fill(got_b, got_a)

    @pl.when(odd == 1)
    def _():
        fill(got_a, got_b)

    def send(out, row, with_stiff):
        for c in range(3):
            out[c, :cols, :] = disp[pl.ds((c * rows + row) * cols, cols), :]
            out[c, cols:, :] = edge_u[pl.ds((c * rows + row) * HALO, HALO), :]
        if with_stiff:
            at = pl.ds(row * cols, cols)
            out[3, :cols, :] = stiffness_of(physical_of(dens[at, :], kind[at, :]))
            out[3, cols:, :] = edge_s[pl.ds(row * HALO, HALO), :]
        else:
            out[3] = jnp.zeros_like(out[3])

    odd_x = lax.axis_index("gx") % 2

    @pl.when(odd_x == 0)
    def _():
        send(out_a, rows - 1, True)
        send(out_b, 0, False)

    @pl.when(odd_x == 1)
    def _():
        send(out_a, 0, False)
        send(out_b, rows - 1, True)


def loads_and_weights(rows, cols, count_x, count_y, after, load_x, load_y, load_z, force, sums, applied, inverse):
    del after
    depth = applied.shape[-1]
    place_x = lax.axis_index("gx") * rows
    place_y = lax.axis_index("gy") * cols
    local_x = load_x[...] - place_x
    local_y = load_y[...] - place_y
    owned = (local_x >= 0) & (local_x < rows) & (local_y >= 0) & (local_y < cols)
    target = jnp.where(owned, local_x * cols + local_y, -1)
    loads = target.shape[1]
    lanes = lax.broadcasted_iota(jnp.int32, (depth, loads), 0)
    hit_z = lanes == load_z[...]
    right = [[], []]
    for c in range(3):
        value = force[c : c + 1, :]
        coarse = value.astype(jnp.bfloat16).astype(jnp.float32)
        for part, piece in zip(right, (coarse, value - coarse)):
            part.append(jnp.where(hit_z, piece, 0.0).astype(jnp.bfloat16))
    place = lax.broadcasted_iota(jnp.int32, (rows * cols, loads), 0)
    left = jnp.where(place == target, 1.0, 0.0).astype(jnp.bfloat16)
    product = lax.dot_general(
        left, jnp.concatenate(right[0] + right[1], axis=0), (((1,), (1,)), ((), ())), preferred_element_type=jnp.float32
    )
    for c in range(3):
        applied[c] = product[:, c * depth : (c + 1) * depth] + product[:, (3 + c) * depth : (4 + c) * depth]

    wide = cols + HALO
    total_x, total_y = rows * count_x, cols * count_y
    sublane = lax.broadcasted_iota(jnp.int32, (wide, depth), 0)
    node_y = jnp.where(sublane >= wide - RADIUS, sublane - wide, sublane) + place_y
    inside_y = {
        shift: ((node_y + shift >= 0) & (node_y + shift < total_y)).astype(jnp.float32)
        for shift in range(-RADIUS, RADIUS + 1)
    }
    for kind in range(2 * RADIUS + 1):
        row = kind if kind <= RADIUS else rows - 2 * RADIUS - 1 + kind
        result = jnp.zeros((wide, depth), jnp.float32)
        for shift_y in range(-RADIUS, RADIUS + 1):
            line = jnp.zeros((1, depth), jnp.float32)
            for shift_x in range(-RADIUS, RADIUS + 1):
                square = shift_x * shift_x + shift_y * shift_y
                if square in CLASSES:
                    at = place_x + (row + shift_x)
                    inside = ((at >= 0) & (at < total_x)).astype(jnp.float32)
                    rank = CLASSES.index(square)
                    line = line + inside * sums[rank : rank + 1, :]
            result = result + inside_y[shift_y] * line
        inverse[kind] = 1.0 / jnp.where(result > 0.0, result, 1.0)


def shifted_z(value, lane, depth):
    beyond = jnp.where(lane == depth - 1, 0.0, pltpu.roll(value, depth - 1, 1))
    return value + beyond, beyond - value


def waves_of(here, there):
    return tuple(a + b for a, b in zip(here, there)) + tuple(b - a for a, b in zip(here, there))


def modal(before, after, stiff, constants):
    shear, normal_off, normal_own, pair_off, pair_own, trio, last = constants
    u = [None] * 24
    for low in range(12):
        if low >= 3:
            u[low] = before[low] + after[low]
        u[12 + low] = after[low] - before[low]
    f = [None] * 24
    terms = []

    def take(degree, pull):
        terms.append(pull * u[degree])
        f[degree] = pull * stiff

    for first, second in SHEARS:
        both = u[first] + u[second]
        pull = shear * both
        terms.append(pull * both)
        f[first] = f[second] = pull * stiff
    common = normal_off * (u[5] + u[7] + u[12])
    for degree in NORMALS:
        take(degree, common + normal_own * u[degree])
    for first, second in PAIRS:
        common = pair_off * (u[first] + u[second])
        take(first, common + pair_own * u[first])
        take(second, common + pair_own * u[second])
    common = u[9] + u[16] + u[20]
    for degree in TRIO:
        take(degree, trio * (common + u[degree]))
    for degree in LASTS:
        take(degree, last * u[degree])
    while len(terms) > 1:
        terms = [sum(terms[k : k + 2][1:], terms[k]) for k in range(0, len(terms), 2)]
    return terms[0], f


def lower_of(f):
    return tuple(f[12 + k] * -1.0 if f[k] is None else f[k] - f[12 + k] for k in range(12))


def upper_of(f):
    return tuple(f[12 + k] if f[k] is None else f[k] + f[12 + k] for k in range(12))


def along_y(g):
    return tuple(g[k] - g[6 + k] for k in range(6)), tuple(g[k] + g[6 + k] for k in range(6))


def along_z(g, lane):
    return [
        (g[c] - g[3 + c]) + jnp.where(lane == 0, 0.0, pltpu.roll(g[c] + g[3 + c], 1, 1)) for c in range(3)
    ]


def class_of(row, rows):
    return jnp.where(row < RADIUS, row, jnp.where(row >= rows - RADIUS, row - (rows - 2 * RADIUS - 1), RADIUS))


def march(rows, block, waves, state, inverse, emit, put, own):
    constants = modal_constants()
    depth = waves.shape[-1]
    first = 8 * block
    zero = jnp.zeros((HALO, depth), jnp.float32)

    def nodes(row):
        return waves_of(
            [waves[k, row, first : first + 8, :] for k in range(6)],
            [waves[k, row, first + 1 : first + 9, :] for k in range(6)],
        )

    def step(row, carry):
        before, held, total, filled = carry
        after = nodes(row + 1)
        physical, stiff, factor = state(row)
        energy, f = modal(before, after, stiff, constants)
        put(row, factor * energy * inverse[class_of(row, rows), first : first + 8, :])
        if own:
            total = total + stiff * energy
            filled = filled + physical
        emit(row, *along_y(tuple(a + b for a, b in zip(held, lower_of(f)))))
        return after, upper_of(f), total, filled

    carry = (nodes(0), (zero,) * 12, zero, zero)
    carry = lax.fori_loop(0, rows - 2, step, carry, unroll=True)
    _, held, total, filled = step(rows - 2, carry)
    emit(rows - 1, *along_y(held))
    if own:
        filled = filled + state(rows - 1)[0]
    return total, filled


def own_state(dens, kind, cols, first):
    def state(row):
        at = pl.ds(pl.multiple_of(row * cols + first, 8), HALO)
        code = kind[at, :]
        physical = physical_of(dens[at, :], code)
        return physical, stiffness_of(physical), factor_of(physical, code)

    return state


def joiner(cols, block, tail_in, tail_out, applied, resid):
    first = 8 * block
    depth = resid.shape[-1]
    lane = lax.broadcasted_iota(jnp.int32, (HALO, depth), 1)
    sublane = lax.broadcasted_iota(jnp.int32, (HALO, depth), 0)

    def emit(row, low, high):
        parts = []
        for k in range(6):
            turned = pltpu.roll(high[k], 1, 0)
            if tail_out is not None:
                tail_out[k, row] = turned
            before = 0.0 if tail_in is None else tail_in[k, row]
            parts.append(low[k] + jnp.where(sublane == 0, before, turned))
        at = pl.ds(pl.multiple_of(row * cols + first, 8), HALO)
        for c, value in enumerate(along_z(parts, lane)):
            resid[c, at, :] = applied[c, at, :] - value

    return emit


def early_elements(
    rows, cols, disp, dens, kind, inverse, applied, waves, tail, resid, scaled, sums, *tails
):
    depth = disp.shape[-1]
    lane = lax.broadcasted_iota(jnp.int32, (HALO, depth), 1)

    def turn(row, nothing):
        for c in range(3):
            for block in range(cols // 8):
                at = pl.ds(pl.multiple_of((c * rows + row) * cols + 8 * block, 8), HALO)
                for r, value in enumerate(shifted_z(disp[at, :], lane, depth)):
                    waves[3 * r + c, row, 8 * block : 8 * block + 8, :] = value
                    if block == 0:
                        waves[3 * r + c, row, cols + HALO :, :] = value
        return nothing

    lax.fori_loop(0, rows, turn, 0, unroll=8)
    total = filled = jnp.zeros((HALO, depth), jnp.float32)
    chain = (None, *tails, tail)
    for block in range(cols // 8 - 1):
        first = 8 * block

        def put(row, value, first=first):
            scaled[row, first + 8 : first + 16, :] = value

        emit = joiner(cols, block, chain[block], chain[block + 1], applied, resid)
        state = own_state(dens, kind, cols, first)
        more = march(rows, block, waves, state, inverse, emit, put, True)
        total, filled = total + more[0], filled + more[1]
    sums[0] = total
    sums[1] = filled


def late_elements(
    rows, cols,
    waves_in, resid_in, scaled_in, tail, dens, kind, edge_u, edge_f, edge_s, applied, inverse, sums_a,
    waves, resid, scaled, sums, resid_out, near, filtered, out_a, out_b, far_h, lines, sems,
):
    depth = dens.shape[-1]
    del waves_in, resid_in, scaled_in
    wide = cols + HALO
    lane = lax.broadcasted_iota(jnp.int32, (HALO, depth), 1)

    def turn(row, nothing):
        for c in range(3):
            at = pl.ds(pl.multiple_of((c * rows + row) * HALO, 8), HALO)
            for r, value in enumerate(shifted_z(edge_u[at, :], lane, depth)):
                waves[3 * r + c, row, cols:wide, :] = value
        return nothing

    lax.fori_loop(0, rows, turn, 0, unroll=16)

    def edge_state(row):
        at = pl.ds(pl.multiple_of(row * HALO, 8), HALO)
        return None, edge_s[at, :], edge_f[at, :]

    def put_edge(row, value):
        scaled[row, :HALO, :] = value
        scaled[row, wide:, :] = value

    def emit_edge(row, low, high):
        for k in range(6):
            far_h[pl.ds(pl.multiple_of((k * rows + row) * HALO, 8), HALO), :] = high[k]

    last = cols // 8 - 1
    source = resid.reshape(3, rows, cols, depth)
    copies = []

    def send(block):
        at = (slice(None), pl.ds(1, rows - 2), pl.ds(8 * block, 8), slice(None))
        copies.append(pltpu.make_async_copy(source.at[at], resid_out.at[at], sems.at[block]))
        copies[-1].start()

    for block in range(1, last):
        send(block)
    march(rows, cols // 8, waves, edge_state, inverse, emit_edge, put_edge, False)
    parts = [far_h[pl.ds(k * rows * HALO + HALO - 1, rows, stride=HALO), :] for k in range(6)]
    at = pl.ds(0, rows, stride=cols)
    for c, value in enumerate(along_z(parts, lax.broadcasted_iota(jnp.int32, (rows, depth), 1))):
        resid[c, at, :] = resid[c, at, :] - value
    send(0)

    def put(row, value):
        scaled[row, cols:wide, :] = value

    emit = joiner(cols, last, tail, None, applied, resid)
    state = own_state(dens, kind, cols, 8 * last)
    total, filled = march(rows, last, waves, state, inverse, emit, put, True)
    send(last)
    sums[0] = sums_a[0] + total
    sums[1] = sums_a[1] + filled

    def out(up, down):
        for index in range(RADIUS - 1):
            up[index] = scaled[rows - RADIUS + index, :wide, :]
        at = pl.ds((rows - 1) * cols, cols)
        code = kind[at, :]
        up[RADIUS - 1, HALO:, :] = factor_of(physical_of(dens[at, :], code), code)
        up[RADIUS - 1, :HALO, :] = edge_f[pl.ds((rows - 1) * HALO, HALO), :]
        for index in range(RADIUS):
            down[index] = scaled[index, :wide, :]

    odd = lax.axis_index("gx") % 2

    @pl.when(odd == 0)
    def _():
        out(out_a, out_b)

    @pl.when(odd == 1)
    def _():
        out(out_b, out_a)

    def own(row, nothing):
        lines_y(near, row + RADIUS, cols, lambda start: scaled[row, start : start + 8, :])
        return nothing

    lax.fori_loop(0, rows - 1, own, 0, unroll=True)
    band = bands(depth)
    inside = range(RADIUS + 1, rows - RADIUS - 1)
    for start in inside[:: FILTER_ROWS]:
        picks = range(start, min(start + FILTER_ROWS, inside.stop))
        rest = filter_rows(near, lines, filtered, picks, cols, band)
        filtered[picks.start : picks.stop] = filtered[picks.start : picks.stop] + rest
    for copy in copies:
        copy.wait()


def outer_elements(
    rows, cols, count_x, devices,
    waves, dens, kind, edge_f, edge_s, got_a, got_b, inner, sums, inverse,
    resid, final, before, parts, ring, stiff_low, carry_y,
):
    depth = dens.shape[-1]
    constants = modal_constants()
    wide = cols + HALO
    blocks = wide // HALO
    lane = lax.broadcasted_iota(jnp.int32, (HALO, depth), 1)
    here = lax.axis_index("gx")
    has_low = here > 0
    has_high = here < count_x - 1
    odd = here % 2

    def take(low, high):
        for block in range(blocks):
            first = 8 * block
            for c in range(3):
                for side, value in enumerate((low[c, first : first + 8, :], high[c, first : first + 8, :])):
                    if side:
                        value = jnp.where(has_high, value, 0.0)
                    for r, wave in enumerate(shifted_z(value, lane, depth)):
                        ring[side, 3 * r + c, first : first + 8, :] = wave
                        if block == 0:
                            ring[side, 3 * r + c, wide:, :] = wave
        stiff_low[...] = jnp.where(has_low, low[3], 0.0)

    @pl.when(odd == 0)
    def _():
        take(got_b, got_a)

    @pl.when(odd == 1)
    def _():
        take(got_a, got_b)

    total = sums[0]
    for block in (blocks - 1, *range(blocks - 1)):
        own = block < blocks - 1
        first = 8 * block

        def nodes(load):
            return waves_of(
                [load(k)[first : first + 8, :] for k in range(6)], [load(k)[first + 1 : first + 9, :] for k in range(6)]
            )

        line = [
            nodes(lambda k: ring.at[0, k]),
            nodes(lambda k: waves.at[k, 0]),
            nodes(lambda k: waves.at[k, rows - 1]),
            nodes(lambda k: ring.at[1, k]),
        ]
        energy, f_low = modal(line[0], line[1], stiff_low[first : first + 8, :], constants)
        place = first + 8 if own else 0
        before[place : place + 8, :] = energy * inverse[RADIUS, first : first + 8, :]
        if own:
            _, stiff, factor = own_state(dens, kind, cols, first)(rows - 1)
        else:
            at = pl.ds((rows - 1) * HALO, HALO)
            stiff, factor = edge_s[at, :], edge_f[at, :]
        energy, f_high = modal(line[2], line[3], stiff, constants)
        value = factor * energy * inverse[2 * RADIUS, first : first + 8, :]
        if own:
            total = total + stiff * energy
            final[first + 8 : first + 16, :] = value
        else:
            final[:HALO, :] = value
            final[wide:, :] = value
        for index, (row, g) in enumerate(((0, upper_of(f_low)), (rows - 1, lower_of(f_high)))):
            low, high = along_y(g)
            if own:
                joined = []
                for k in range(6):
                    carry_y[index, k, first + 9 : first + 17, :] = high[k]
                    joined.append(low[k] + carry_y[index, k, first + 8 : first + 16, :])
                for c, value in enumerate(along_z(joined, lane)):
                    resid[index, c, first : first + 8, :] = inner[c, pl.ds(row * cols + first, HALO), :] - value
            else:
                for k in range(6):
                    carry_y[index, k, 1:9, :] = high[k]

    half = depth // 2
    pieces = []
    for value in (total, sums[1]):
        line = jnp.sum(value, axis=0, keepdims=True)
        pieces.append(line + pltpu.roll(line, half, 1))
    line = jnp.where(lax.broadcasted_iota(jnp.int32, (1, depth), 1) < half, pieces[0], pieces[1])
    parts[...] = jnp.broadcast_to(line, (devices, depth))


def lines_y(near, row, cols, load):
    for block in range(cols // 8):
        start = HALO + 8 * block
        near[0, row, 8 * block : 8 * block + 8, :] = load(start)
        for shift in range(1, RADIUS + 1):
            near[shift, row, 8 * block : 8 * block + 8, :] = load(start + shift) + load(start - shift)


def filter_row(near, row, block, lane):
    depth = near.shape[-1]
    at = pl.ds(block * 8, 8)
    classes = {}
    for shift_x in range(RADIUS + 1):
        for shift_y in range(RADIUS + 1):
            square = shift_x * shift_x + shift_y * shift_y
            if square not in CLASSES:
                continue
            value = near[shift_y, row + (RADIUS + shift_x), at, :]
            if shift_x:
                value = value + near[shift_y, row + (RADIUS - shift_x), at, :]
            classes[square] = value if square not in classes else classes[square] + value
    result = None
    for shift_z in range(RADIUS + 1):
        line = None
        for square, value in classes.items():
            weight = weight_of(square + shift_z * shift_z)
            if weight > 0.0:
                line = weight * value if line is None else line + weight * value
        if shift_z:
            up = jnp.where(lane < shift_z, 0.0, pltpu.roll(line, shift_z, 1))
            down = jnp.where(lane >= depth - shift_z, 0.0, pltpu.roll(line, depth - shift_z, 1))
            line = up + down
        result = line if result is None else result + line
    return result


def bands(depth):
    row = lax.broadcasted_iota(jnp.int32, (depth, depth), 0)
    column = lax.broadcasted_iota(jnp.int32, (depth, depth), 1)
    away = jnp.abs(row - column)
    return jnp.concatenate(
        [jnp.where(away == shift, 1.0, 0.0).astype(jnp.bfloat16) for shift in range(1, RADIUS + 1)], axis=0
    )


def filter_rows(near, lines, result, picks, cols, band):
    depth = near.shape[-1]
    for rank, row in enumerate(picks):
        for block in range(cols // 8):
            at = pl.ds(block * 8, 8)
            classes = {}
            for shift_x in range(RADIUS + 1):
                for shift_y in range(RADIUS + 1):
                    square = shift_x * shift_x + shift_y * shift_y
                    if square not in CLASSES:
                        continue
                    value = near[shift_y, row + (RADIUS + shift_x), at, :]
                    if shift_x:
                        value = value + near[shift_y, row + (RADIUS - shift_x), at, :]
                    classes[square] = value if square not in classes else classes[square] + value
            for shift_z in range(RADIUS + 1):
                line = None
                for square, value in classes.items():
                    weight = weight_of(square + shift_z * shift_z)
                    if weight > 0.0:
                        line = weight * value if line is None else line + weight * value
                if shift_z:
                    first = rank * cols + 8 * block
                    lines[first : first + 8, (shift_z - 1) * depth : shift_z * depth] = line
                else:
                    result[row, at, :] = line
    value = lines[: len(picks) * cols, :]
    coarse = value.astype(jnp.bfloat16)
    rest = (value - coarse.astype(jnp.float32)).astype(jnp.bfloat16)
    total = jnp.dot(coarse, band, preferred_element_type=jnp.float32)
    total = total + jnp.dot(rest, band, preferred_element_type=jnp.float32)
    return total.reshape(len(picks), cols, depth)


def filter_rest(
    rows, cols, count_x, cells,
    near_in, inner, final, before, got_a, got_b, parts, outer, resid_in,
    sens, resid, comp, vol, near, ends, result_v, sems,
):
    depth = sens.shape[-1]
    del near_in, resid_in
    wide = cols + HALO
    copies = [
        pltpu.make_async_copy(outer.at[index], resid.at[:, row], sems.at[index])
        for index, row in enumerate((0, rows - 1))
    ]
    for copy in copies:
        copy.start()
    here = lax.axis_index("gx")
    has_low = here > 0
    has_high = here < count_x - 1
    odd = here % 2
    half = depth // 2
    line = jnp.sum(parts[...], axis=0, keepdims=True)
    first = lax.broadcasted_iota(jnp.int32, (1, depth), 1) < half
    compliance = jnp.sum(jnp.where(first, line, 0.0))
    volume = jnp.sum(jnp.where(first, 0.0, line))
    comp[0, 0] = compliance
    vol[0, 0] = volume / cells
    scale = cells / jnp.broadcast_to(compliance, (8, depth))

    def send(start, size):
        at = pl.ds(start, size)
        copies.append(pltpu.make_async_copy(result_v.at[at], sens.at[at], sems.at[len(copies)]))
        copies[-1].start()

    low_end, high_start = RADIUS + 1, rows - RADIUS - 1
    for row in range(low_end, high_start):
        for block in range(cols // 8):
            at = pl.ds(block * 8, 8)
            result_v[row, at, :] = inner[row, at, :] * scale
    send(low_end, high_start - low_end)

    def take(low, high):
        for index in range(RADIUS):
            for source, has, at in ((low, has_low, index), (high, has_high, RADIUS + index)):
                value = source[index]
                if source is low and index == RADIUS - 1:
                    value = value * before[...]
                value = jnp.where(has, value, 0.0)
                ends[at, :wide, :] = value
                ends[at, wide:, :] = value[:HALO]

    @pl.when(odd == 0)
    def _():
        take(got_b, got_a)

    @pl.when(odd == 1)
    def _():
        take(got_a, got_b)

    for index in range(RADIUS):
        lines_y(near, index, cols, lambda start, at=index: ends[at, start : start + 8, :])
        lines_y(near, rows + RADIUS + index, cols, lambda start, at=RADIUS + index: ends[at, start : start + 8, :])
    lines_y(near, rows + RADIUS - 1, cols, lambda start: final[start : start + 8, :])
    lane = lax.broadcasted_iota(jnp.int32, (8, depth), 1)
    for start, stop in ((0, low_end), (high_start, rows)):
        for row in range(start, stop):
            for block in range(cols // 8):
                result_v[row, 8 * block : 8 * block + 8, :] = filter_row(near, row, block, lane) * scale
        send(start, stop - start)
    for copy in copies:
        copy.wait()


def call(body, shapes, inputs, scratch=(), places=None, out_places=None, flops=0, limit=24, aliases=None):
    places, out_places = places or {}, out_places or {}
    in_specs = [pl.BlockSpec(memory_space=places.get(rank, pltpu.VMEM)) for rank in range(len(inputs))]
    out_specs = [pl.BlockSpec(memory_space=out_places.get(rank, pltpu.VMEM)) for rank in range(len(shapes))]
    moved = sum(int(np.prod(v.shape)) * 4 for v in list(inputs) + list(shapes))
    return pl.pallas_call(
        body,
        out_shape=[FULL(v.shape, v.dtype) for v in shapes],
        in_specs=in_specs,
        out_specs=out_specs,
        scratch_shapes=list(scratch),
        input_output_aliases=aliases or {},
        cost_estimate=pl.CostEstimate(flops=flops, bytes_accessed=moved, transcendentals=0),
        compiler_params=pltpu.CompilerParams(vmem_limit_bytes=int(limit * 1024 * 1024)),
    )(*inputs)


def f32(*shape):
    return FULL(shape, jnp.float32)


def vmem(*shape, dtype=jnp.float32):
    return pltpu.VMEM(shape, dtype)


def on_device(count_x, count_y, displacement, density, element_kind, load_x, load_y, load_z, load_force):
    rows, cols, depth = density.shape
    wide = cols + HALO
    devices = count_x * count_y
    cells = float(rows * cols * depth * devices)

    pairs_ya = [(k, k ^ 1) for k in range(count_y)]
    pairs_xa = [(k, k ^ 1) for k in range(count_x)]
    pairs_yb, pairs_xb = [], []
    for i in range(count_x):
        for j in range(count_y):
            here = i * count_y + j
            inside_y, inside_x = 0 < j < count_y - 1, 0 < i < count_x - 1
            pairs_yb.append((here, i * count_y + ((j + 1) ^ 1) - 1 if inside_y else (i ^ 1) * count_y + j))
            pairs_xb.append((here, (((i + 1) ^ 1) - 1) * count_y + j if inside_x else i * count_y + (j ^ 1)))

    disp = displacement.reshape(3 * rows * cols, depth)
    dens = density.reshape(rows * cols, depth)
    kind = element_kind.reshape(rows * cols, depth)

    slots = 4 * RADIUS + RADIUS
    send_a, send_b, mark = call(
        functools.partial(pack_y, rows, cols),
        [f32(slots * rows, depth)] * 2 + [f32(8, depth)],
        [displacement, density, element_kind],
        scratch=[
            vmem(3, rows, HALO, depth),
            vmem(rows, HALO, depth),
            vmem(rows, HALO, depth, dtype=jnp.int32),
            pltpu.SemaphoreType.DMA((6,)),
        ],
        places={0: pltpu.HBM, 1: pltpu.HBM, 2: pltpu.HBM},
        limit=53.25,
    )
    got_b = lax.ppermute(send_b, BOTH, pairs_yb)
    got_a = lax.ppermute(send_a, "gy", pairs_ya)

    sums = np.zeros((8, depth), np.float32)
    for rank, square in enumerate(CLASSES):
        for z in range(depth):
            sums[rank, z] = sum(
                weight_of(square + s * s) for s in range(-RADIUS, RADIUS + 1) if 0 <= z + s < depth
            )
    count = load_x.shape[0]
    applied, inverse = call(
        functools.partial(loads_and_weights, rows, cols, count_x, count_y),
        [f32(3, rows * cols, depth), f32(2 * RADIUS + 1, wide, depth)],
        [mark, load_x.reshape(1, count), load_y.reshape(1, count), load_z.reshape(1, count), load_force, jnp.asarray(sums)],
        places={0: pl.ANY},
        flops=2 * rows * cols * count * 6 * depth,
    )

    early = cols - HALO
    waves, tail, inner, scaled, sums = call(
        functools.partial(early_elements, rows, cols),
        [
            f32(6, rows, wide + HALO, depth),
            f32(6, rows, HALO, depth),
            f32(3, rows * cols, depth),
            f32(rows, wide + HALO, depth),
            f32(2, 8, depth),
        ],
        [disp, dens, kind, inverse, applied],
        scratch=[vmem(6, rows, HALO, depth)] * (cols // HALO - 2),
        flops=250 * rows * early * depth,
    )

    edge_u, edge_f, edge_s, send_a, send_b = call(
        functools.partial(unpack_y, rows, cols, count_y),
        [f32(3 * rows * HALO, depth), f32(rows * HALO, depth), f32(rows * HALO, depth)] + [f32(4, wide, depth)] * 2,
        [sums, disp, dens, kind, got_a, got_b],
        places={0: pl.ANY},
    )
    got_b = lax.ppermute(send_b, BOTH, pairs_xb)
    got_a = lax.ppermute(send_a, "gx", pairs_xa)

    waves, inner, scaled, sums, resid, near, filtered, send_a, send_b = call(
        functools.partial(late_elements, rows, cols),
        [f32(*v.shape) for v in (waves, inner, scaled, sums)]
        + [f32(3, rows, cols, depth), f32(RADIUS + 1, rows + 2 * RADIUS, cols, depth), f32(rows, cols, depth)]
        + [f32(RADIUS, wide, depth)] * 2,
        [waves, inner, scaled, tail, dens, kind, edge_u, edge_f, edge_s, applied, inverse, sums],
        scratch=[
            vmem(6 * rows * HALO, depth),
            vmem(FILTER_ROWS * cols, RADIUS * depth),
            pltpu.SemaphoreType.DMA((cols // HALO,)),
        ],
        out_places={4: pltpu.HBM},
        flops=250 * rows * 2 * HALO * depth,
        aliases={0: 0, 1: 1, 2: 2},
    )
    more_b = lax.ppermute(send_b, BOTH, pairs_xb)
    more_a = lax.ppermute(send_a, "gx", pairs_xa)
    outer, final, before, parts = call(
        functools.partial(outer_elements, rows, cols, count_x, devices),
        [f32(2, 3, cols, depth), f32(wide + HALO, depth), f32(wide, depth), f32(devices, depth)],
        [waves, dens, kind, edge_f, edge_s, got_a, got_b, inner, sums, inverse],
        scratch=[vmem(2, 6, wide + HALO, depth), vmem(wide, depth), vmem(2, 6, wide + 2 * HALO, depth)],
        flops=500 * wide * depth,
    )
    parts = lax.all_to_all(parts, BOTH, 0, 0, tiled=True)

    sens, resid, comp, volume, _ = call(
        functools.partial(filter_rest, rows, cols, count_x, cells),
        [f32(rows, cols, depth), f32(3, rows, cols, depth), f32(1, 1), f32(1, 1), f32(*near.shape)],
        [near, filtered, final, before, more_a, more_b, parts, outer, resid],
        scratch=[
            vmem(2 * RADIUS, wide + HALO, depth),
            vmem(rows, cols, depth),
            pltpu.SemaphoreType.DMA((5,)),
        ],
        places={8: pltpu.HBM},
        out_places={0: pltpu.HBM, 1: pltpu.HBM, 2: pltpu.SMEM, 3: pltpu.SMEM},
        flops=20 * rows * cols * depth,
        aliases={0: 4, 8: 1},
    )
    return (
        sens,
        resid,
        comp.reshape(()),
        volume.reshape(()),
    )


def solution(mesh):
    placed = (
        P(None, "gx", "gy", None),
        P("gx", "gy", None),
        P("gx", "gy", None),
        P(),
        P(),
        P(),
        P(),
    )
    return jax.shard_map(
        functools.partial(on_device, mesh.shape["gx"], mesh.shape["gy"]),
        mesh=mesh,
        in_specs=placed,
        out_specs=(P("gx", "gy", None), P(None, "gx", "gy", None), P(), P()),
        check_vma=False,
    )
```

```python
import functools

import jax
import jax.numpy as jnp
import numpy as np
from jax import lax
from jax.experimental import pallas as pl
from jax.experimental.pallas import tpu as pltpu
from jax.sharding import PartitionSpec as P

RADIUS = 3
PENALTY = 3.0
STIFF_FLOOR = 0.001
POISSON = 0.3
HALO = 8
BOTH = ("gx", "gy")
FULL = jax.ShapeDtypeStruct
FILTER_ROWS = 12


def element_matrix():
    lame_first = POISSON / ((1.0 + POISSON) * (1.0 - 2.0 * POISSON))
    shear_modulus = 0.5 / (1.0 + POISSON)
    material = np.zeros((6, 6))
    material[:3, :3] = lame_first
    for diagonal in range(3):
        material[diagonal, diagonal] += 2.0 * shear_modulus
        material[diagonal + 3, diagonal + 3] = shear_modulus
    points = [0.5 - 0.5 / np.sqrt(3.0), 0.5 + 0.5 / np.sqrt(3.0)]
    corners = [(a, b, e) for a in (0, 1) for b in (0, 1) for e in (0, 1)]
    result = np.zeros((24, 24))
    for point_x in points:
        for point_y in points:
            for point_z in points:
                strain = np.zeros((6, 24))
                for corner, (side_x, side_y, side_z) in enumerate(corners):
                    value_x = point_x if side_x else 1.0 - point_x
                    value_y = point_y if side_y else 1.0 - point_y
                    value_z = point_z if side_z else 1.0 - point_z
                    slope_x = (1.0 if side_x else -1.0) * value_y * value_z
                    slope_y = value_x * (1.0 if side_y else -1.0) * value_z
                    slope_z = value_x * value_y * (1.0 if side_z else -1.0)
                    column = 3 * corner
                    strain[0, column] = slope_x
                    strain[1, column + 1] = slope_y
                    strain[2, column + 2] = slope_z
                    strain[3, column] = slope_y
                    strain[3, column + 1] = slope_x
                    strain[4, column + 1] = slope_z
                    strain[4, column + 2] = slope_y
                    strain[5, column + 2] = slope_x
                    strain[5, column] = slope_z
                result += strain.T @ material @ strain / 8.0
    return result


def modal_matrix():
    pair = np.array([[1.0, 1.0], [-1.0, 1.0]])
    turn = np.kron(np.kron(np.kron(pair, pair), pair), np.eye(3))
    return turn @ element_matrix() @ turn.T / 64.0


SHEARS = ((3, 14), (4, 8), (6, 13))
NORMALS = (5, 7, 12)
PAIRS = ((10, 15), (11, 18), (17, 19))
TRIO = (9, 16, 20)
LASTS = (21, 22, 23)


def modal_constants():
    modal = modal_matrix()
    known = np.zeros((24, 24))
    shear = modal[3, 3]
    for first, second in SHEARS:
        known[np.ix_((first, second), (first, second))] = shear
    normal_off = modal[5, 7]
    normal_own = modal[5, 5] - normal_off
    known[np.ix_(NORMALS, NORMALS)] = normal_off
    pair_off = modal[10, 15]
    pair_own = modal[10, 10] - pair_off
    for both in PAIRS:
        known[np.ix_(both, both)] = pair_off
    trio = modal[9, 16]
    known[np.ix_(TRIO, TRIO)] = trio
    last = modal[21, 21]
    for group, own in ((NORMALS, normal_own), (sum(PAIRS, ()), pair_own), (TRIO, trio), (LASTS, last)):
        for degree in group:
            known[degree, degree] += own
    assert np.abs(known - modal).max() < 1e-12
    return tuple(float(v) for v in (shear, normal_off, normal_own, pair_off, pair_own, trio, last))


def weight_of(square):
    return max(0.0, RADIUS + 0.5 - float(np.sqrt(square)))


CLASSES = (0, 1, 2, 4, 5, 8, 9, 10)


def stiffness_of(physical):
    return STIFF_FLOOR + (1.0 - STIFF_FLOOR) * (physical * physical * physical)


def physical_of(density, kind):
    return jnp.where(kind == 1, 0.0, jnp.where(kind == 2, 1.0, density))


def factor_of(physical, kind):
    design = (kind != 1) & (kind != 2)
    return jnp.where(design, (-PENALTY * (1.0 - STIFF_FLOOR)) * (physical * physical), 0.0)


def pack_y(rows, cols, disp, dens, kind, out_a, out_b, mark, edge_d, edge_p, edge_k, sems):
    half = HALO // 2
    copies = []
    for side, start in ((0, 0), (half, cols - half)):
        for source, target in ((disp, edge_d), (dens, edge_p), (kind, edge_k)):
            lead = (slice(None),) * (len(source.shape) - 2)
            copies.append(
                pltpu.make_async_copy(
                    source.at[(*lead, pl.ds(start, half), slice(None))],
                    target.at[(*lead, pl.ds(side, half), slice(None))],
                    sems.at[len(copies)],
                )
            )
    for copy in copies:
        copy.start()
    for copy in copies:
        copy.wait()
    depth = disp.shape[-1]
    flat_d = edge_d.reshape(3 * rows * HALO, depth)
    flat_p = edge_p.reshape(rows * HALO, depth)
    flat_k = edge_k.reshape(rows * HALO, depth)

    def state(index):
        code = flat_k[pl.ds(index, rows, stride=HALO), :]
        return physical_of(flat_p[pl.ds(index, rows, stride=HALO), :], code), code

    def fill(low, high):
        slot = 0
        for c in range(3):
            for index in range(RADIUS + 1):
                low[pl.ds(slot * rows, rows), :] = flat_d[pl.ds(c * rows * HALO + index, rows, stride=HALO), :]
                slot += 1
        for index in range(RADIUS):
            low[pl.ds(slot * rows, rows), :] = factor_of(*state(index))
            slot += 1
        slot = 0
        for c in range(3):
            for index in range(HALO - RADIUS, HALO):
                high[pl.ds(slot * rows, rows), :] = flat_d[pl.ds(c * rows * HALO + index, rows, stride=HALO), :]
                slot += 1
        for index in range(HALO - RADIUS, HALO):
            physical, code = state(index)
            high[pl.ds(slot * rows, rows), :] = factor_of(physical, code)
            slot += 1
        high[pl.ds(slot * rows, rows), :] = stiffness_of(physical)

    mark[...] = jnp.zeros_like(mark)
    odd = lax.axis_index("gy") % 2

    @pl.when(odd == 0)
    def _():
        fill(out_b, out_a)

    @pl.when(odd == 1)
    def _():
        fill(out_a, out_b)


def unpack_y(rows, cols, count_y, after, disp, dens, kind, got_a, got_b, edge_u, edge_f, edge_s, out_a, out_b):
    del after
    here = lax.axis_index("gy")
    depth = disp.shape[-1]
    has_low = here > 0
    has_high = here < count_y - 1

    def fill(low, high):
        def put(ref, start, sublane, value):
            ref[pl.ds(start + sublane, rows, stride=HALO), :] = value

        zero = jnp.zeros((rows, depth), jnp.float32)
        slot = 0
        for c in range(3):
            for index in range(RADIUS + 1):
                put(edge_u, c * rows * HALO, index, jnp.where(has_high, high[pl.ds(slot * rows, rows), :], 0.0))
                slot += 1
        for index in range(RADIUS):
            put(edge_f, 0, index, jnp.where(has_high, high[pl.ds(slot * rows, rows), :], 0.0))
            slot += 1
        slot = 0
        for c in range(3):
            put(edge_u, c * rows * HALO, RADIUS + 1, zero)
            for index in range(HALO - RADIUS, HALO):
                put(edge_u, c * rows * HALO, index, low[pl.ds(slot * rows, rows), :])
                slot += 1
        for index in range(RADIUS, HALO - RADIUS):
            put(edge_f, 0, index, zero)
        for index in range(HALO - RADIUS, HALO):
            put(edge_f, 0, index, jnp.where(has_low, low[pl.ds(slot * rows, rows), :], 0.0))
            slot += 1
        edge_s[...] = jnp.zeros_like(edge_s)
        put(edge_s, 0, HALO - 1, jnp.where(has_low, low[pl.ds(slot * rows, rows), :], 0.0))

    odd = here % 2

    @pl.when(odd == 0)
    def _():
        fill(got_b, got_a)

    @pl.when(odd == 1)
    def _():
        fill(got_a, got_b)

    def send(out, row, with_stiff):
        for c in range(3):
            out[c, :cols, :] = disp[pl.ds((c * rows + row) * cols, cols), :]
            out[c, cols:, :] = edge_u[pl.ds((c * rows + row) * HALO, HALO), :]
        if with_stiff:
            at = pl.ds(row * cols, cols)
            out[3, :cols, :] = stiffness_of(physical_of(dens[at, :], kind[at, :]))
            out[3, cols:, :] = edge_s[pl.ds(row * HALO, HALO), :]
        else:
            out[3] = jnp.zeros_like(out[3])

    odd_x = lax.axis_index("gx") % 2

    @pl.when(odd_x == 0)
    def _():
        send(out_a, rows - 1, True)
        send(out_b, 0, False)

    @pl.when(odd_x == 1)
    def _():
        send(out_a, 0, False)
        send(out_b, rows - 1, True)


def loads_and_weights(rows, cols, count_x, count_y, after, load_x, load_y, load_z, force, sums, applied, inverse):
    del after
    depth = applied.shape[-1]
    place_x = lax.axis_index("gx") * rows
    place_y = lax.axis_index("gy") * cols
    local_x = load_x[...] - place_x
    local_y = load_y[...] - place_y
    owned = (local_x >= 0) & (local_x < rows) & (local_y >= 0) & (local_y < cols)
    target = jnp.where(owned, local_x * cols + local_y, -1)
    loads = target.shape[1]
    lanes = lax.broadcasted_iota(jnp.int32, (depth, loads), 0)
    hit_z = lanes == load_z[...]
    right = [[], []]
    for c in range(3):
        value = force[c : c + 1, :]
        coarse = value.astype(jnp.bfloat16).astype(jnp.float32)
        for part, piece in zip(right, (coarse, value - coarse)):
            part.append(jnp.where(hit_z, piece, 0.0).astype(jnp.bfloat16))
    place = lax.broadcasted_iota(jnp.int32, (rows * cols, loads), 0)
    left = jnp.where(place == target, 1.0, 0.0).astype(jnp.bfloat16)
    product = lax.dot_general(
        left, jnp.concatenate(right[0] + right[1], axis=0), (((1,), (1,)), ((), ())), preferred_element_type=jnp.float32
    )
    for c in range(3):
        applied[c] = product[:, c * depth : (c + 1) * depth] + product[:, (3 + c) * depth : (4 + c) * depth]

    wide = cols + HALO
    total_x, total_y = rows * count_x, cols * count_y
    sublane = lax.broadcasted_iota(jnp.int32, (wide, depth), 0)
    node_y = jnp.where(sublane >= wide - RADIUS, sublane - wide, sublane) + place_y
    inside_y = {
        shift: ((node_y + shift >= 0) & (node_y + shift < total_y)).astype(jnp.float32)
        for shift in range(-RADIUS, RADIUS + 1)
    }
    for kind in range(2 * RADIUS + 1):
        row = kind if kind <= RADIUS else rows - 2 * RADIUS - 1 + kind
        result = jnp.zeros((wide, depth), jnp.float32)
        for shift_y in range(-RADIUS, RADIUS + 1):
            line = jnp.zeros((1, depth), jnp.float32)
            for shift_x in range(-RADIUS, RADIUS + 1):
                square = shift_x * shift_x + shift_y * shift_y
                if square in CLASSES:
                    at = place_x + (row + shift_x)
                    inside = ((at >= 0) & (at < total_x)).astype(jnp.float32)
                    rank = CLASSES.index(square)
                    line = line + inside * sums[rank : rank + 1, :]
            result = result + inside_y[shift_y] * line
        inverse[kind] = 1.0 / jnp.where(result > 0.0, result, 1.0)


def shifted_z(value, lane, depth):
    beyond = jnp.where(lane == depth - 1, 0.0, pltpu.roll(value, depth - 1, 1))
    return value + beyond, beyond - value


def waves_of(here, there):
    return tuple(a + b for a, b in zip(here, there)) + tuple(b - a for a, b in zip(here, there))


def modal(before, after, stiff, constants):
    shear, normal_off, normal_own, pair_off, pair_own, trio, last = constants
    u = [None] * 24
    for low in range(12):
        if low >= 3:
            u[low] = before[low] + after[low]
        u[12 + low] = after[low] - before[low]
    f = [None] * 24
    terms = []

    def take(degree, pull):
        terms.append(pull * u[degree])
        f[degree] = pull * stiff

    for first, second in SHEARS:
        both = u[first] + u[second]
        pull = shear * both
        terms.append(pull * both)
        f[first] = f[second] = pull * stiff
    common = normal_off * (u[5] + u[7] + u[12])
    for degree in NORMALS:
        take(degree, common + normal_own * u[degree])
    for first, second in PAIRS:
        common = pair_off * (u[first] + u[second])
        take(first, common + pair_own * u[first])
        take(second, common + pair_own * u[second])
    common = u[9] + u[16] + u[20]
    for degree in TRIO:
        take(degree, trio * (common + u[degree]))
    for degree in LASTS:
        take(degree, last * u[degree])
    while len(terms) > 1:
        terms = [sum(terms[k : k + 2][1:], terms[k]) for k in range(0, len(terms), 2)]
    return terms[0], f


def lower_of(f):
    return tuple(f[12 + k] * -1.0 if f[k] is None else f[k] - f[12 + k] for k in range(12))


def upper_of(f):
    return tuple(f[12 + k] if f[k] is None else f[k] + f[12 + k] for k in range(12))


def along_y(g):
    return tuple(g[k] - g[6 + k] for k in range(6)), tuple(g[k] + g[6 + k] for k in range(6))


def along_z(g, lane):
    return [
        (g[c] - g[3 + c]) + jnp.where(lane == 0, 0.0, pltpu.roll(g[c] + g[3 + c], 1, 1)) for c in range(3)
    ]


def class_of(row, rows):
    return jnp.where(row < RADIUS, row, jnp.where(row >= rows - RADIUS, row - (rows - 2 * RADIUS - 1), RADIUS))


def march(rows, block, waves, state, inverse, emit, put, own):
    constants = modal_constants()
    depth = waves.shape[-1]
    first = 8 * block
    zero = jnp.zeros((HALO, depth), jnp.float32)

    def nodes(row):
        return waves_of(
            [waves[k, row, first : first + 8, :] for k in range(6)],
            [waves[k, row, first + 1 : first + 9, :] for k in range(6)],
        )

    def step(row, carry):
        before, held, total, filled = carry
        after = nodes(row + 1)
        physical, stiff, factor = state(row)
        energy, f = modal(before, after, stiff, constants)
        put(row, factor * energy * inverse[class_of(row, rows), first : first + 8, :])
        if own:
            total = total + stiff * energy
            filled = filled + physical
        emit(row, *along_y(tuple(a + b for a, b in zip(held, lower_of(f)))))
        return after, upper_of(f), total, filled

    carry = (nodes(0), (zero,) * 12, zero, zero)
    carry = lax.fori_loop(0, rows - 2, step, carry, unroll=True)
    _, held, total, filled = step(rows - 2, carry)
    emit(rows - 1, *along_y(held))
    if own:
        filled = filled + state(rows - 1)[0]
    return total, filled


def own_state(dens, kind, cols, first):
    def state(row):
        at = pl.ds(pl.multiple_of(row * cols + first, 8), HALO)
        code = kind[at, :]
        physical = physical_of(dens[at, :], code)
        return physical, stiffness_of(physical), factor_of(physical, code)

    return state


def joiner(cols, block, tail_in, tail_out, applied, resid):
    first = 8 * block
    depth = resid.shape[-1]
    lane = lax.broadcasted_iota(jnp.int32, (HALO, depth), 1)
    sublane = lax.broadcasted_iota(jnp.int32, (HALO, depth), 0)

    def emit(row, low, high):
        parts = []
        for k in range(6):
            turned = pltpu.roll(high[k], 1, 0)
            if tail_out is not None:
                tail_out[k, row] = turned
            before = 0.0 if tail_in is None else tail_in[k, row]
            parts.append(low[k] + jnp.where(sublane == 0, before, turned))
        at = pl.ds(pl.multiple_of(row * cols + first, 8), HALO)
        for c, value in enumerate(along_z(parts, lane)):
            resid[c, at, :] = applied[c, at, :] - value

    return emit


def early_elements(
    rows, cols, disp, dens, kind, inverse, applied, waves, tail, resid, scaled, sums, *tails
):
    depth = disp.shape[-1]
    lane = lax.broadcasted_iota(jnp.int32, (HALO, depth), 1)

    def turn(row, nothing):
        for c in range(3):
            for block in range(cols // 8):
                at = pl.ds(pl.multiple_of((c * rows + row) * cols + 8 * block, 8), HALO)
                for r, value in enumerate(shifted_z(disp[at, :], lane, depth)):
                    waves[3 * r + c, row, 8 * block : 8 * block + 8, :] = value
                    if block == 0:
                        waves[3 * r + c, row, cols + HALO :, :] = value
        return nothing

    lax.fori_loop(0, rows, turn, 0, unroll=8)
    total = filled = jnp.zeros((HALO, depth), jnp.float32)
    chain = (None, *tails, tail)
    for block in range(cols // 8 - 1):
        first = 8 * block

        def put(row, value, first=first):
            scaled[row, first + 8 : first + 16, :] = value

        emit = joiner(cols, block, chain[block], chain[block + 1], applied, resid)
        state = own_state(dens, kind, cols, first)
        more = march(rows, block, waves, state, inverse, emit, put, True)
        total, filled = total + more[0], filled + more[1]
    sums[0] = total
    sums[1] = filled


def late_elements(
    rows, cols,
    waves_in, resid_in, scaled_in, tail, dens, kind, edge_u, edge_f, edge_s, applied, inverse, sums_a,
    waves, resid, scaled, sums, resid_out, out_a, out_b, far_h, sems,
):
    depth = dens.shape[-1]
    del waves_in, resid_in, scaled_in
    wide = cols + HALO
    lane = lax.broadcasted_iota(jnp.int32, (HALO, depth), 1)

    def turn(row, nothing):
        for c in range(3):
            at = pl.ds(pl.multiple_of((c * rows + row) * HALO, 8), HALO)
            for r, value in enumerate(shifted_z(edge_u[at, :], lane, depth)):
                waves[3 * r + c, row, cols:wide, :] = value
        return nothing

    lax.fori_loop(0, rows, turn, 0, unroll=16)

    def edge_state(row):
        at = pl.ds(pl.multiple_of(row * HALO, 8), HALO)
        return None, edge_s[at, :], edge_f[at, :]

    def put_edge(row, value):
        scaled[row, :HALO, :] = value
        scaled[row, wide:, :] = value

    def emit_edge(row, low, high):
        for k in range(6):
            far_h[pl.ds(pl.multiple_of((k * rows + row) * HALO, 8), HALO), :] = high[k]

    last = cols // 8 - 1
    source = resid.reshape(3, rows, cols, depth)
    copies = []

    def send(block):
        at = (slice(None), pl.ds(1, rows - 2), pl.ds(8 * block, 8), slice(None))
        copies.append(pltpu.make_async_copy(source.at[at], resid_out.at[at], sems.at[block]))
        copies[-1].start()

    for block in range(1, last):
        send(block)
    march(rows, cols // 8, waves, edge_state, inverse, emit_edge, put_edge, False)
    parts = [far_h[pl.ds(k * rows * HALO + HALO - 1, rows, stride=HALO), :] for k in range(6)]
    at = pl.ds(0, rows, stride=cols)
    for c, value in enumerate(along_z(parts, lax.broadcasted_iota(jnp.int32, (rows, depth), 1))):
        resid[c, at, :] = resid[c, at, :] - value
    send(0)

    def put(row, value):
        scaled[row, cols:wide, :] = value

    emit = joiner(cols, last, tail, None, applied, resid)
    state = own_state(dens, kind, cols, 8 * last)
    total, filled = march(rows, last, waves, state, inverse, emit, put, True)
    send(last)
    sums[0] = sums_a[0] + total
    sums[1] = sums_a[1] + filled

    def out(up, down):
        for index in range(RADIUS - 1):
            up[index] = scaled[rows - RADIUS + index, :wide, :]
        at = pl.ds((rows - 1) * cols, cols)
        code = kind[at, :]
        up[RADIUS - 1, HALO:, :] = factor_of(physical_of(dens[at, :], code), code)
        up[RADIUS - 1, :HALO, :] = edge_f[pl.ds((rows - 1) * HALO, HALO), :]
        for index in range(RADIUS):
            down[index] = scaled[index, :wide, :]

    odd = lax.axis_index("gx") % 2

    @pl.when(odd == 0)
    def _():
        out(out_a, out_b)

    @pl.when(odd == 1)
    def _():
        out(out_b, out_a)
    for copy in copies:
        copy.wait()


def outer_elements(
    rows, cols, count_x, devices,
    waves, dens, kind, edge_f, edge_s, got_a, got_b, inner, sums, inverse,
    resid, final, before, parts, ring, stiff_low, carry_y,
):
    depth = dens.shape[-1]
    constants = modal_constants()
    wide = cols + HALO
    blocks = wide // HALO
    lane = lax.broadcasted_iota(jnp.int32, (HALO, depth), 1)
    here = lax.axis_index("gx")
    has_low = here > 0
    has_high = here < count_x - 1
    odd = here % 2

    def take(low, high):
        for block in range(blocks):
            first = 8 * block
            for c in range(3):
                for side, value in enumerate((low[c, first : first + 8, :], high[c, first : first + 8, :])):
                    if side:
                        value = jnp.where(has_high, value, 0.0)
                    for r, wave in enumerate(shifted_z(value, lane, depth)):
                        ring[side, 3 * r + c, first : first + 8, :] = wave
                        if block == 0:
                            ring[side, 3 * r + c, wide:, :] = wave
        stiff_low[...] = jnp.where(has_low, low[3], 0.0)

    @pl.when(odd == 0)
    def _():
        take(got_b, got_a)

    @pl.when(odd == 1)
    def _():
        take(got_a, got_b)

    total = sums[0]
    for block in (blocks - 1, *range(blocks - 1)):
        own = block < blocks - 1
        first = 8 * block

        def nodes(load):
            return waves_of(
                [load(k)[first : first + 8, :] for k in range(6)], [load(k)[first + 1 : first + 9, :] for k in range(6)]
            )

        line = [
            nodes(lambda k: ring.at[0, k]),
            nodes(lambda k: waves.at[k, 0]),
            nodes(lambda k: waves.at[k, rows - 1]),
            nodes(lambda k: ring.at[1, k]),
        ]
        energy, f_low = modal(line[0], line[1], stiff_low[first : first + 8, :], constants)
        place = first + 8 if own else 0
        before[place : place + 8, :] = energy * inverse[RADIUS, first : first + 8, :]
        if own:
            _, stiff, factor = own_state(dens, kind, cols, first)(rows - 1)
        else:
            at = pl.ds((rows - 1) * HALO, HALO)
            stiff, factor = edge_s[at, :], edge_f[at, :]
        energy, f_high = modal(line[2], line[3], stiff, constants)
        value = factor * energy * inverse[2 * RADIUS, first : first + 8, :]
        if own:
            total = total + stiff * energy
            final[first + 8 : first + 16, :] = value
        else:
            final[:HALO, :] = value
            final[wide:, :] = value
        for index, (row, g) in enumerate(((0, upper_of(f_low)), (rows - 1, lower_of(f_high)))):
            low, high = along_y(g)
            if own:
                joined = []
                for k in range(6):
                    carry_y[index, k, first + 9 : first + 17, :] = high[k]
                    joined.append(low[k] + carry_y[index, k, first + 8 : first + 16, :])
                for c, value in enumerate(along_z(joined, lane)):
                    resid[index, c, first : first + 8, :] = inner[c, pl.ds(row * cols + first, HALO), :] - value
            else:
                for k in range(6):
                    carry_y[index, k, 1:9, :] = high[k]

    half = depth // 2
    pieces = []
    for value in (total, sums[1]):
        line = jnp.sum(value, axis=0, keepdims=True)
        pieces.append(line + pltpu.roll(line, half, 1))
    line = jnp.where(lax.broadcasted_iota(jnp.int32, (1, depth), 1) < half, pieces[0], pieces[1])
    parts[...] = jnp.broadcast_to(line, (devices, depth))


def lines_y(near, row, cols, load):
    for block in range(cols // 8):
        start = HALO + 8 * block
        near[0, row, 8 * block : 8 * block + 8, :] = load(start)
        for shift in range(1, RADIUS + 1):
            near[shift, row, 8 * block : 8 * block + 8, :] = load(start + shift) + load(start - shift)


def bands(depth):
    row = lax.broadcasted_iota(jnp.int32, (depth, depth), 0)
    column = lax.broadcasted_iota(jnp.int32, (depth, depth), 1)
    away = jnp.abs(row - column)
    return jnp.concatenate(
        [jnp.where(away == shift, 1.0, 0.0).astype(jnp.bfloat16) for shift in range(1, RADIUS + 1)], axis=0
    )


def filter_rows(near, lines, result, picks, cols, band):
    depth = near.shape[-1]
    for rank, row in enumerate(picks):
        for block in range(cols // 8):
            at = pl.ds(block * 8, 8)
            classes = {}
            for shift_x in range(RADIUS + 1):
                for shift_y in range(RADIUS + 1):
                    square = shift_x * shift_x + shift_y * shift_y
                    if square not in CLASSES:
                        continue
                    value = near[shift_y, row + (RADIUS + shift_x), at, :]
                    if shift_x:
                        value = value + near[shift_y, row + (RADIUS - shift_x), at, :]
                    classes[square] = value if square not in classes else classes[square] + value
            for shift_z in range(RADIUS + 1):
                line = None
                for square, value in classes.items():
                    weight = weight_of(square + shift_z * shift_z)
                    if weight > 0.0:
                        line = weight * value if line is None else line + weight * value
                if shift_z:
                    first = rank * cols + 8 * block
                    lines[first : first + 8, (shift_z - 1) * depth : shift_z * depth] = line
                else:
                    result[row, at, :] = line
    value = lines[: len(picks) * cols, :]
    coarse = value.astype(jnp.bfloat16)
    rest = (value - coarse.astype(jnp.float32)).astype(jnp.bfloat16)
    total = jnp.dot(coarse, band, preferred_element_type=jnp.float32)
    total = total + jnp.dot(rest, band, preferred_element_type=jnp.float32)
    return total.reshape(len(picks), cols, depth)


def filter_all(rows, cols, count_x, scaled, final, before, got_a, got_b, result, near, ends, lines):
    depth = result.shape[-1]
    wide = cols + HALO
    here = lax.axis_index("gx")
    has_low = here > 0
    has_high = here < count_x - 1
    odd = here % 2

    def take(low, high):
        for index in range(RADIUS):
            for source, has, at in ((low, has_low, index), (high, has_high, RADIUS + index)):
                value = source[index]
                if source is low and index == RADIUS - 1:
                    value = value * before[...]
                value = jnp.where(has, value, 0.0)
                ends[at, :wide, :] = value
                ends[at, wide:, :] = value[:HALO]

    @pl.when(odd == 0)
    def _():
        take(got_b, got_a)

    @pl.when(odd == 1)
    def _():
        take(got_a, got_b)

    for index in range(RADIUS):
        lines_y(near, index, cols, lambda start, at=index: ends[at, start : start + 8, :])
        lines_y(near, rows + RADIUS + index, cols, lambda start, at=RADIUS + index: ends[at, start : start + 8, :])
    lines_y(near, rows + RADIUS - 1, cols, lambda start: final[start : start + 8, :])
    for row in range(rows - 1):
        lines_y(near, row + RADIUS, cols, lambda start, row=row: scaled[row, start : start + 8, :])
    band = bands(depth)
    for start in range(0, rows, FILTER_ROWS):
        picks = range(start, min(start + FILTER_ROWS, rows))
        rest = filter_rows(near, lines, result, picks, cols, band)
        result[picks.start : picks.stop] = result[picks.start : picks.stop] + rest


def finish(rows, cols, cells, inner, parts, outer, resid_in, sens, resid, comp, vol, result_v, sems):
    depth = sens.shape[-1]
    del resid_in
    copies = [
        pltpu.make_async_copy(outer.at[index], resid.at[:, row], sems.at[index])
        for index, row in enumerate((0, rows - 1))
    ]
    for copy in copies:
        copy.start()
    half = depth // 2
    line = jnp.sum(parts[...], axis=0, keepdims=True)
    first = lax.broadcasted_iota(jnp.int32, (1, depth), 1) < half
    compliance = jnp.sum(jnp.where(first, line, 0.0))
    volume = jnp.sum(jnp.where(first, 0.0, line))
    comp[0, 0] = compliance
    vol[0, 0] = volume / cells
    scale = cells / jnp.broadcast_to(compliance, (8, depth))
    size = rows // 2
    for start in range(0, rows, size):
        for row in range(start, start + size):
            for block in range(cols // 8):
                at = pl.ds(block * 8, 8)
                result_v[row, at, :] = inner[row, at, :] * scale
        at = pl.ds(start, size)
        copies.append(pltpu.make_async_copy(result_v.at[at], sens.at[at], sems.at[len(copies)]))
        copies[-1].start()
    for copy in copies:
        copy.wait()


def call(body, shapes, inputs, scratch=(), places=None, out_places=None, flops=0, limit=24, aliases=None):
    places, out_places = places or {}, out_places or {}
    in_specs = [pl.BlockSpec(memory_space=places.get(rank, pltpu.VMEM)) for rank in range(len(inputs))]
    out_specs = [pl.BlockSpec(memory_space=out_places.get(rank, pltpu.VMEM)) for rank in range(len(shapes))]
    moved = sum(int(np.prod(v.shape)) * 4 for v in list(inputs) + list(shapes))
    return pl.pallas_call(
        body,
        out_shape=[FULL(v.shape, v.dtype) for v in shapes],
        in_specs=in_specs,
        out_specs=out_specs,
        scratch_shapes=list(scratch),
        input_output_aliases=aliases or {},
        cost_estimate=pl.CostEstimate(flops=flops, bytes_accessed=moved, transcendentals=0),
        compiler_params=pltpu.CompilerParams(vmem_limit_bytes=int(limit * 1024 * 1024)),
    )(*inputs)


def f32(*shape):
    return FULL(shape, jnp.float32)


def vmem(*shape, dtype=jnp.float32):
    return pltpu.VMEM(shape, dtype)


def on_device(count_x, count_y, displacement, density, element_kind, load_x, load_y, load_z, load_force):
    rows, cols, depth = density.shape
    wide = cols + HALO
    devices = count_x * count_y
    cells = float(rows * cols * depth * devices)

    pairs_ya = [(k, k ^ 1) for k in range(count_y)]
    pairs_xa = [(k, k ^ 1) for k in range(count_x)]
    pairs_yb, pairs_xb = [], []
    for i in range(count_x):
        for j in range(count_y):
            here = i * count_y + j
            inside_y, inside_x = 0 < j < count_y - 1, 0 < i < count_x - 1
            pairs_yb.append((here, i * count_y + ((j + 1) ^ 1) - 1 if inside_y else (i ^ 1) * count_y + j))
            pairs_xb.append((here, (((i + 1) ^ 1) - 1) * count_y + j if inside_x else i * count_y + (j ^ 1)))

    disp = displacement.reshape(3 * rows * cols, depth)
    dens = density.reshape(rows * cols, depth)
    kind = element_kind.reshape(rows * cols, depth)

    slots = 4 * RADIUS + RADIUS
    send_a, send_b, mark = call(
        functools.partial(pack_y, rows, cols),
        [f32(slots * rows, depth)] * 2 + [f32(8, depth)],
        [displacement, density, element_kind],
        scratch=[
            vmem(3, rows, HALO, depth),
            vmem(rows, HALO, depth),
            vmem(rows, HALO, depth, dtype=jnp.int32),
            pltpu.SemaphoreType.DMA((6,)),
        ],
        places={0: pltpu.HBM, 1: pltpu.HBM, 2: pltpu.HBM},
        limit=53.25,
    )
    got_b = lax.ppermute(send_b, BOTH, pairs_yb)
    got_a = lax.ppermute(send_a, "gy", pairs_ya)

    sums = np.zeros((8, depth), np.float32)
    for rank, square in enumerate(CLASSES):
        for z in range(depth):
            sums[rank, z] = sum(
                weight_of(square + s * s) for s in range(-RADIUS, RADIUS + 1) if 0 <= z + s < depth
            )
    count = load_x.shape[0]
    applied, inverse = call(
        functools.partial(loads_and_weights, rows, cols, count_x, count_y),
        [f32(3, rows * cols, depth), f32(2 * RADIUS + 1, wide, depth)],
        [mark, load_x.reshape(1, count), load_y.reshape(1, count), load_z.reshape(1, count), load_force, jnp.asarray(sums)],
        places={0: pl.ANY},
        flops=2 * rows * cols * count * 6 * depth,
    )

    early = cols - HALO
    waves, tail, inner, scaled, sums = call(
        functools.partial(early_elements, rows, cols),
        [
            f32(6, rows, wide + HALO, depth),
            f32(6, rows, HALO, depth),
            f32(3, rows * cols, depth),
            f32(rows, wide + HALO, depth),
            f32(2, 8, depth),
        ],
        [disp, dens, kind, inverse, applied],
        scratch=[vmem(6, rows, HALO, depth)] * (cols // HALO - 2),
        flops=250 * rows * early * depth,
    )

    edge_u, edge_f, edge_s, send_a, send_b = call(
        functools.partial(unpack_y, rows, cols, count_y),
        [f32(3 * rows * HALO, depth), f32(rows * HALO, depth), f32(rows * HALO, depth)] + [f32(4, wide, depth)] * 2,
        [sums, disp, dens, kind, got_a, got_b],
        places={0: pl.ANY},
    )
    got_b = lax.ppermute(send_b, BOTH, pairs_xb)
    got_a = lax.ppermute(send_a, "gx", pairs_xa)

    waves, inner, scaled, sums, resid, send_a, send_b = call(
        functools.partial(late_elements, rows, cols),
        [f32(*v.shape) for v in (waves, inner, scaled, sums)]
        + [f32(3, rows, cols, depth)]
        + [f32(RADIUS, wide, depth)] * 2,
        [waves, inner, scaled, tail, dens, kind, edge_u, edge_f, edge_s, applied, inverse, sums],
        scratch=[
            vmem(6 * rows * HALO, depth),
            pltpu.SemaphoreType.DMA((cols // HALO,)),
        ],
        out_places={4: pltpu.HBM},
        flops=250 * rows * 2 * HALO * depth,
        aliases={0: 0, 1: 1, 2: 2},
    )
    more_b = lax.ppermute(send_b, BOTH, pairs_xb)
    more_a = lax.ppermute(send_a, "gx", pairs_xa)
    outer, final, before, parts = call(
        functools.partial(outer_elements, rows, cols, count_x, devices),
        [f32(2, 3, cols, depth), f32(wide + HALO, depth), f32(wide, depth), f32(devices, depth)],
        [waves, dens, kind, edge_f, edge_s, got_a, got_b, inner, sums, inverse],
        scratch=[vmem(2, 6, wide + HALO, depth), vmem(wide, depth), vmem(2, 6, wide + 2 * HALO, depth)],
        flops=500 * wide * depth,
    )
    parts = lax.all_to_all(parts, BOTH, 0, 0, tiled=True)

    filtered, = call(
        functools.partial(filter_all, rows, cols, count_x),
        [f32(rows, cols, depth)],
        [scaled, final, before, more_a, more_b],
        scratch=[
            vmem(RADIUS + 1, rows + 2 * RADIUS, cols, depth),
            vmem(2 * RADIUS, wide + HALO, depth),
            vmem(FILTER_ROWS * cols, RADIUS * depth),
        ],
        flops=80 * rows * cols * depth,
    )
    sens, resid, comp, volume = call(
        functools.partial(finish, rows, cols, cells),
        [f32(rows, cols, depth), f32(3, rows, cols, depth), f32(1, 1), f32(1, 1)],
        [filtered, parts, outer, resid],
        scratch=[vmem(rows, cols, depth), pltpu.SemaphoreType.DMA((4,))],
        places={3: pltpu.HBM},
        out_places={0: pltpu.HBM, 1: pltpu.HBM, 2: pltpu.SMEM, 3: pltpu.SMEM},
        flops=rows * cols * depth,
        aliases={3: 1},
    )
    return (
        sens,
        resid,
        comp.reshape(()),
        volume.reshape(()),
    )


def solution(mesh):
    placed = (
        P(None, "gx", "gy", None),
        P("gx", "gy", None),
        P("gx", "gy", None),
        P(),
        P(),
        P(),
        P(),
    )
    return jax.shard_map(
        functools.partial(on_device, mesh.shape["gx"], mesh.shape["gy"]),
        mesh=mesh,
        in_specs=placed,
        out_specs=(P("gx", "gy", None), P(None, "gx", "gy", None), P(), P()),
        check_vma=False,
    )
```

```python
import functools

import jax
import jax.numpy as jnp
import numpy as np
from jax import lax
from jax.experimental import pallas as pl
from jax.experimental.pallas import tpu as pltpu
from jax.sharding import PartitionSpec as P

RADIUS = 3
PENALTY = 3.0
STIFF_FLOOR = 0.001
POISSON = 0.3
HALO = 8
BOTH = ("gx", "gy")
FULL = jax.ShapeDtypeStruct
FILTER_ROWS = 12


def element_matrix():
    lame_first = POISSON / ((1.0 + POISSON) * (1.0 - 2.0 * POISSON))
    shear_modulus = 0.5 / (1.0 + POISSON)
    material = np.zeros((6, 6))
    material[:3, :3] = lame_first
    for diagonal in range(3):
        material[diagonal, diagonal] += 2.0 * shear_modulus
        material[diagonal + 3, diagonal + 3] = shear_modulus
    points = [0.5 - 0.5 / np.sqrt(3.0), 0.5 + 0.5 / np.sqrt(3.0)]
    corners = [(a, b, e) for a in (0, 1) for b in (0, 1) for e in (0, 1)]
    result = np.zeros((24, 24))
    for point_x in points:
        for point_y in points:
            for point_z in points:
                strain = np.zeros((6, 24))
                for corner, (side_x, side_y, side_z) in enumerate(corners):
                    value_x = point_x if side_x else 1.0 - point_x
                    value_y = point_y if side_y else 1.0 - point_y
                    value_z = point_z if side_z else 1.0 - point_z
                    slope_x = (1.0 if side_x else -1.0) * value_y * value_z
                    slope_y = value_x * (1.0 if side_y else -1.0) * value_z
                    slope_z = value_x * value_y * (1.0 if side_z else -1.0)
                    column = 3 * corner
                    strain[0, column] = slope_x
                    strain[1, column + 1] = slope_y
                    strain[2, column + 2] = slope_z
                    strain[3, column] = slope_y
                    strain[3, column + 1] = slope_x
                    strain[4, column + 1] = slope_z
                    strain[4, column + 2] = slope_y
                    strain[5, column + 2] = slope_x
                    strain[5, column] = slope_z
                result += strain.T @ material @ strain / 8.0
    return result


def modal_matrix():
    pair = np.array([[1.0, 1.0], [-1.0, 1.0]])
    turn = np.kron(np.kron(np.kron(pair, pair), pair), np.eye(3))
    return turn @ element_matrix() @ turn.T / 64.0


SHEARS = ((3, 14), (4, 8), (6, 13))
NORMALS = (5, 7, 12)
PAIRS = ((10, 15), (11, 18), (17, 19))
TRIO = (9, 16, 20)
LASTS = (21, 22, 23)


def modal_constants():
    modal = modal_matrix()
    known = np.zeros((24, 24))
    shear = modal[3, 3]
    for first, second in SHEARS:
        known[np.ix_((first, second), (first, second))] = shear
    normal_off = modal[5, 7]
    normal_own = modal[5, 5] - normal_off
    known[np.ix_(NORMALS, NORMALS)] = normal_off
    pair_off = modal[10, 15]
    pair_own = modal[10, 10] - pair_off
    for both in PAIRS:
        known[np.ix_(both, both)] = pair_off
    trio = modal[9, 16]
    known[np.ix_(TRIO, TRIO)] = trio
    last = modal[21, 21]
    for group, own in ((NORMALS, normal_own), (sum(PAIRS, ()), pair_own), (TRIO, trio), (LASTS, last)):
        for degree in group:
            known[degree, degree] += own
    assert np.abs(known - modal).max() < 1e-12
    return tuple(float(v) for v in (shear, normal_off, normal_own, pair_off, pair_own, trio, last))


def weight_of(square):
    return max(0.0, RADIUS + 0.5 - float(np.sqrt(square)))


CLASSES = (0, 1, 2, 4, 5, 8, 9, 10)


def stiffness_of(physical):
    return STIFF_FLOOR + (1.0 - STIFF_FLOOR) * (physical * physical * physical)


def physical_of(density, kind):
    return jnp.where(kind == 1, 0.0, jnp.where(kind == 2, 1.0, density))


def factor_of(physical, kind):
    design = (kind != 1) & (kind != 2)
    return jnp.where(design, (-PENALTY * (1.0 - STIFF_FLOOR)) * (physical * physical), 0.0)


def pack_y(rows, cols, disp, dens, kind, out_a, out_b, mark, edge_d, edge_p, edge_k, sems):
    half = HALO // 2
    copies = []
    for side, start in ((0, 0), (half, cols - half)):
        for source, target in ((disp, edge_d), (dens, edge_p), (kind, edge_k)):
            lead = (slice(None),) * (len(source.shape) - 2)
            copies.append(
                pltpu.make_async_copy(
                    source.at[(*lead, pl.ds(start, half), slice(None))],
                    target.at[(*lead, pl.ds(side, half), slice(None))],
                    sems.at[len(copies)],
                )
            )
    for copy in copies:
        copy.start()
    for copy in copies:
        copy.wait()
    depth = disp.shape[-1]
    flat_d = edge_d.reshape(3 * rows * HALO, depth)
    flat_p = edge_p.reshape(rows * HALO, depth)
    flat_k = edge_k.reshape(rows * HALO, depth)

    def state(index):
        code = flat_k[pl.ds(index, rows, stride=HALO), :]
        return physical_of(flat_p[pl.ds(index, rows, stride=HALO), :], code), code

    def fill(low, high):
        slot = 0
        for c in range(3):
            for index in range(RADIUS + 1):
                low[pl.ds(slot * rows, rows), :] = flat_d[pl.ds(c * rows * HALO + index, rows, stride=HALO), :]
                slot += 1
        for index in range(RADIUS):
            low[pl.ds(slot * rows, rows), :] = factor_of(*state(index))
            slot += 1
        slot = 0
        for c in range(3):
            for index in range(HALO - RADIUS, HALO):
                high[pl.ds(slot * rows, rows), :] = flat_d[pl.ds(c * rows * HALO + index, rows, stride=HALO), :]
                slot += 1
        for index in range(HALO - RADIUS, HALO):
            physical, code = state(index)
            high[pl.ds(slot * rows, rows), :] = factor_of(physical, code)
            slot += 1
        high[pl.ds(slot * rows, rows), :] = stiffness_of(physical)

    mark[...] = jnp.zeros_like(mark)
    odd = lax.axis_index("gy") % 2

    @pl.when(odd == 0)
    def _():
        fill(out_b, out_a)

    @pl.when(odd == 1)
    def _():
        fill(out_a, out_b)


def unpack_y(rows, cols, count_y, after, disp, dens, kind, got_a, got_b, edge_u, edge_f, edge_s, out_a, out_b):
    del after
    here = lax.axis_index("gy")
    depth = disp.shape[-1]
    has_low = here > 0
    has_high = here < count_y - 1

    def fill(low, high):
        def put(ref, start, sublane, value):
            ref[pl.ds(start + sublane, rows, stride=HALO), :] = value

        zero = jnp.zeros((rows, depth), jnp.float32)
        slot = 0
        for c in range(3):
            for index in range(RADIUS + 1):
                put(edge_u, c * rows * HALO, index, jnp.where(has_high, high[pl.ds(slot * rows, rows), :], 0.0))
                slot += 1
        for index in range(RADIUS):
            put(edge_f, 0, index, jnp.where(has_high, high[pl.ds(slot * rows, rows), :], 0.0))
            slot += 1
        slot = 0
        for c in range(3):
            put(edge_u, c * rows * HALO, RADIUS + 1, zero)
            for index in range(HALO - RADIUS, HALO):
                put(edge_u, c * rows * HALO, index, low[pl.ds(slot * rows, rows), :])
                slot += 1
        for index in range(RADIUS, HALO - RADIUS):
            put(edge_f, 0, index, zero)
        for index in range(HALO - RADIUS, HALO):
            put(edge_f, 0, index, jnp.where(has_low, low[pl.ds(slot * rows, rows), :], 0.0))
            slot += 1
        edge_s[...] = jnp.zeros_like(edge_s)
        put(edge_s, 0, HALO - 1, jnp.where(has_low, low[pl.ds(slot * rows, rows), :], 0.0))

    odd = here % 2

    @pl.when(odd == 0)
    def _():
        fill(got_b, got_a)

    @pl.when(odd == 1)
    def _():
        fill(got_a, got_b)

    def send(out, row, with_stiff):
        for c in range(3):
            out[c, :cols, :] = disp[pl.ds((c * rows + row) * cols, cols), :]
            out[c, cols:, :] = edge_u[pl.ds((c * rows + row) * HALO, HALO), :]
        if with_stiff:
            at = pl.ds(row * cols, cols)
            out[3, :cols, :] = stiffness_of(physical_of(dens[at, :], kind[at, :]))
            out[3, cols:, :] = edge_s[pl.ds(row * HALO, HALO), :]
        else:
            out[3] = jnp.zeros_like(out[3])

    odd_x = lax.axis_index("gx") % 2

    @pl.when(odd_x == 0)
    def _():
        send(out_a, rows - 1, True)
        send(out_b, 0, False)

    @pl.when(odd_x == 1)
    def _():
        send(out_a, 0, False)
        send(out_b, rows - 1, True)


def loads_and_weights(rows, cols, count_x, count_y, after, load_x, load_y, load_z, force, sums, applied, inverse):
    del after
    depth = applied.shape[-1]
    place_x = lax.axis_index("gx") * rows
    place_y = lax.axis_index("gy") * cols
    local_x = load_x[...] - place_x
    local_y = load_y[...] - place_y
    owned = (local_x >= 0) & (local_x < rows) & (local_y >= 0) & (local_y < cols)
    target = jnp.where(owned, local_x * cols + local_y, -1)
    loads = target.shape[1]
    lanes = lax.broadcasted_iota(jnp.int32, (depth, loads), 0)
    hit_z = lanes == load_z[...]
    right = [[], []]
    for c in range(3):
        value = force[c : c + 1, :]
        coarse = value.astype(jnp.bfloat16).astype(jnp.float32)
        for part, piece in zip(right, (coarse, value - coarse)):
            part.append(jnp.where(hit_z, piece, 0.0).astype(jnp.bfloat16))
    place = lax.broadcasted_iota(jnp.int32, (rows * cols, loads), 0)
    left = jnp.where(place == target, 1.0, 0.0).astype(jnp.bfloat16)
    product = lax.dot_general(
        left, jnp.concatenate(right[0] + right[1], axis=0), (((1,), (1,)), ((), ())), preferred_element_type=jnp.float32
    )
    for c in range(3):
        applied[c] = product[:, c * depth : (c + 1) * depth] + product[:, (3 + c) * depth : (4 + c) * depth]

    wide = cols + HALO
    total_x, total_y = rows * count_x, cols * count_y
    sublane = lax.broadcasted_iota(jnp.int32, (wide, depth), 0)
    node_y = jnp.where(sublane >= wide - RADIUS, sublane - wide, sublane) + place_y
    inside_y = {
        shift: ((node_y + shift >= 0) & (node_y + shift < total_y)).astype(jnp.float32)
        for shift in range(-RADIUS, RADIUS + 1)
    }
    for kind in range(2 * RADIUS + 1):
        row = kind if kind <= RADIUS else rows - 2 * RADIUS - 1 + kind
        result = jnp.zeros((wide, depth), jnp.float32)
        for shift_y in range(-RADIUS, RADIUS + 1):
            line = jnp.zeros((1, depth), jnp.float32)
            for shift_x in range(-RADIUS, RADIUS + 1):
                square = shift_x * shift_x + shift_y * shift_y
                if square in CLASSES:
                    at = place_x + (row + shift_x)
                    inside = ((at >= 0) & (at < total_x)).astype(jnp.float32)
                    rank = CLASSES.index(square)
                    line = line + inside * sums[rank : rank + 1, :]
            result = result + inside_y[shift_y] * line
        inverse[kind] = 1.0 / jnp.where(result > 0.0, result, 1.0)


def shifted_z(value, lane, depth):
    beyond = jnp.where(lane == depth - 1, 0.0, pltpu.roll(value, depth - 1, 1))
    return value + beyond, beyond - value


def waves_of(here, there):
    return tuple(a + b for a, b in zip(here, there)) + tuple(b - a for a, b in zip(here, there))


def modal(before, after, stiff, constants):
    shear, normal_off, normal_own, pair_off, pair_own, trio, last = constants
    u = [None] * 24
    for low in range(12):
        if low >= 3:
            u[low] = before[low] + after[low]
        u[12 + low] = after[low] - before[low]
    f = [None] * 24
    terms = []

    def take(degree, pull):
        terms.append(pull * u[degree])
        f[degree] = pull * stiff

    for first, second in SHEARS:
        both = u[first] + u[second]
        pull = shear * both
        terms.append(pull * both)
        f[first] = f[second] = pull * stiff
    common = normal_off * (u[5] + u[7] + u[12])
    for degree in NORMALS:
        take(degree, common + normal_own * u[degree])
    for first, second in PAIRS:
        common = pair_off * (u[first] + u[second])
        take(first, common + pair_own * u[first])
        take(second, common + pair_own * u[second])
    common = u[9] + u[16] + u[20]
    for degree in TRIO:
        take(degree, trio * (common + u[degree]))
    for degree in LASTS:
        take(degree, last * u[degree])
    while len(terms) > 1:
        terms = [sum(terms[k : k + 2][1:], terms[k]) for k in range(0, len(terms), 2)]
    return terms[0], f


def lower_of(f):
    return tuple(f[12 + k] * -1.0 if f[k] is None else f[k] - f[12 + k] for k in range(12))


def upper_of(f):
    return tuple(f[12 + k] if f[k] is None else f[k] + f[12 + k] for k in range(12))


def along_y(g):
    return tuple(g[k] - g[6 + k] for k in range(6)), tuple(g[k] + g[6 + k] for k in range(6))


def along_z(g, lane):
    return [
        (g[c] - g[3 + c]) + jnp.where(lane == 0, 0.0, pltpu.roll(g[c] + g[3 + c], 1, 1)) for c in range(3)
    ]


def class_of(row, rows):
    return jnp.where(row < RADIUS, row, jnp.where(row >= rows - RADIUS, row - (rows - 2 * RADIUS - 1), RADIUS))


def march(rows, block, waves, state, inverse, emit, put, own):
    constants = modal_constants()
    depth = waves.shape[-1]
    first = 8 * block
    zero = jnp.zeros((HALO, depth), jnp.float32)

    def nodes(row):
        return waves_of(
            [waves[k, row, first : first + 8, :] for k in range(6)],
            [waves[k, row, first + 1 : first + 9, :] for k in range(6)],
        )

    def step(row, carry):
        before, held, total, filled = carry
        after = nodes(row + 1)
        physical, stiff, factor = state(row)
        energy, f = modal(before, after, stiff, constants)
        put(row, factor * energy * inverse[class_of(row, rows), first : first + 8, :])
        if own:
            total = total + stiff * energy
            filled = filled + physical
        emit(row, *along_y(tuple(a + b for a, b in zip(held, lower_of(f)))))
        return after, upper_of(f), total, filled

    carry = (nodes(0), (zero,) * 12, zero, zero)
    carry = lax.fori_loop(0, rows - 2, step, carry, unroll=True)
    _, held, total, filled = step(rows - 2, carry)
    emit(rows - 1, *along_y(held))
    if own:
        filled = filled + state(rows - 1)[0]
    return total, filled


def own_state(dens, kind, cols, first):
    def state(row):
        at = pl.ds(pl.multiple_of(row * cols + first, 8), HALO)
        code = kind[at, :]
        physical = physical_of(dens[at, :], code)
        return physical, stiffness_of(physical), factor_of(physical, code)

    return state


def joiner(cols, block, tail_in, tail_out, applied, resid):
    first = 8 * block
    depth = resid.shape[-1]
    lane = lax.broadcasted_iota(jnp.int32, (HALO, depth), 1)
    sublane = lax.broadcasted_iota(jnp.int32, (HALO, depth), 0)

    def emit(row, low, high):
        parts = []
        for k in range(6):
            turned = pltpu.roll(high[k], 1, 0)
            if tail_out is not None:
                tail_out[k, row] = turned
            before = 0.0 if tail_in is None else tail_in[k, row]
            parts.append(low[k] + jnp.where(sublane == 0, before, turned))
        at = pl.ds(pl.multiple_of(row * cols + first, 8), HALO)
        for c, value in enumerate(along_z(parts, lane)):
            resid[c, at, :] = applied[c, at, :] - value

    return emit


def early_elements(
    rows, cols, disp, dens, kind, inverse, applied, waves, tail, resid, scaled, sums, *tails
):
    depth = disp.shape[-1]
    lane = lax.broadcasted_iota(jnp.int32, (HALO, depth), 1)

    def turn(row, nothing):
        for c in range(3):
            for block in range(cols // 8):
                at = pl.ds(pl.multiple_of((c * rows + row) * cols + 8 * block, 8), HALO)
                for r, value in enumerate(shifted_z(disp[at, :], lane, depth)):
                    waves[3 * r + c, row, 8 * block : 8 * block + 8, :] = value
                    if block == 0:
                        waves[3 * r + c, row, cols + HALO :, :] = value
        return nothing

    lax.fori_loop(0, rows, turn, 0, unroll=8)
    total = filled = jnp.zeros((HALO, depth), jnp.float32)
    chain = (None, *tails, tail)
    for block in range(cols // 8 - 1):
        first = 8 * block

        def put(row, value, first=first):
            scaled[row, first + 8 : first + 16, :] = value

        emit = joiner(cols, block, chain[block], chain[block + 1], applied, resid)
        state = own_state(dens, kind, cols, first)
        more = march(rows, block, waves, state, inverse, emit, put, True)
        total, filled = total + more[0], filled + more[1]
    sums[0] = total
    sums[1] = filled


def late_elements(
    rows, cols,
    waves_in, resid_in, scaled_in, tail, dens, kind, edge_u, edge_f, edge_s, applied, inverse, sums_a,
    waves, resid, scaled, sums, out_a, out_b, far_h,
):
    depth = dens.shape[-1]
    del waves_in, resid_in, scaled_in
    wide = cols + HALO
    lane = lax.broadcasted_iota(jnp.int32, (HALO, depth), 1)

    def turn(row, nothing):
        for c in range(3):
            at = pl.ds(pl.multiple_of((c * rows + row) * HALO, 8), HALO)
            for r, value in enumerate(shifted_z(edge_u[at, :], lane, depth)):
                waves[3 * r + c, row, cols:wide, :] = value
        return nothing

    lax.fori_loop(0, rows, turn, 0, unroll=16)

    def edge_state(row):
        at = pl.ds(pl.multiple_of(row * HALO, 8), HALO)
        return None, edge_s[at, :], edge_f[at, :]

    def put_edge(row, value):
        scaled[row, :HALO, :] = value
        scaled[row, wide:, :] = value

    def emit_edge(row, low, high):
        for k in range(6):
            far_h[pl.ds(pl.multiple_of((k * rows + row) * HALO, 8), HALO), :] = high[k]

    last = cols // 8 - 1
    march(rows, cols // 8, waves, edge_state, inverse, emit_edge, put_edge, False)
    parts = [far_h[pl.ds(k * rows * HALO + HALO - 1, rows, stride=HALO), :] for k in range(6)]
    at = pl.ds(0, rows, stride=cols)
    for c, value in enumerate(along_z(parts, lax.broadcasted_iota(jnp.int32, (rows, depth), 1))):
        resid[c, at, :] = resid[c, at, :] - value

    def put(row, value):
        scaled[row, cols:wide, :] = value

    emit = joiner(cols, last, tail, None, applied, resid)
    state = own_state(dens, kind, cols, 8 * last)
    total, filled = march(rows, last, waves, state, inverse, emit, put, True)
    sums[0] = sums_a[0] + total
    sums[1] = sums_a[1] + filled

    def out(up, down):
        for index in range(RADIUS - 1):
            up[index] = scaled[rows - RADIUS + index, :wide, :]
        at = pl.ds((rows - 1) * cols, cols)
        code = kind[at, :]
        up[RADIUS - 1, HALO:, :] = factor_of(physical_of(dens[at, :], code), code)
        up[RADIUS - 1, :HALO, :] = edge_f[pl.ds((rows - 1) * HALO, HALO), :]
        for index in range(RADIUS):
            down[index] = scaled[index, :wide, :]

    odd = lax.axis_index("gx") % 2

    @pl.when(odd == 0)
    def _():
        out(out_a, out_b)

    @pl.when(odd == 1)
    def _():
        out(out_b, out_a)


def outer_elements(
    rows, cols, count_x, devices,
    waves, dens, kind, edge_f, edge_s, got_a, got_b, inner, sums, inverse,
    resid, final, before, parts, ring, stiff_low, carry_y,
):
    depth = dens.shape[-1]
    constants = modal_constants()
    wide = cols + HALO
    blocks = wide // HALO
    lane = lax.broadcasted_iota(jnp.int32, (HALO, depth), 1)
    here = lax.axis_index("gx")
    has_low = here > 0
    has_high = here < count_x - 1
    odd = here % 2

    def take(low, high):
        for block in range(blocks):
            first = 8 * block
            for c in range(3):
                for side, value in enumerate((low[c, first : first + 8, :], high[c, first : first + 8, :])):
                    if side:
                        value = jnp.where(has_high, value, 0.0)
                    for r, wave in enumerate(shifted_z(value, lane, depth)):
                        ring[side, 3 * r + c, first : first + 8, :] = wave
                        if block == 0:
                            ring[side, 3 * r + c, wide:, :] = wave
        stiff_low[...] = jnp.where(has_low, low[3], 0.0)

    @pl.when(odd == 0)
    def _():
        take(got_b, got_a)

    @pl.when(odd == 1)
    def _():
        take(got_a, got_b)

    total = sums[0]
    for block in (blocks - 1, *range(blocks - 1)):
        own = block < blocks - 1
        first = 8 * block

        def nodes(load):
            return waves_of(
                [load(k)[first : first + 8, :] for k in range(6)], [load(k)[first + 1 : first + 9, :] for k in range(6)]
            )

        line = [
            nodes(lambda k: ring.at[0, k]),
            nodes(lambda k: waves.at[k, 0]),
            nodes(lambda k: waves.at[k, rows - 1]),
            nodes(lambda k: ring.at[1, k]),
        ]
        energy, f_low = modal(line[0], line[1], stiff_low[first : first + 8, :], constants)
        place = first + 8 if own else 0
        before[place : place + 8, :] = energy * inverse[RADIUS, first : first + 8, :]
        if own:
            _, stiff, factor = own_state(dens, kind, cols, first)(rows - 1)
        else:
            at = pl.ds((rows - 1) * HALO, HALO)
            stiff, factor = edge_s[at, :], edge_f[at, :]
        energy, f_high = modal(line[2], line[3], stiff, constants)
        value = factor * energy * inverse[2 * RADIUS, first : first + 8, :]
        if own:
            total = total + stiff * energy
            final[first + 8 : first + 16, :] = value
        else:
            final[:HALO, :] = value
            final[wide:, :] = value
        for index, (row, g) in enumerate(((0, upper_of(f_low)), (rows - 1, lower_of(f_high)))):
            low, high = along_y(g)
            if own:
                joined = []
                for k in range(6):
                    carry_y[index, k, first + 9 : first + 17, :] = high[k]
                    joined.append(low[k] + carry_y[index, k, first + 8 : first + 16, :])
                for c, value in enumerate(along_z(joined, lane)):
                    resid[index, c, first : first + 8, :] = inner[c, pl.ds(row * cols + first, HALO), :] - value
            else:
                for k in range(6):
                    carry_y[index, k, 1:9, :] = high[k]

    half = depth // 2
    pieces = []
    for value in (total, sums[1]):
        line = jnp.sum(value, axis=0, keepdims=True)
        pieces.append(line + pltpu.roll(line, half, 1))
    line = jnp.where(lax.broadcasted_iota(jnp.int32, (1, depth), 1) < half, pieces[0], pieces[1])
    parts[...] = jnp.broadcast_to(line, (devices, depth))


def lines_y(near, row, cols, load):
    for block in range(cols // 8):
        start = HALO + 8 * block
        near[0, row, 8 * block : 8 * block + 8, :] = load(start)
        for shift in range(1, RADIUS + 1):
            near[shift, row, 8 * block : 8 * block + 8, :] = load(start + shift) + load(start - shift)


def bands(depth):
    row = lax.broadcasted_iota(jnp.int32, (depth, depth), 0)
    column = lax.broadcasted_iota(jnp.int32, (depth, depth), 1)
    away = jnp.abs(row - column)
    return jnp.concatenate(
        [jnp.where(away == shift, 1.0, 0.0).astype(jnp.bfloat16) for shift in range(1, RADIUS + 1)], axis=0
    )


def filter_rows(near, lines, result, picks, cols, band):
    depth = near.shape[-1]
    for rank, row in enumerate(picks):
        for block in range(cols // 8):
            at = pl.ds(block * 8, 8)
            classes = {}
            for shift_x in range(RADIUS + 1):
                for shift_y in range(RADIUS + 1):
                    square = shift_x * shift_x + shift_y * shift_y
                    if square not in CLASSES:
                        continue
                    value = near[shift_y, row + (RADIUS + shift_x), at, :]
                    if shift_x:
                        value = value + near[shift_y, row + (RADIUS - shift_x), at, :]
                    classes[square] = value if square not in classes else classes[square] + value
            for shift_z in range(RADIUS + 1):
                line = None
                for square, value in classes.items():
                    weight = weight_of(square + shift_z * shift_z)
                    if weight > 0.0:
                        line = weight * value if line is None else line + weight * value
                if shift_z:
                    first = rank * cols + 8 * block
                    lines[first : first + 8, (shift_z - 1) * depth : shift_z * depth] = line
                else:
                    result[row, at, :] = line
    value = lines[: len(picks) * cols, :]
    coarse = value.astype(jnp.bfloat16)
    rest = (value - coarse.astype(jnp.float32)).astype(jnp.bfloat16)
    total = jnp.dot(coarse, band, preferred_element_type=jnp.float32)
    total = total + jnp.dot(rest, band, preferred_element_type=jnp.float32)
    return total.reshape(len(picks), cols, depth)


def filter_all(rows, cols, count_x, scaled, final, before, got_a, got_b, inner, outer, result, resid, near, ends, lines, sems):
    depth = result.shape[-1]
    wide = cols + HALO
    middle = pl.ds(1, rows - 2)
    copies = [
        pltpu.make_async_copy(inner.reshape(3, rows, cols, depth).at[:, middle], resid.at[:, middle], sems.at[0]),
        pltpu.make_async_copy(outer.at[0], resid.at[:, 0], sems.at[1]),
        pltpu.make_async_copy(outer.at[1], resid.at[:, rows - 1], sems.at[2]),
    ]
    for copy in copies:
        copy.start()
    here = lax.axis_index("gx")
    has_low = here > 0
    has_high = here < count_x - 1
    odd = here % 2

    def take(low, high):
        for index in range(RADIUS):
            for source, has, at in ((low, has_low, index), (high, has_high, RADIUS + index)):
                value = source[index]
                if source is low and index == RADIUS - 1:
                    value = value * before[...]
                value = jnp.where(has, value, 0.0)
                ends[at, :wide, :] = value
                ends[at, wide:, :] = value[:HALO]

    @pl.when(odd == 0)
    def _():
        take(got_b, got_a)

    @pl.when(odd == 1)
    def _():
        take(got_a, got_b)

    for index in range(RADIUS):
        lines_y(near, index, cols, lambda start, at=index: ends[at, start : start + 8, :])
        lines_y(near, rows + RADIUS + index, cols, lambda start, at=RADIUS + index: ends[at, start : start + 8, :])
    lines_y(near, rows + RADIUS - 1, cols, lambda start: final[start : start + 8, :])
    for row in range(rows - 1):
        lines_y(near, row + RADIUS, cols, lambda start, row=row: scaled[row, start : start + 8, :])
    band = bands(depth)
    for start in range(0, rows, FILTER_ROWS):
        picks = range(start, min(start + FILTER_ROWS, rows))
        rest = filter_rows(near, lines, result, picks, cols, band)
        result[picks.start : picks.stop] = result[picks.start : picks.stop] + rest
    for copy in copies:
        copy.wait()


def finish(rows, cols, cells, inner, parts, sens, comp, vol, result_v, sems):
    depth = sens.shape[-1]
    copies = []
    half = depth // 2
    line = jnp.sum(parts[...], axis=0, keepdims=True)
    first = lax.broadcasted_iota(jnp.int32, (1, depth), 1) < half
    compliance = jnp.sum(jnp.where(first, line, 0.0))
    volume = jnp.sum(jnp.where(first, 0.0, line))
    comp[0, 0] = compliance
    vol[0, 0] = volume / cells
    scale = cells / jnp.broadcast_to(compliance, (8, depth))
    size = rows // 2
    for start in range(0, rows, size):
        for row in range(start, start + size):
            for block in range(cols // 8):
                at = pl.ds(block * 8, 8)
                result_v[row, at, :] = inner[row, at, :] * scale
        at = pl.ds(start, size)
        copies.append(pltpu.make_async_copy(result_v.at[at], sens.at[at], sems.at[len(copies)]))
        copies[-1].start()
    for copy in copies:
        copy.wait()


def call(body, shapes, inputs, scratch=(), places=None, out_places=None, flops=0, limit=24, aliases=None):
    places, out_places = places or {}, out_places or {}
    in_specs = [pl.BlockSpec(memory_space=places.get(rank, pltpu.VMEM)) for rank in range(len(inputs))]
    out_specs = [pl.BlockSpec(memory_space=out_places.get(rank, pltpu.VMEM)) for rank in range(len(shapes))]
    moved = sum(int(np.prod(v.shape)) * 4 for v in list(inputs) + list(shapes))
    return pl.pallas_call(
        body,
        out_shape=[FULL(v.shape, v.dtype) for v in shapes],
        in_specs=in_specs,
        out_specs=out_specs,
        scratch_shapes=list(scratch),
        input_output_aliases=aliases or {},
        cost_estimate=pl.CostEstimate(flops=flops, bytes_accessed=moved, transcendentals=0),
        compiler_params=pltpu.CompilerParams(vmem_limit_bytes=int(limit * 1024 * 1024)),
    )(*inputs)


def f32(*shape):
    return FULL(shape, jnp.float32)


def vmem(*shape, dtype=jnp.float32):
    return pltpu.VMEM(shape, dtype)


def on_device(count_x, count_y, displacement, density, element_kind, load_x, load_y, load_z, load_force):
    rows, cols, depth = density.shape
    wide = cols + HALO
    devices = count_x * count_y
    cells = float(rows * cols * depth * devices)

    pairs_ya = [(k, k ^ 1) for k in range(count_y)]
    pairs_xa = [(k, k ^ 1) for k in range(count_x)]
    pairs_yb, pairs_xb = [], []
    for i in range(count_x):
        for j in range(count_y):
            here = i * count_y + j
            inside_y, inside_x = 0 < j < count_y - 1, 0 < i < count_x - 1
            pairs_yb.append((here, i * count_y + ((j + 1) ^ 1) - 1 if inside_y else (i ^ 1) * count_y + j))
            pairs_xb.append((here, (((i + 1) ^ 1) - 1) * count_y + j if inside_x else i * count_y + (j ^ 1)))

    disp = displacement.reshape(3 * rows * cols, depth)
    dens = density.reshape(rows * cols, depth)
    kind = element_kind.reshape(rows * cols, depth)

    slots = 4 * RADIUS + RADIUS
    send_a, send_b, mark = call(
        functools.partial(pack_y, rows, cols),
        [f32(slots * rows, depth)] * 2 + [f32(8, depth)],
        [displacement, density, element_kind],
        scratch=[
            vmem(3, rows, HALO, depth),
            vmem(rows, HALO, depth),
            vmem(rows, HALO, depth, dtype=jnp.int32),
            pltpu.SemaphoreType.DMA((6,)),
        ],
        places={0: pltpu.HBM, 1: pltpu.HBM, 2: pltpu.HBM},
        limit=53.25,
    )
    got_b = lax.ppermute(send_b, BOTH, pairs_yb)
    got_a = lax.ppermute(send_a, "gy", pairs_ya)

    sums = np.zeros((8, depth), np.float32)
    for rank, square in enumerate(CLASSES):
        for z in range(depth):
            sums[rank, z] = sum(
                weight_of(square + s * s) for s in range(-RADIUS, RADIUS + 1) if 0 <= z + s < depth
            )
    count = load_x.shape[0]
    applied, inverse = call(
        functools.partial(loads_and_weights, rows, cols, count_x, count_y),
        [f32(3, rows * cols, depth), f32(2 * RADIUS + 1, wide, depth)],
        [mark, load_x.reshape(1, count), load_y.reshape(1, count), load_z.reshape(1, count), load_force, jnp.asarray(sums)],
        places={0: pl.ANY},
        flops=2 * rows * cols * count * 6 * depth,
    )

    early = cols - HALO
    waves, tail, inner, scaled, sums = call(
        functools.partial(early_elements, rows, cols),
        [
            f32(6, rows, wide + HALO, depth),
            f32(6, rows, HALO, depth),
            f32(3, rows * cols, depth),
            f32(rows, wide + HALO, depth),
            f32(2, 8, depth),
        ],
        [disp, dens, kind, inverse, applied],
        scratch=[vmem(6, rows, HALO, depth)] * (cols // HALO - 2),
        flops=250 * rows * early * depth,
    )

    edge_u, edge_f, edge_s, send_a, send_b = call(
        functools.partial(unpack_y, rows, cols, count_y),
        [f32(3 * rows * HALO, depth), f32(rows * HALO, depth), f32(rows * HALO, depth)] + [f32(4, wide, depth)] * 2,
        [sums, disp, dens, kind, got_a, got_b],
        places={0: pl.ANY},
    )
    got_b = lax.ppermute(send_b, BOTH, pairs_xb)
    got_a = lax.ppermute(send_a, "gx", pairs_xa)

    waves, inner, scaled, sums, send_a, send_b = call(
        functools.partial(late_elements, rows, cols),
        [f32(*v.shape) for v in (waves, inner, scaled, sums)]
        + [f32(RADIUS, wide, depth)] * 2,
        [waves, inner, scaled, tail, dens, kind, edge_u, edge_f, edge_s, applied, inverse, sums],
        scratch=[vmem(6 * rows * HALO, depth)],
        flops=250 * rows * 2 * HALO * depth,
        aliases={0: 0, 1: 1, 2: 2},
    )
    more_b = lax.ppermute(send_b, BOTH, pairs_xb)
    more_a = lax.ppermute(send_a, "gx", pairs_xa)
    outer, final, before, parts = call(
        functools.partial(outer_elements, rows, cols, count_x, devices),
        [f32(2, 3, cols, depth), f32(wide + HALO, depth), f32(wide, depth), f32(devices, depth)],
        [waves, dens, kind, edge_f, edge_s, got_a, got_b, inner, sums, inverse],
        scratch=[vmem(2, 6, wide + HALO, depth), vmem(wide, depth), vmem(2, 6, wide + 2 * HALO, depth)],
        flops=500 * wide * depth,
    )
    parts = lax.all_to_all(parts, BOTH, 0, 0, tiled=True)

    filtered, resid = call(
        functools.partial(filter_all, rows, cols, count_x),
        [f32(rows, cols, depth), f32(3, rows, cols, depth)],
        [scaled, final, before, more_a, more_b, inner, outer],
        scratch=[
            vmem(RADIUS + 1, rows + 2 * RADIUS, cols, depth),
            vmem(2 * RADIUS, wide + HALO, depth),
            vmem(FILTER_ROWS * cols, RADIUS * depth),
            pltpu.SemaphoreType.DMA((3,)),
        ],
        out_places={1: pltpu.HBM},
        flops=80 * rows * cols * depth,
    )
    sens, comp, volume = call(
        functools.partial(finish, rows, cols, cells),
        [f32(rows, cols, depth), f32(1, 1), f32(1, 1)],
        [filtered, parts],
        scratch=[vmem(rows, cols, depth), pltpu.SemaphoreType.DMA((2,))],
        out_places={0: pltpu.HBM, 1: pltpu.SMEM, 2: pltpu.SMEM},
        flops=rows * cols * depth,
    )
    return (
        sens,
        resid,
        comp.reshape(()),
        volume.reshape(()),
    )


def solution(mesh):
    placed = (
        P(None, "gx", "gy", None),
        P("gx", "gy", None),
        P("gx", "gy", None),
        P(),
        P(),
        P(),
        P(),
    )
    return jax.shard_map(
        functools.partial(on_device, mesh.shape["gx"], mesh.shape["gy"]),
        mesh=mesh,
        in_specs=placed,
        out_specs=(P("gx", "gy", None), P(None, "gx", "gy", None), P(), P()),
        check_vma=False,
    )
```
